32 devices in a mesh: dp: 16 (over z, y, x), tensor: 2 (over core).
Axes of the slice: x: 2, y: 2, z: 4, core: 2. Of those that a mesh axis runs over, the one named last changes fastest.
Arguments:
- tokens: bfloat16 [32768, 768], P(('dp', 'tensor')), may hold values from -6 to 6
- segment: int32 [32768], P('dp'), may hold values from -1 to 4, as said below
- ln1_gain: float32 [768], replicated, may hold values from 0.5 to 1.5
- w_qkv: bfloat16 [768, 3, 768], P(None, None, 'tensor'), may hold values from -0.21875 to 0.21875
- q_gain: float32 [64], replicated, may hold values from 0.25 to 1.75
- k_gain: float32 [64], replicated, may hold values from 0.25 to 1.75
- w_out: bfloat16 [768, 768], P('tensor'), may hold values from -1.75 to 1.75
- ln2_gain: float32 [768], replicated, may hold values from 0.5 to 1.5
- w_up: bfloat16 [768, 3072], P(None, 'tensor'), may hold values from -0.21875 to 0.21875
- w_down: bfloat16 [3072, 768], P('tensor'), may hold values from -0.109375 to 0.109375
- cotangent: bfloat16 [32768, 768], P(('dp', 'tensor')), may hold values from -6 to 6
Outputs:
- layer_out: bfloat16 [32768, 768], P(('dp', 'tensor'))
- input_grad: bfloat16 [32768, 768], P(('dp', 'tensor'))
- ln1_gain_grad: float32 [768], replicated
- qkv_grad: float32 [768, 3, 768], P('dp', None, 'tensor')
- q_gain_grad: float32 [64], replicated
- k_gain_grad: float32 [64], replicated
- proj_grad: float32 [768, 768], P('tensor', 'dp')
- ln2_gain_grad: float32 [768], replicated
- up_grad: float32 [768, 3072], P('dp', 'tensor')
- down_grad: float32 [3072, 768], P('tensor', 'dp')
The draws below stay inside these ranges and needn't reach their ends.
Inputs may be any that keep to these rules, and one draw needn't show every extreme that they name: `segment`: rows k * 1024 to (k + 1) * 1024 - 1 form a sequence that holds 5 images of 196 positions, numbered 0 to 4 in order, and one run of 44 padding positions marked -1 before, between or after them.
All inputs are finite; a program needn't handle non-finite values.
Results may differ from the reference program's by a relative error of at most 0.017.
Values may be sent and summed in bfloat16 or wider, within the bound.
A program may use at most 192 MiB of HBM per device.

```python
import jax
import jax.numpy as jnp
from jax import lax

D = 768
FF = 3072
HD = 64
HEADS = 12
LENGTH = 1024
PATCHES = 196
IMAGES = 5
TOKENS = 32768
N_DP = 16


def draw_segment(key, part):
    key = jax.random.fold_in(key, 7)
    seq_count = TOKENS // LENGTH
    slot_index = jax.random.randint(key, (seq_count, 1), 0, IMAGES + 1)
    position = jnp.arange(LENGTH, dtype=jnp.int32)[None, :]
    padding = LENGTH - IMAGES * PATCHES
    pad_begin = slot_index * PATCHES
    earlier = position // PATCHES
    following = (position - padding) // PATCHES
    inside = jnp.where(position < pad_begin + padding, -1, following)
    ids = jnp.where(position < pad_begin, earlier, inside)
    return ids.reshape(TOKENS).astype(jnp.int32)


def with_spikes(entries, key, source, target, parts, factor):
    owner, partner = [(jnp.arange(entries.shape[axis_at]) // (entries.shape[axis_at] // parts)).reshape([-1 if axis == axis_at else 1 for axis in range(entries.ndim)]) for axis_at in (source, target)]
    chosen = jax.random.permutation(key, parts)[partner]
    strong = (owner == chosen) | (owner == (partner + parts // 2) % parts)
    return jnp.where(strong, factor * entries, entries)


def block_scale(own_key, shape, shards, smallest, largest):
    def one(axis_at, parts):
        steps = jax.random.uniform(jax.random.fold_in(jax.random.fold_in(own_key, 6), axis_at), (parts,), jnp.float32, smallest / len(shards), largest / len(shards))
        return jnp.repeat(jnp.exp(steps), shape[axis_at] // parts).reshape((-1,) + (1,) * (len(shape) - axis_at - 1))

    level = one(*shards[0])
    for cut in shards[1:]:
        level = level * one(*cut)
    return level


def scatter_about(own_key, extent, scale, limit, cuts=(), held_as=jnp.bfloat16):
    values = scale * jax.random.normal(own_key, extent, jnp.float32)
    if cuts:
        values = values * block_scale(own_key, extent, cuts, -0.22, 0.18)
    return jnp.clip(values, -limit, limit).astype(held_as)


def heavy_noise(stream_key, dims, scale, reach, cuts, heavy, held_as=jnp.bfloat16):
    values = scale * jax.random.normal(stream_key, dims, jnp.float32)
    if cuts:
        values = values * block_scale(stream_key, dims, cuts, -0.22, 0.18)
    return jnp.clip(with_spikes(values, jax.random.fold_in(stream_key, 3), *heavy), -reach, reach).astype(held_as)


def setup_inputs(seed: int = 0) -> dict:
    keys = jax.random.split(jax.random.key(seed), 12)
    tokens = heavy_noise(keys[0], (TOKENS, D), 1.0, 6.0, ((0, 32),), (0, 1, 32, 2.75))
    segment = draw_segment(jax.random.fold_in(keys[11], 71), 0)
    ln1_gain = jnp.clip(1.0 + 0.1 * jax.random.normal(keys[2], (D,), jnp.float32), 0.5, 1.5)
    w_qkv = scatter_about(keys[3], (D, 3, D), D ** -0.5, 0.21875, ((2, 2),))
    q_gain = jnp.clip(1.0 + 0.15 * jax.random.normal(keys[4], (HD,), jnp.float32), 0.25, 1.75)
    k_gain = jnp.clip(1.0 + 0.15 * jax.random.normal(keys[5], (HD,), jnp.float32), 0.25, 1.75)
    w_out = scatter_about(keys[6], (D, D), (max(D // 64, 4)) ** -0.5, 1.75, ((0, 2),))
    ln2_gain = jnp.clip(1.0 + 0.1 * jax.random.normal(keys[7], (D,), jnp.float32), 0.5, 1.5)
    w_up = scatter_about(keys[8], (D, FF), D ** -0.5, 0.21875, ((1, 2),))
    w_down = scatter_about(keys[9], (FF, D), FF ** -0.5, 0.109375, ((0, 2),))
    cotangent = heavy_noise(keys[10], (TOKENS, D), 1.0, 6.0, ((0, 32),), (0, 1, 32, 2.75))
    return dict(tokens=tokens, segment=segment, ln1_gain=ln1_gain, w_qkv=w_qkv, q_gain=q_gain, k_gain=k_gain, w_out=w_out, ln2_gain=ln2_gain, w_up=w_up, w_down=w_down, cotangent=cotangent)


@jax.custom_vjp
def low(v):
    return lax.optimization_barrier(v.astype(jnp.bfloat16)).astype(jnp.float32)

@jax.custom_vjp
def low_back(v):
    return v

def low_keep(v):
    return (low(v), None)

def low_pass(kept, grad):
    return (grad,)

def back_keep(v):
    return (v, None)

def back_low(kept, grad):
    return (low(grad),)
low.defvjp(low_keep, low_pass)
low_back.defvjp(back_keep, back_low)
epsilon = 1e-06
highest = lax.Precision.HIGHEST

def layer_norm(values, gain):
    centred = values - lax.optimization_barrier(jnp.mean(values, axis=-1, keepdims=True))
    spread = lax.optimization_barrier(jnp.mean(centred * centred, axis=-1, keepdims=True))
    return centred * lax.rsqrt(spread + epsilon) * gain

def attend_sequence(pieces):
    queries, key_rows, value_rows, segment_ids = pieces
    scores = jnp.einsum('qhd,khd->hqk', queries, key_rows, precision=highest) * HD ** (-0.5)
    scores = low_back(scores)
    matching = segment_ids[:, None] == segment_ids[None, :]
    scores = jnp.where(matching[None], scores, -1e+30)
    row_top = lax.optimization_barrier(jnp.max(scores, axis=-1, keepdims=True))
    exponent = jnp.exp(scores - row_top)
    attn_probs = exponent / lax.optimization_barrier(jnp.sum(exponent, axis=-1, keepdims=True))
    return jnp.einsum('hqk,khd->qhd', low(attn_probs), value_rows, precision=highest)

def layer(inputs, segment_ids, ln1_gain, w_qkv, q_gain, k_gain, w_out, ln2_gain, w_up, w_down):
    row_count = inputs.shape[0]
    seq_count = row_count // LENGTH
    normed_in = low(layer_norm(inputs, ln1_gain))
    projected = low_back(jnp.dot(normed_in, w_qkv.reshape(D, 3 * D), precision=highest))
    projected = projected.reshape(row_count, 3, HEADS, HD)
    queries = low(layer_norm(projected[:, 0], q_gain))
    key_rows = low(layer_norm(projected[:, 1], k_gain))
    value_rows = low(projected[:, 2])
    attended = lax.map(jax.checkpoint(attend_sequence), (queries.reshape(seq_count, LENGTH, HEADS, HD), key_rows.reshape(seq_count, LENGTH, HEADS, HD), value_rows.reshape(seq_count, LENGTH, HEADS, HD), segment_ids.reshape(seq_count, LENGTH)))
    attended = low(low_back(attended.reshape(row_count, D)))
    branch = low_back(jnp.dot(attended, w_out, precision=highest))
    middle = inputs + branch
    normed_mid = low(layer_norm(middle, ln2_gain))
    hidden = low_back(jnp.dot(normed_mid, w_up, precision=highest))
    activated = low(jax.nn.gelu(hidden, approximate=False))
    return middle + low_back(jnp.dot(activated, w_down, precision=highest))

def reference(tokens, segment, ln1_gain, w_qkv, q_gain, k_gain, w_out, ln2_gain, w_up, w_down, cotangent):
    params = (ln1_gain.astype(jnp.float32), w_qkv.astype(jnp.float32), q_gain.astype(jnp.float32), k_gain.astype(jnp.float32), w_out.astype(jnp.float32), ln2_gain.astype(jnp.float32), w_up.astype(jnp.float32), w_down.astype(jnp.float32))
    group_rows = TOKENS // N_DP
    inputs = tokens.astype(jnp.float32).reshape(N_DP, group_rows, D)
    segments = segment.reshape(N_DP, group_rows)
    grads_out = cotangent.astype(jnp.float32).reshape(N_DP, group_rows, D)

    def one_group(totals, items):
        group_in, group_seg, group_cot = items

        def apply(values, ln1, wqkv, qgain, kgain, wout, ln2, wup, wdown):
            return layer(values, group_seg, ln1, wqkv, qgain, kgain, wout, ln2, wup, wdown)
        result, pullback = jax.vjp(apply, group_in, params[0], params[1], params[2], params[3], params[4], params[5], params[6], params[7])
        grads = pullback(group_cot)
        totals = tuple((summed + fresh for summed, fresh in zip(totals, grads[1:])))
        return (totals, (result.astype(jnp.bfloat16), grads[0].astype(jnp.bfloat16)))
    zeros = tuple((jnp.zeros_like(weight) for weight in params))
    totals, (results, grads_in) = lax.scan(one_group, zeros, (inputs, segments, grads_out))
    return (results.reshape(TOKENS, D), grads_in.reshape(TOKENS, D), totals[0], totals[1], totals[2], totals[3], totals[4], totals[5], totals[6], totals[7])
```

```python
import functools

import jax
import jax.numpy as jnp
from jax import lax
from jax.experimental import pallas as pl
from jax.experimental.pallas import tpu as pltpu
from jax.sharding import PartitionSpec as P

D = 768
HD = 64
LENGTH = 1024
PATCHES = 196
IMAGES = 5
PADDING = LENGTH - IMAGES * PATCHES
PADDED = 1040
PAIRS = 6
EPS = 1e-06
MESH = pl.DeviceIdType.MESH
f32, bf16 = jnp.float32, jnp.bfloat16

WINDOWS = [
    (PATCHES * i // 16 * 16, 208, PATCHES * i, PATCHES * (i + 1)) for i in range(IMAGES)
] + [(976, 48, 980, 1024)]

FF_CHUNKS = 6
FW = 256
CHUNKS = 10
BITS = 4


def dot(left, right):
    return jnp.dot(left, right, preferred_element_type=f32)


def dot_nt(left, right):
    return lax.dot_general(left, right, (((1,), (1,)), ((), ())), preferred_element_type=f32)


def dot_tn(left, right):
    return lax.dot_general(left, right, (((0,), (0,)), ((), ())), preferred_element_type=f32)


def gelu_and_slope(h):
    e = jnp.exp(h * h * -0.5)
    t = 1.0 / (1.0 + jnp.abs(h) * (0.3275911 * 0.7071067811865476))
    poly = t * (
        0.5 * 0.254829592
        + t
        * (
            0.5 * -0.284496736
            + t * (0.5 * 1.421413741 + t * (0.5 * -1.453152027 + t * (0.5 * 1.061405429)))
        )
    )
    tail = poly * e
    phi = jnp.where(h >= 0, 1.0 - tail, tail)
    return h * phi, phi + h * e * 0.3989422804014327


def split(x):
    high = x.astype(bf16)
    return high, (x - high.astype(f32)).astype(bf16)


def iota(shape, axis):
    return lax.broadcasted_iota(jnp.int32, shape, axis)


def norm_rows(x):
    centred = x - jnp.mean(x, axis=-1, keepdims=True)
    inverse = lax.rsqrt(jnp.mean(centred * centred, axis=-1, keepdims=True) + EPS)
    return centred * inverse, inverse


def norm_rows_back(grad, standard, inverse, gain):
    c = grad * gain
    return inverse * (
        c
        - jnp.mean(c, axis=-1, keepdims=True)
        - standard * jnp.mean(c * standard, axis=-1, keepdims=True)
    )


def swap(pos):
    return (pos & 4) | (pos & 1) | ((pos & 8) >> 2) | ((pos & 2) << 2)


def kernel(
    dp_low,
    slot_ref,
    tok,
    cot,
    ln1,
    ln2,
    qgain,
    kgain,
    wqkv,
    wout,
    wup,
    wdn,
    lay_out,
    inp_out,
    up_out,
    dn_out,
    pr_out,
    qk_out,
    gains_out,
    wup_x,
    wdn_x,
    tokv,
    cotv,
    xp,
    cp,
    ni,
    q,
    k,
    v,
    invq,
    invk,
    lse,
    nlg,
    dlt,
    mid,
    outa,
    gna,
    big,
    wus,
    wds,
    wq,
    wo,
    do,
    sbuf,
    r0,
    af,
    r1f,
    r2f,
    r3f,
    r4f,
    ap,
    r1p,
    r2p,
    r3p,
    r4p,
    gsend,
    grecv,
    ssem,
    rsem,
    gssem,
    grsem,
    wssem,
    wrsem,
    lsem,
    fsem,
    osem,
):
    att = tokv
    gb = cotv
    g = lax.axis_index("dp")
    t = lax.axis_index("tensor")
    top, low = g // dp_low, g % dp_low
    mine = [(top // (1 << b)) % 2 for b in range(BITS)]

    def peer(b):
        return ((top + (1 - 2 * mine[b]) * (1 << b)) * dp_low + low, t)

    d0, d1 = peer(0)[0], peer(1)[0]
    core = (g, 1 - t)
    first = (jnp.where(t == 0, d0, d1), t)
    third = (jnp.where(t == 0, d1, d0), t)
    partners = (core, first, peer(2), third, peer(3))

    def place(b):
        rel = [mine[i] if (b >> i) & 1 == 0 else 1 - mine[i] for i in range(BITS)]
        one = rel[0] * 8 + rel[1] * 2
        two = rel[1] * 8 + rel[0] * 2
        return one + t * (two - one) + rel[2] * 4 + rel[3]

    places = [place(b) for b in range(16)]

    barrier = pltpu.get_barrier_semaphore()
    for partner in partners:
        pl.semaphore_signal(barrier, inc=1, device_id=partner, device_id_type=MESH)

    loads = [
        pltpu.make_async_copy(tok, tokv, lsem.at[0]),
        pltpu.make_async_copy(cot, cotv, lsem.at[1]),
        pltpu.make_async_copy(wqkv, wq.at[0], lsem.at[2]),
        pltpu.make_async_copy(wout, wo.at[pl.ds(0, 384)], lsem.at[3]),
    ]
    for c in loads:
        c.start()
    pl.semaphore_wait(barrier, len(partners))

    def weight_copy(i, src, dst):
        return pltpu.make_async_remote_copy(
            src_ref=src,
            dst_ref=dst,
            send_sem=wssem.at[i],
            recv_sem=wrsem.at[i],
            device_id=core,
            device_id_type=MESH,
        )

    weights = [
        weight_copy(0, wqkv, wq.at[1]),
        weight_copy(1, wout, wo.at[pl.ds(384, 384)]),
        weight_copy(2, wup, wup_x),
        weight_copy(3, wdn, wdn_x),
    ]
    for c in weights:
        c.start()

    def chunk_refs(c, is_ff):
        if is_ff:
            return 2 * FW, af.at[c], (r1f.at[c], r2f.at[c], r3f.at[c], r4f.at[c])
        return 384, ap.at[c - FF_CHUNKS], tuple(r.at[c - FF_CHUNKS] for r in (r1p, r2p, r3p, r4p))

    def rs_copy(stage, c, is_ff):
        width, a, rs = chunk_refs(c, is_ff)
        if stage == 0:
            slot = lax.rem(c, 2)
            src = sbuf.at[slot, :, :, pl.ds(0, width)]
            dst = r0.at[slot, :, :, pl.ds(0, width)]
        else:
            half = 16 >> stage
            src, dst = a.at[pl.ds(half, half)], rs[stage - 1]
        return pltpu.make_async_remote_copy(
            src_ref=src,
            dst_ref=dst,
            send_sem=ssem.at[c, stage],
            recv_sem=rsem.at[c, stage],
            device_id=partners[stage],
            device_id_type=MESH,
        )

    def finish(c, is_ff, total):
        if is_ff:
            cols = pl.ds(pl.multiple_of(c * FW, FW), FW)
            up_out[:, cols] = total[:, :FW]
            dn_out[:, cols] = total[:, FW:]
        elif c == FF_CHUNKS:
            pr_out[...] = total
        else:
            m = c - FF_CHUNKS - 1
            for part in range(3):
                qk_out[part, :, 128 * m : 128 * m + 128] = total[:, 128 * part : 128 * part + 128]

    def advance(stage, c, is_ff):
        width, a, rs = chunk_refs(c, is_ff)
        rs_copy(stage, c, is_ff).wait()
        if stage == 0:
            slot = lax.rem(c, 2)
            for pos in range(16):
                a[pos] = a[pos] + r0[slot, swap(pos), :, 0:width]
        elif stage < 4:
            half = 16 >> stage
            for pos in range(half):
                a[pos] = a[pos] + rs[stage - 1][pos]
        else:
            finish(c, is_ff, a[0].astype(f32) + rs[3][0].astype(f32))
        if stage < 4:
            rs_copy(stage + 1, c, is_ff).start()

    def event(e):
        for stage in range(4, -1, -1):
            c = e - stage - 1
            if 0 <= c < CHUNKS:
                advance(stage, c, c < FF_CHUNKS)
        if e < CHUNKS:
            rs_copy(0, e, e < FF_CHUNKS).start()

    s = slot_ref[0]
    loads[0].wait()
    loads[1].wait()
    zero_rows = jnp.zeros((PADDED - LENGTH, 128), bf16)
    for pp in range(PAIRS):
        for ref in (q, k, v, do):
            ref[pp, LENGTH:, :] = zero_rows
    nlg[LENGTH:, :] = zero_rows
    dlt[LENGTH:, :] = zero_rows

    def rows_of(i):
        return pl.ds(pl.multiple_of(i * 256, 256), 256)

    def permute(i, _):
        rows = rows_of(i)
        r = iota((256, 1), 0) + i * 256
        source = jnp.where(
            r < IMAGES * PATCHES,
            r + jnp.where(r >= PATCHES * s, PADDING, 0),
            PATCHES * s + r - IMAGES * PATCHES,
        )
        pick = (iota((256, LENGTH), 1) == source).astype(f32).astype(bf16)
        cp[rows] = dot(pick, cotv[...]).astype(bf16)
        x = dot(pick, tokv[...])
        xp[rows] = x.astype(bf16)
        standard, _unused = norm_rows(x)
        ni[rows] = (standard * ln1[...]).astype(bf16)
        return 0

    lax.fori_loop(0, 4, permute, 0)

    block = (iota((256, 256), 0) // HD == iota((256, 256), 1) // HD).astype(f32) * (1.0 / HD)
    block = block.astype(bf16)
    qg, kg = qgain[...], kgain[...]

    def head_norm(y, gain, pair_of, out, inv_out, factor):
        high, rest = split(y)
        centred = y - (dot(high, block) + dot(rest, block))
        inverse = lax.rsqrt(dot((centred * centred).astype(bf16), block) + EPS)
        standard = centred * inverse
        for half in range(2):
            lanes = slice(128 * half, 128 * half + 128)
            dest, inv_dest, dest_gain, pp = pair_of(half)
            dest[pp, 0:LENGTH, :] = (standard[:, lanes] * dest_gain).astype(bf16)
            inv_dest[pp] = inverse[:, lanes].astype(bf16)

    def project(p):
        for tile in range(3):
            parts = []
            for half in range(2):
                idx = 2 * tile + half
                part, m = idx // 3, idx % 3
                parts.append(wq[p, part, :, 128 * m : 128 * m + 128])
            y = dot(ni[...], jnp.concatenate(parts, axis=1))

            def pair_of(half, tile=tile):
                idx = 2 * tile + half
                pp = p * 3 + idx % 3
                if idx < 3:
                    return q, invq, qg * 0.125, pp
                return k, invk, kg, pp

            head_norm(y, None, pair_of, None, None, None)
        y = dot(ni[...], wq[p, 2]).astype(bf16)
        for m in range(3):
            v[p * 3 + m, 0:LENGTH, :] = y[:, 128 * m : 128 * m + 128]

    loads[2].wait()
    project(0)
    weights[0].wait()
    project(1)

    def low_lanes(rows):
        return iota((rows, 128), 1) < HD

    def two_heads(x, rows):
        low = low_lanes(rows)
        zero = jnp.zeros_like(x)
        return jnp.concatenate([jnp.where(low, x, zero), jnp.where(low, zero, x)], axis=0)

    def attend(pp, _):
        cols = pl.ds(pl.multiple_of(pp * 128, 128), 128)
        for start, rows, begin, end in WINDOWS:
            window = slice(start, start + rows)
            krows = 256 if rows > 48 else 48
            kwin = slice(start, start + krows)
            scores = dot_nt(two_heads(q[pp, window, :], rows), k[pp, kwin, :])
            weight = jnp.exp(scores).astype(bf16)
            kr = iota((krows, 256), 0) + start
            vone = jnp.concatenate([v[pp, kwin, :], jnp.ones((krows, 128), bf16)], axis=1)
            vone = jnp.where((kr >= begin) & (kr < end), vone, jnp.zeros_like(vone))
            both = dot(weight, vone)
            total = both[:, 128:]
            heads = both[:, :128] / total
            merged = jnp.where(low_lanes(rows), heads[:rows], heads[rows:]).astype(bf16)
            keep = iota((rows, 128), 0) + start < begin
            att[window, cols] = jnp.where(keep, att[window, cols], merged)
            lane = iota((rows, 128), 1) // 2
            sums = lse[window, :]
            sums = jnp.where((lane == 2 * pp) & ~keep, total[:rows], sums)
            sums = jnp.where((lane == 2 * pp + 1) & ~keep, total[rows:], sums)
            lse[window, :] = sums
        return 0

    lse[...] = jnp.ones_like(lse)
    lax.fori_loop(0, PAIRS, attend, 0)
    even = iota((LENGTH, 128), 1) % 2 == 0
    high, rest = split(-jnp.log(lse[...]))
    nlg[0:LENGTH, :] = jnp.where(even, high, rest)

    loads[3].wait()
    weights[1].wait()
    nm = big.at[:, pl.ds(1024, D)]
    act = big.at[:, pl.ds(0, 2 * FW)]
    gh = big.at[:, pl.ds(512, 2 * FW)]

    def middle(i, _):
        rows = rows_of(i)
        m = xp[rows].astype(f32) + dot(att[rows], wo[...])
        mid[rows] = m
        standard, _unused = norm_rows(m)
        nm[rows] = (standard * ln2[...]).astype(bf16)
        return 0

    lax.fori_loop(0, 4, middle, 0)

    def ff_loads(j, slot):
        cols = pl.ds(pl.multiple_of(j * FW, FW), FW)
        return [
            pltpu.make_async_copy(wup.at[:, cols], wus.at[slot, :, pl.ds(0, FW)], fsem.at[slot, 0]),
            pltpu.make_async_copy(
                wup_x.at[:, cols], wus.at[slot, :, pl.ds(FW, FW)], fsem.at[slot, 1]
            ),
            pltpu.make_async_copy(wdn.at[cols], wds.at[slot, pl.ds(0, FW)], fsem.at[slot, 2]),
            pltpu.make_async_copy(wdn_x.at[cols], wds.at[slot, pl.ds(FW, FW)], fsem.at[slot, 3]),
        ]

    weights[2].wait()
    weights[3].wait()
    for c in ff_loads(0, 0):
        c.start()
    outa[...] = jnp.zeros_like(outa)
    gna[...] = jnp.zeros_like(gna)

    def feed(j, _):
        slot = lax.rem(j, 2)
        for c in ff_loads(j, slot):
            c.wait()

        @pl.when(j < FF_CHUNKS - 1)
        def _():
            for c in ff_loads(j + 1, 1 - slot):
                c.start()

        wu, wd = wus[slot], wds[slot]
        for r in range(0, LENGTH, 256):
            rows = slice(r, r + 256)
            a, slope = gelu_and_slope(dot(nm[rows], wu))
            act[rows] = a.astype(bf16)
            gh[rows] = (dot_nt(cp[rows], wd) * slope).astype(bf16)
        outa[...] += dot(act[...], wd)
        gna[...] += dot_nt(gh[...], wu)
        up = dot_tn(nm[...], gh[...]).astype(bf16)
        dn = dot_tn(cp[...], act[...]).astype(bf16)
        for b in range(16):
            part = slice(48 * b, 48 * b + 48)
            af[j, places[b], :, 0:FW] = up[part, :FW]
            af[j, places[b], :, FW : 2 * FW] = dn[part, :FW]
            sbuf[slot, places[b], :, 0:FW] = up[part, FW:]
            sbuf[slot, places[b], :, FW : 2 * FW] = dn[part, FW:]
        for stage in range(4, -1, -1):

            @pl.when(j >= stage + 1)
            def _(stage=stage):
                advance(stage, j - stage - 1, True)

        rs_copy(0, j, True).start()
        return 0

    lax.fori_loop(0, FF_CHUNKS, feed, 0)

    def norm2_back(i, total):
        rows = rows_of(i)
        m = mid[rows]
        mid[rows] = m + outa[rows]
        standard, inverse = norm_rows(m)
        grad = gna[rows]
        grad_mid = cp[rows].astype(f32) + norm_rows_back(grad, standard, inverse, ln2[...])
        gna[rows] = grad_mid
        gb[rows] = grad_mid.astype(bf16)
        return total + jnp.sum(grad * standard, axis=0, keepdims=True)

    ln2_terms = lax.fori_loop(0, 4, norm2_back, jnp.zeros((1, D), f32))

    def put(c, slot, own, other):
        for b in range(16):
            part = slice(48 * b, 48 * b + 48)
            ap[c - FF_CHUNKS, places[b]] = own[part]
            sbuf[slot, places[b], :, 0:384] = other[part]

    pg = dot_tn(gb[...], att[...]).astype(bf16)
    put(FF_CHUNKS, 0, pg[:, :384], pg[:, 384:])
    event(FF_CHUNKS)

    ga = dot_nt(gb[...], wo[...])
    gab = ga.astype(bf16)
    for pp in range(PAIRS):
        do[pp, 0:LENGTH, :] = gab[:, 128 * pp : 128 * pp + 128]
    high, rest = split(gab.astype(f32) * att[...].astype(f32))
    gather = (iota((D, 128), 0) // HD == iota((D, 128), 1) // 2).astype(f32).astype(bf16)
    delta = dot(high, gather) + dot(rest, gather)
    high, rest = split(delta)
    dlt[0:LENGTH, :] = jnp.where(even, high, rest)

    block2 = (iota((256, 128), 0) % 128 // HD == iota((256, 128), 1) // HD).astype(f32) * (1.0 / HD)
    block2 = block2.astype(bf16)

    def head_mean(x):
        return dot(jnp.concatenate(split(x), axis=1), block2)

    def head_norm_back(grad, standard, inverse, gain):
        c = grad * gain
        return inverse * (c - head_mean(c) - standard * head_mean(c * standard))

    dq, dk, dv = (outa.at[:, pl.ds(128 * i, 128)] for i in range(3))

    def attend_back(pp, col):
        for start, rows, begin, end in WINDOWS:
            window = slice(start, start + rows)
            qrows = 256 if rows > 48 else 48
            qwin = slice(start, start + qrows)
            lane = iota((2 * rows, 128), 1)
            head = 2 * pp + jnp.where(iota((2 * rows, 128), 0) < rows, 0, 1)
            hot = (lane // 2 == head).astype(f32).astype(bf16)
            kb = k[pp, window, :]
            qb = q[pp, qwin, :]
            st = dot_nt(
                jnp.concatenate([two_heads(kb, rows), hot], axis=1),
                jnp.concatenate([qb, nlg[qwin, :]], axis=1),
            )
            pt = jnp.exp(st)
            qr = iota((qrows, 128), 0) + start
            valid = (qr >= begin) & (qr < end)
            dob = do[pp, qwin, :]
            zero = jnp.zeros_like(dob)
            dob = jnp.where(valid, dob, zero)
            dpt = dot_nt(
                jnp.concatenate([two_heads(v[pp, window, :], rows), -hot], axis=1),
                jnp.concatenate([dob, jnp.where(valid, dlt[qwin, :], zero)], axis=1),
            )
            dst = (pt * dpt).astype(bf16)
            dv2 = dot(pt.astype(bf16), dob)
            dk2 = dot(dst, qb)
            kr = iota((rows, 128), 0) + start
            kz = jnp.where((kr >= begin) & (kr < end), kb, jnp.zeros_like(kb))
            dq2 = dot_tn(dst, two_heads(kz, rows))[:rows]
            keep = kr < begin
            low = low_lanes(rows)
            dv[window, :] = jnp.where(keep, dv[window, :], jnp.where(low, dv2[:rows], dv2[rows:]))
            dk[window, :] = jnp.where(keep, dk[window, :], jnp.where(low, dk2[:rows], dk2[rows:]))
            dq[window, :] = jnp.where(keep, dq[window, :], dq2)
        standard = q[pp, 0:LENGTH, :].astype(f32) * (8.0 / qg)
        grad = dq[...] * 0.125
        q_terms = jnp.sum(grad * standard, axis=0, keepdims=True)
        big[:, col(0)] = head_norm_back(grad, standard, invq[pp].astype(f32), qg).astype(bf16)
        standard = k[pp, 0:LENGTH, :].astype(f32) * (1.0 / kg)
        grad = dk[...]
        k_terms = jnp.sum(grad * standard, axis=0, keepdims=True)
        big[:, col(1)] = head_norm_back(grad, standard, invk[pp].astype(f32), kg).astype(bf16)
        big[:, col(2)] = dv[...].astype(bf16)
        return q_terms, k_terms

    q_terms = jnp.zeros((1, 128), f32)
    k_terms = jnp.zeros((1, 128), f32)
    for m in range(3):

        def pair(i, carry, m=m):
            def col(part):
                return pl.ds(pl.multiple_of(768 * m + 384 * i + 128 * part, 128), 128)

            a, b = attend_back(3 * i + m, col)
            return carry[0] + a, carry[1] + b

        q_terms, k_terms = lax.fori_loop(0, 2, pair, (q_terms, k_terms))
        c = FF_CHUNKS + 1 + m
        both = dot_tn(ni[...], big[:, 768 * m : 768 * m + 768]).astype(bf16)
        put(c, c % 2, both[:, :384], both[:, 384:])
        event(c)

    def unpick(i):
        r = iota((256, 1), 0) + i * 256
        source = jnp.where(
            r < PATCHES * s,
            r,
            jnp.where(r < PATCHES * s + PADDING, r - PATCHES * s + IMAGES * PATCHES, r - PADDING),
        )
        return (iota((256, LENGTH), 1) == source).astype(f32).astype(bf16)

    def weight_of(m):
        return jnp.concatenate(
            [wq[p, part, :, 128 * m : 128 * m + 128] for p in range(2) for part in range(3)], axis=1
        )

    gsum = outa
    gsum[...] = dot_nt(big[:, 0:768], weight_of(0))
    gsum[...] += dot_nt(big[:, 768:1536], weight_of(1))
    event(CHUNKS)
    gsum[...] += dot_nt(big[:, 1536:2304], weight_of(2))
    igb = ni
    lob = cp

    def norm1_back(i, total):
        rows = rows_of(i)
        standard, inverse = norm_rows(xp[rows].astype(f32))
        grad = gsum[rows]
        igb[rows] = (gna[rows] + norm_rows_back(grad, standard, inverse, ln1[...])).astype(bf16)
        lob[rows] = mid[rows].astype(bf16)
        return total + jnp.sum(grad * standard, axis=0, keepdims=True)

    ln1_terms = lax.fori_loop(0, 4, norm1_back, jnp.zeros((1, D), f32))
    event(CHUNKS + 1)

    gsend[...] = jnp.zeros_like(gsend)
    for i in range(6):
        gsend[0, i : i + 1, :] = ln1_terms[:, 128 * i : 128 * i + 128]
        gsend[0, 6 + i : 7 + i, :] = ln2_terms[:, 128 * i : 128 * i + 128]
    gsend[0, 12:13, :] = q_terms
    gsend[0, 13:14, :] = k_terms

    def gain_copy(i):
        return pltpu.make_async_remote_copy(
            src_ref=gsend.at[i],
            dst_ref=grecv.at[i],
            send_sem=gssem.at[i],
            recv_sem=grsem.at[i],
            device_id=partners[i],
            device_id_type=MESH,
        )

    def gain_step(i):
        gain_copy(i).wait()
        total = gsend[i] + grecv[i]
        if i < 4:
            gsend[i + 1] = total
            gain_copy(i + 1).start()
        else:
            gains_out[...] = total

    gain_copy(0).start()

    def unpermute(i, _):
        rows = rows_of(i)
        pick = unpick(i)
        tokv[rows] = dot(pick, lob[...]).astype(bf16)
        cotv[rows] = dot(pick, igb[...]).astype(bf16)
        return 0

    lax.fori_loop(0, 4, unpermute, 0)
    outs = [
        pltpu.make_async_copy(tokv, lay_out, osem.at[0]),
        pltpu.make_async_copy(cotv, inp_out, osem.at[1]),
    ]
    for c in outs:
        c.start()
    gain_step(0)
    event(CHUNKS + 2)
    gain_step(1)
    gain_step(2)
    event(CHUNKS + 3)
    gain_step(3)
    gain_step(4)
    event(CHUNKS + 4)
    for c in outs:
        c.wait()


def local(
    tokens, segment, ln1_gain, w_qkv, q_gain, k_gain, w_out, ln2_gain, w_up, w_down, cotangent
):
    groups = lax.axis_size("dp")
    dp_low = groups // (1 << BITS)
    rows = D >> BITS
    own = lax.dynamic_slice_in_dim(segment, lax.axis_index("tensor") * LENGTH, LENGTH, 0)
    firsts = own[:: PATCHES][: IMAGES + 1]
    slot = jnp.sum(jnp.where(firsts == -1, jnp.arange(IMAGES + 1, dtype=jnp.int32), 0))
    hbm = pl.BlockSpec(memory_space=pl.ANY)
    vmem = pl.BlockSpec(memory_space=pltpu.VMEM)
    shape = jax.ShapeDtypeStruct
    half_ff = w_up.shape[1]
    ff, wide, n_proj = FF_CHUNKS, 2 * FW, CHUNKS - FF_CHUNKS

    def mem(*dims, dtype=bf16):
        return pltpu.VMEM(dims, dtype)

    outs = pl.pallas_call(
        functools.partial(kernel, dp_low),
        out_shape=(
            shape((LENGTH, D), bf16),
            shape((LENGTH, D), bf16),
            shape((rows, half_ff), f32),
            shape((rows, half_ff), f32),
            shape((rows, 384), f32),
            shape((3, rows, 384), f32),
            shape((16, 128), f32),
            shape((D, half_ff), bf16),
            shape((half_ff, D), bf16),
        ),
        in_specs=[pl.BlockSpec(memory_space=pltpu.SMEM), hbm, hbm, vmem, vmem, vmem, vmem]
        + [hbm] * 4,
        out_specs=(hbm, hbm, vmem, vmem, vmem, vmem, vmem, hbm, hbm),
        scratch_shapes=[
            mem(LENGTH, D),
            mem(LENGTH, D),
            mem(LENGTH, D),
            mem(LENGTH, D),
            mem(LENGTH, D),
            mem(PAIRS, PADDED, 128),
            mem(PAIRS, PADDED, 128),
            mem(PAIRS, PADDED, 128),
            mem(PAIRS, LENGTH, 128),
            mem(PAIRS, LENGTH, 128),
            mem(LENGTH, 128, dtype=f32),
            mem(PADDED, 128),
            mem(PADDED, 128),
            mem(LENGTH, D, dtype=f32),
            mem(LENGTH, D, dtype=f32),
            mem(LENGTH, D, dtype=f32),
            mem(LENGTH, 3 * D),
            mem(2, D, wide),
            mem(2, wide, D),
            mem(2, 3, D, 384),
            mem(D, D),
            mem(PAIRS, PADDED, 128),
            mem(2, 16, rows, wide),
            mem(2, 16, rows, wide),
            mem(ff, 16, rows, wide),
            mem(ff, 8, rows, wide),
            mem(ff, 4, rows, wide),
            mem(ff, 2, rows, wide),
            mem(ff, 1, rows, wide),
            mem(n_proj, 16, rows, 384),
            mem(n_proj, 8, rows, 384),
            mem(n_proj, 4, rows, 384),
            mem(n_proj, 2, rows, 384),
            mem(n_proj, 1, rows, 384),
            mem(5, 16, 128, dtype=f32),
            mem(5, 16, 128, dtype=f32),
            pltpu.SemaphoreType.DMA((CHUNKS, 5)),
            pltpu.SemaphoreType.DMA((CHUNKS, 5)),
            pltpu.SemaphoreType.DMA((5,)),
            pltpu.SemaphoreType.DMA((5,)),
            pltpu.SemaphoreType.DMA((4,)),
            pltpu.SemaphoreType.DMA((4,)),
            pltpu.SemaphoreType.DMA((4,)),
            pltpu.SemaphoreType.DMA((2, 4)),
            pltpu.SemaphoreType.DMA((2,)),
        ],
        compiler_params=pltpu.CompilerParams(
            collective_id=0, has_side_effects=True, vmem_limit_bytes=63 * 2**20
        ),
        name="layer",
    )(
        slot.reshape(1),
        tokens,
        cotangent,
        ln1_gain.reshape(1, D),
        ln2_gain.reshape(1, D),
        jnp.tile(q_gain, 2).reshape(1, 128),
        jnp.tile(k_gain, 2).reshape(1, 128),
        jnp.transpose(w_qkv, (1, 0, 2)),
        w_out,
        w_up,
        w_down,
    )
    layer_out, input_grad, up_grad, down_grad, proj_grad, qkv_grad, gains = outs[:7]
    if dp_low > 1:
        peers = [[hi * dp_low + lo for lo in range(dp_low)] for hi in range(1 << BITS)]

        def rest(x, axis):
            return lax.psum_scatter(
                x, "dp", scatter_dimension=axis, axis_index_groups=peers, tiled=True
            )

        up_grad, down_grad, proj_grad = rest(up_grad, 0), rest(down_grad, 0), rest(proj_grad, 0)
        qkv_grad = rest(qkv_grad, 1)
        gains = lax.psum(gains, "dp", axis_index_groups=peers)
    q_terms, k_terms = gains[12], gains[13]
    return (
        layer_out,
        input_grad,
        gains[0:6].reshape(D),
        jnp.transpose(qkv_grad, (1, 0, 2)),
        q_terms[:HD] + q_terms[HD:],
        k_terms[:HD] + k_terms[HD:],
        proj_grad.T,
        gains[6:12].reshape(D),
        up_grad,
        down_grad.T,
    )


def solution(mesh):
    return jax.shard_map(
        local,
        mesh=mesh,
        in_specs=(
            P(("dp", "tensor"), None),
            P("dp"),
            P(),
            P(None, None, "tensor"),
            P(),
            P(),
            P("tensor", None),
            P(),
            P(None, "tensor"),
            P("tensor", None),
            P(("dp", "tensor"), None),
        ),
        out_specs=(
            P(("dp", "tensor"), None),
            P(("dp", "tensor"), None),
            P(),
            P("dp", None, "tensor"),
            P(),
            P(),
            P("tensor", "dp"),
            P(),
            P("dp", "tensor"),
            P("tensor", "dp"),
        ),
        check_vma=False,
    )
```

```python
import functools

import jax
import jax.numpy as jnp
from jax import lax
from jax.experimental import pallas as pl
from jax.experimental.pallas import tpu as pltpu
from jax.sharding import PartitionSpec as P

D = 768
HD = 64
LENGTH = 1024
PATCHES = 196
IMAGES = 5
PADDING = LENGTH - IMAGES * PATCHES
PADDED = 1040
PAIRS = 6
EPS = 1e-06
MESH = pl.DeviceIdType.MESH
f32, bf16 = jnp.float32, jnp.bfloat16

WINDOWS = [
    (PATCHES * i // 16 * 16, 208, PATCHES * i, PATCHES * (i + 1)) for i in range(IMAGES)
] + [(976, 48, 980, 1024)]

FF_CHUNKS = 6
FW = 256
BITS = 4

CHUNKS = 12
START = list(range(10)) + [9, 9]
FF_LAG = (1, 3, 5, 7, 8)
LAG = [FF_LAG] * FF_CHUNKS + [(1, 3, 5, 6, 7)] + [(1, 2, 4, 5, 6)] * 2 + [(1, 2, 3, 4, 5)] * 3


def dot(left, right):
    return jnp.dot(left, right, preferred_element_type=f32)


def dot_nt(left, right):
    return lax.dot_general(left, right, (((1,), (1,)), ((), ())), preferred_element_type=f32)


def dot_tn(left, right):
    return lax.dot_general(left, right, (((0,), (0,)), ((), ())), preferred_element_type=f32)


def gelu_and_slope(h):
    e = jnp.exp(h * h * -0.5)
    t = 1.0 / (1.0 + jnp.abs(h) * (0.3275911 * 0.7071067811865476))
    poly = t * (
        0.5 * 0.254829592
        + t
        * (
            0.5 * -0.284496736
            + t * (0.5 * 1.421413741 + t * (0.5 * -1.453152027 + t * (0.5 * 1.061405429)))
        )
    )
    tail = poly * e
    phi = jnp.where(h >= 0, 1.0 - tail, tail)
    return h * phi, phi + h * e * 0.3989422804014327


def split(x):
    high = x.astype(bf16)
    return high, (x - high.astype(f32)).astype(bf16)


def iota(shape, axis):
    return lax.broadcasted_iota(jnp.int32, shape, axis)


def norm_rows(x):
    centred = x - jnp.mean(x, axis=-1, keepdims=True)
    inverse = lax.rsqrt(jnp.mean(centred * centred, axis=-1, keepdims=True) + EPS)
    return centred * inverse, inverse


def norm_rows_back(grad, standard, inverse, gain):
    c = grad * gain
    return inverse * (
        c
        - jnp.mean(c, axis=-1, keepdims=True)
        - standard * jnp.mean(c * standard, axis=-1, keepdims=True)
    )


def swap(pos):
    return (pos & 4) | (pos & 1) | ((pos & 8) >> 2) | ((pos & 2) << 2)


def kernel(
    dp_low,
    seg_hbm,
    tok,
    cot,
    ln1_hbm,
    ln2_hbm,
    qgain_hbm,
    kgain_hbm,
    wqkv,
    wout,
    wup,
    wdn,
    lay_out,
    inp_out,
    up_out,
    dn_out,
    pr_out,
    qk_out,
    gains_out,
    wup_x,
    wdn_x,
    seg,
    ln1v,
    ln2v,
    qgv,
    kgv,
    tokv,
    cotv,
    xp,
    cp,
    ni,
    q,
    k,
    v,
    invq,
    invk,
    nlg,
    dlt,
    mid,
    outa,
    gna,
    big,
    wus,
    wds,
    wq,
    wo,
    sbuf,
    r0,
    af,
    r1f,
    r2f,
    r3f,
    r4f,
    ap,
    r1p,
    r2p,
    r3p,
    r4p,
    gsend,
    grecv,
    ssem,
    rsem,
    gssem,
    grsem,
    wssem,
    wrsem,
    lsem,
    fsem,
    osem,
):
    att = tokv
    gb = cotv
    lse = mid.at[:, pl.ds(0, 128)]
    do = wds
    g = lax.axis_index("dp")
    t = lax.axis_index("tensor")
    top, low = g // dp_low, g % dp_low
    mine = [(top // (1 << b)) % 2 for b in range(BITS)]

    def peer(b):
        return ((top + (1 - 2 * mine[b]) * (1 << b)) * dp_low + low, t)

    d0, d1 = peer(0)[0], peer(1)[0]
    core = (g, 1 - t)
    first = (jnp.where(t == 0, d0, d1), t)
    third = (jnp.where(t == 0, d1, d0), t)
    partners = (core, first, peer(2), third, peer(3))

    def place(b):
        rel = [mine[i] if (b >> i) & 1 == 0 else 1 - mine[i] for i in range(BITS)]
        one = rel[0] * 8 + rel[1] * 2
        two = rel[1] * 8 + rel[0] * 2
        return one + t * (two - one) + rel[2] * 4 + rel[3]

    places = [place(b) for b in range(16)]

    barrier = pltpu.get_barrier_semaphore()
    for partner in partners:
        pl.semaphore_signal(barrier, inc=1, device_id=partner, device_id_type=MESH)

    loads = [
        pltpu.make_async_copy(tok, tokv, lsem.at[0]),
        pltpu.make_async_copy(cot, cotv, lsem.at[1]),
        pltpu.make_async_copy(wqkv, wq.at[0], lsem.at[2]),
        pltpu.make_async_copy(wout, wo.at[pl.ds(0, 384)], lsem.at[3]),
        pltpu.make_async_copy(seg_hbm, seg, lsem.at[4]),
        pltpu.make_async_copy(ln1_hbm, ln1v, lsem.at[5]),
        pltpu.make_async_copy(ln2_hbm, ln2v, lsem.at[6]),
        pltpu.make_async_copy(qgain_hbm, qgv, lsem.at[7]),
        pltpu.make_async_copy(kgain_hbm, kgv, lsem.at[8]),
    ]
    for c in loads[4:] + loads[:4]:
        c.start()

    def weight_copy(i, src, dst):
        return pltpu.make_async_remote_copy(
            src_ref=src,
            dst_ref=dst,
            send_sem=wssem.at[i],
            recv_sem=wrsem.at[i],
            device_id=core,
            device_id_type=MESH,
        )

    weights = [
        weight_copy(0, wqkv, wq.at[1]),
        weight_copy(1, wout, wo.at[pl.ds(384, 384)]),
        weight_copy(2, wup, wup_x),
        weight_copy(3, wdn, wdn_x),
    ]

    def chunk_refs(c, is_ff):
        if is_ff:
            slot = lax.rem(c, 2)
            return sbuf.at[slot], r0.at[slot], af.at[c], [r.at[c] for r in (r1f, r2f, r3f, r4f)]
        n = min(c, 9) - FF_CHUNKS
        lanes = pl.ds(128 * (c - 9), 128) if c >= 9 else pl.ds(0, 384)
        slot = min(c, 9) % 2
        return (
            sbuf.at[slot, :, :, lanes],
            r0.at[slot, :, :, lanes],
            ap.at[n, :, :, lanes],
            [r.at[n, :, :, lanes] for r in (r1p, r2p, r3p, r4p)],
        )

    def rs_copy(stage, c, is_ff):
        src, dst, a, rs = chunk_refs(c, is_ff)
        if stage > 0:
            half = 16 >> stage
            src, dst = a.at[pl.ds(half, half)], rs[stage - 1]
        return pltpu.make_async_remote_copy(
            src_ref=src,
            dst_ref=dst,
            send_sem=ssem.at[c, stage],
            recv_sem=rsem.at[c, stage],
            device_id=partners[stage],
            device_id_type=MESH,
        )

    def finish(c, is_ff, total):
        if is_ff:
            cols = pl.ds(pl.multiple_of(c * FW, FW), FW)
            up_out[:, cols] = total[:, :FW]
            dn_out[:, cols] = total[:, FW:]
        elif c == FF_CHUNKS:
            pr_out[...] = total
        elif c < 9:
            m = c - FF_CHUNKS - 1
            for part in range(3):
                qk_out[part, :, 128 * m : 128 * m + 128] = total[:, 128 * part : 128 * part + 128]
        else:
            qk_out[c - 9, :, 256:384] = total

    def advance(stage, c, is_ff):
        _src, arrived, a, rs = chunk_refs(c, is_ff)
        rs_copy(stage, c, is_ff).wait()
        if stage == 0:
            for pos in range(16):
                a[pos] = a[pos] + arrived[swap(pos)]
        elif stage < 4:
            half = 16 >> stage
            for pos in range(half):
                a[pos] = a[pos] + rs[stage - 1][pos]
        else:
            finish(c, is_ff, a[0].astype(f32) + rs[3][0].astype(f32))
        if stage < 4:
            rs_copy(stage + 1, c, is_ff).start()

    def event(e):
        for stage in range(4, -1, -1):
            for c in range(CHUNKS):
                if START[c] + LAG[c][stage] == e:
                    advance(stage, c, c < FF_CHUNKS)
        for c in range(CHUNKS):
            if START[c] == e:
                rs_copy(0, c, c < FF_CHUNKS).start()

    for c in loads[4:]:
        c.wait()
    s = jnp.int32(0)
    for image in range(IMAGES + 1):
        s = s + jnp.where(seg[t * LENGTH + PATCHES * image] == -1, image, 0)
    ln1 = ln1v[...].reshape(1, D)
    ln2 = ln2v[...].reshape(1, D)
    qg = qgv[...].reshape(1, HD)
    qg = jnp.concatenate([qg, qg], axis=1)
    kg = kgv[...].reshape(1, HD)
    kg = jnp.concatenate([kg, kg], axis=1)
    zero_rows = jnp.zeros((PADDED - LENGTH, 128), bf16)
    for pp in range(PAIRS):
        for ref in (q, k, v):
            ref[pp, LENGTH:, :] = zero_rows
    do[LENGTH:, :] = jnp.zeros((PADDED - LENGTH, D), bf16)
    nlg[LENGTH:, :] = zero_rows
    dlt[LENGTH:, :] = zero_rows

    def rows_of(i):
        return pl.ds(pl.multiple_of(i * 256, 256), 256)

    def permute(i, _):
        rows = rows_of(i)
        r = iota((256, 1), 0) + i * 256
        source = jnp.where(
            r < IMAGES * PATCHES,
            r + jnp.where(r >= PATCHES * s, PADDING, 0),
            PATCHES * s + r - IMAGES * PATCHES,
        )
        pick = (iota((256, LENGTH), 1) == source).astype(f32).astype(bf16)
        cp[rows] = dot(pick, cotv[...]).astype(bf16)
        x = dot(pick, tokv[...])
        xp[rows] = x.astype(bf16)
        standard, _unused = norm_rows(x)
        ni[rows] = (standard * ln1).astype(bf16)
        return 0

    loads[0].wait()
    loads[1].wait()
    lax.fori_loop(0, 2, permute, 0)
    pl.semaphore_wait(barrier, len(partners))
    for c in weights:
        c.start()
    lax.fori_loop(2, 4, permute, 0)

    block = (iota((256, 256), 0) // HD == iota((256, 256), 1) // HD).astype(f32) * (1.0 / HD)
    block = block.astype(bf16)

    def head_norm(y, pair_of):
        high, rest = split(y)
        centred = y - (dot(high, block) + dot(rest, block))
        inverse = lax.rsqrt(dot((centred * centred).astype(bf16), block) + EPS)
        standard = centred * inverse
        for half in range(2):
            lanes = slice(128 * half, 128 * half + 128)
            dest, inv_dest, dest_gain, pp = pair_of(half)
            dest[pp, 0:LENGTH, :] = (standard[:, lanes] * dest_gain).astype(bf16)
            inv_dest[pp] = inverse[:, lanes].astype(bf16)

    def project(p):
        for tile in range(3):
            parts = []
            for half in range(2):
                idx = 2 * tile + half
                part, m = idx // 3, idx % 3
                parts.append(wq[p, part, :, 128 * m : 128 * m + 128])
            y = dot(ni[...], jnp.concatenate(parts, axis=1))

            def pair_of(half, tile=tile):
                idx = 2 * tile + half
                pp = p * 3 + idx % 3
                if idx < 3:
                    return q, invq, qg * 0.125, pp
                return k, invk, kg, pp

            head_norm(y, pair_of)
        y = dot(ni[...], wq[p, 2]).astype(bf16)
        for m in range(3):
            v[p * 3 + m, 0:LENGTH, :] = y[:, 128 * m : 128 * m + 128]

    loads[2].wait()
    project(0)
    weights[0].wait()
    project(1)

    def low_lanes(rows):
        return iota((rows, 128), 1) < HD

    def two_heads(x, rows):
        low = low_lanes(rows)
        zero = jnp.zeros_like(x)
        return jnp.concatenate([jnp.where(low, x, zero), jnp.where(low, zero, x)], axis=0)

    def attend(pp, _):
        cols = pl.ds(pl.multiple_of(pp * 128, 128), 128)
        for start, rows, begin, end in WINDOWS:
            window = slice(start, start + rows)
            krows = 256 if rows > 48 else 48
            kwin = slice(start, start + krows)
            scores = dot_nt(two_heads(q[pp, window, :], rows), k[pp, kwin, :])
            weight = jnp.exp(scores).astype(bf16)
            kr = iota((krows, 256), 0) + start
            vone = jnp.concatenate([v[pp, kwin, :], jnp.ones((krows, 128), bf16)], axis=1)
            vone = jnp.where((kr >= begin) & (kr < end), vone, jnp.zeros_like(vone))
            both = dot(weight, vone)
            total = both[:, 128:]
            heads = both[:, :128] / total
            merged = jnp.where(low_lanes(rows), heads[:rows], heads[rows:]).astype(bf16)
            keep = iota((rows, 128), 0) + start < begin
            att[window, cols] = jnp.where(keep, att[window, cols], merged)
            lane = iota((rows, 128), 1) // 2
            sums = lse[window, :]
            sums = jnp.where((lane == 2 * pp) & ~keep, total[:rows], sums)
            sums = jnp.where((lane == 2 * pp + 1) & ~keep, total[rows:], sums)
            lse[window, :] = sums
        return 0

    lse[...] = jnp.ones_like(lse)
    lax.fori_loop(0, PAIRS, attend, 0)
    even = iota((LENGTH, 128), 1) % 2 == 0
    high, rest = split(-jnp.log(lse[...]))
    nlg[0:LENGTH, :] = jnp.where(even, high, rest)

    loads[3].wait()
    weights[1].wait()
    nm = big.at[:, pl.ds(1024, D)]
    act = big.at[:, pl.ds(0, 2 * FW)]
    gh = big.at[:, pl.ds(512, 2 * FW)]

    def middle(i, _):
        rows = rows_of(i)
        m = xp[rows].astype(f32) + dot(att[rows], wo[...])
        mid[rows] = m
        standard, _unused = norm_rows(m)
        nm[rows] = (standard * ln2).astype(bf16)
        return 0

    lax.fori_loop(0, 4, middle, 0)

    def down_rows(i):
        return wds.at[pl.ds(pl.multiple_of(i * FW, FW), FW)]

    def ff_loads(j, slot):
        cols = pl.ds(pl.multiple_of(j * FW, FW), FW)
        return [
            pltpu.make_async_copy(wup.at[:, cols], wus.at[slot, :, pl.ds(0, FW)], fsem.at[slot, 0]),
            pltpu.make_async_copy(
                wup_x.at[:, cols], wus.at[slot, :, pl.ds(FW, FW)], fsem.at[slot, 1]
            ),
            pltpu.make_async_copy(wdn.at[cols], down_rows(2 * slot), fsem.at[slot, 2]),
            pltpu.make_async_copy(wdn_x.at[cols], down_rows(2 * slot + 1), fsem.at[slot, 3]),
        ]

    weights[2].wait()
    weights[3].wait()
    for c in ff_loads(0, 0):
        c.start()
    outa[...] = jnp.zeros_like(outa)
    gna[...] = jnp.zeros_like(gna)

    def feed(j, _):
        slot = lax.rem(j, 2)
        for c in ff_loads(j, slot):
            c.wait()

        @pl.when(j < FF_CHUNKS - 1)
        def _():
            for c in ff_loads(j + 1, 1 - slot):
                c.start()

        wu = wus[slot]
        wd = wds[pl.ds(pl.multiple_of(slot * 2 * FW, 2 * FW), 2 * FW), :]
        for r in range(0, LENGTH, 256):
            rows = slice(r, r + 256)
            a, slope = gelu_and_slope(dot(nm[rows], wu))
            act[rows] = a.astype(bf16)
            gh[rows] = (dot_nt(cp[rows], wd) * slope).astype(bf16)
        outa[...] += dot(act[...], wd)
        gna[...] += dot_nt(gh[...], wu)
        up = dot_tn(nm[...], gh[...]).astype(bf16)
        dn = dot_tn(cp[...], act[...]).astype(bf16)
        for b in range(16):
            part = slice(48 * b, 48 * b + 48)
            af[j, places[b], :, 0:FW] = up[part, :FW]
            af[j, places[b], :, FW : 2 * FW] = dn[part, :FW]
            sbuf[slot, places[b], :, 0:FW] = up[part, FW:]
            sbuf[slot, places[b], :, FW : 2 * FW] = dn[part, FW:]
        for stage in range(4, -1, -1):
            lag = FF_LAG[stage]
            if lag < FF_CHUNKS:

                @pl.when(j >= lag)
                def _(stage=stage, lag=lag):
                    advance(stage, j - lag, True)

        rs_copy(0, j, True).start()
        return 0

    lax.fori_loop(0, FF_CHUNKS, feed, 0)

    def norm2_back(i, total):
        rows = rows_of(i)
        m = mid[rows]
        mid[rows] = m + outa[rows]
        standard, inverse = norm_rows(m)
        grad = gna[rows]
        grad_mid = cp[rows].astype(f32) + norm_rows_back(grad, standard, inverse, ln2)
        gna[rows] = grad_mid
        gb[rows] = grad_mid.astype(bf16)
        return total + jnp.sum(grad * standard, axis=0, keepdims=True)

    ln2_terms = lax.fori_loop(0, 4, norm2_back, jnp.zeros((1, D), f32))

    def put(c, slot, own, other):
        for b in range(16):
            part = slice(48 * b, 48 * b + 48)
            ap[c - FF_CHUNKS, places[b]] = own[part]
            sbuf[slot, places[b], :, 0:384] = other[part]

    pg = dot_tn(gb[...], att[...]).astype(bf16)
    put(FF_CHUNKS, 0, pg[:, :384], pg[:, 384:])
    event(FF_CHUNKS)

    ga = dot_nt(gb[...], wo[...])
    gab = ga.astype(bf16)
    do[0:LENGTH, :] = gab
    high, rest = split(gab.astype(f32) * att[...].astype(f32))
    gather = (iota((D, 128), 0) // HD == iota((D, 128), 1) // 2).astype(f32).astype(bf16)
    delta = dot(high, gather) + dot(rest, gather)
    high, rest = split(delta)
    dlt[0:LENGTH, :] = jnp.where(even, high, rest)

    block2 = (iota((256, 128), 0) % 128 // HD == iota((256, 128), 1) // HD).astype(f32) * (1.0 / HD)
    block2 = block2.astype(bf16)

    def head_mean(x):
        return dot(jnp.concatenate(split(x), axis=1), block2)

    def head_norm_back(grad, standard, inverse, gain):
        c = grad * gain
        return inverse * (c - head_mean(c) - standard * head_mean(c * standard))

    dq, dk, dv = (outa.at[:, pl.ds(128 * i, 128)] for i in range(3))

    def attend_back(pp, col):
        for start, rows, begin, end in WINDOWS:
            window = slice(start, start + rows)
            qrows = 256 if rows > 48 else 48
            qwin = slice(start, start + qrows)
            lane = iota((2 * rows, 128), 1)
            head = 2 * pp + jnp.where(iota((2 * rows, 128), 0) < rows, 0, 1)
            hot = (lane // 2 == head).astype(f32).astype(bf16)
            kb = k[pp, window, :]
            qb = q[pp, qwin, :]
            st = dot_nt(
                jnp.concatenate([two_heads(kb, rows), hot], axis=1),
                jnp.concatenate([qb, nlg[qwin, :]], axis=1),
            )
            pt = jnp.exp(st)
            qr = iota((qrows, 128), 0) + start
            valid = (qr >= begin) & (qr < end)
            dob = do[qwin, pl.ds(pl.multiple_of(pp * 128, 128), 128)]
            zero = jnp.zeros_like(dob)
            dob = jnp.where(valid, dob, zero)
            dpt = dot_nt(
                jnp.concatenate([two_heads(v[pp, window, :], rows), -hot], axis=1),
                jnp.concatenate([dob, jnp.where(valid, dlt[qwin, :], zero)], axis=1),
            )
            dst = (pt * dpt).astype(bf16)
            dv2 = dot(pt.astype(bf16), dob)
            dk2 = dot(dst, qb)
            kr = iota((rows, 128), 0) + start
            kz = jnp.where((kr >= begin) & (kr < end), kb, jnp.zeros_like(kb))
            dq2 = dot_tn(dst, two_heads(kz, rows))[:rows]
            keep = kr < begin
            low = low_lanes(rows)
            dv[window, :] = jnp.where(keep, dv[window, :], jnp.where(low, dv2[:rows], dv2[rows:]))
            dk[window, :] = jnp.where(keep, dk[window, :], jnp.where(low, dk2[:rows], dk2[rows:]))
            dq[window, :] = jnp.where(keep, dq[window, :], dq2)
        standard = q[pp, 0:LENGTH, :].astype(f32) * (8.0 / qg)
        grad = dq[...] * 0.125
        q_terms = jnp.sum(grad * standard, axis=0, keepdims=True)
        big[:, col(0)] = head_norm_back(grad, standard, invq[pp].astype(f32), qg).astype(bf16)
        standard = k[pp, 0:LENGTH, :].astype(f32) * (1.0 / kg)
        grad = dk[...]
        k_terms = jnp.sum(grad * standard, axis=0, keepdims=True)
        big[:, col(1)] = head_norm_back(grad, standard, invk[pp].astype(f32), kg).astype(bf16)
        big[:, col(2)] = dv[...].astype(bf16)
        return q_terms, k_terms

    def weight_of(m):
        return jnp.concatenate(
            [wq[p, part, :, 128 * m : 128 * m + 128] for p in range(2) for part in range(3)], axis=1
        )

    def gain_copy(i):
        return pltpu.make_async_remote_copy(
            src_ref=gsend.at[i],
            dst_ref=grecv.at[i],
            send_sem=gssem.at[i],
            recv_sem=grsem.at[i],
            device_id=partners[i],
            device_id_type=MESH,
        )

    def gain_step(i):
        gain_copy(i).wait()
        total = gsend[i] + grecv[i]
        if i < 4:
            gsend[i + 1] = total
            gain_copy(i + 1).start()
        else:
            gains_out[...] = total

    ln1_sum = jnp.zeros((D, 128), f32)
    q_terms = jnp.zeros((1, 128), f32)
    k_terms = jnp.zeros((1, 128), f32)
    for m in range(3):

        def pair(i, carry, m=m):
            def col(part):
                return pl.ds(pl.multiple_of(768 * m + 384 * i + 128 * part, 128), 128)

            a, b = attend_back(3 * i + m, col)
            return carry[0] + a, carry[1] + b

        q_terms, k_terms = lax.fori_loop(0, 2, pair, (q_terms, k_terms))
        both = dot_tn(ni[...], big[:, 768 * m : 768 * m + 768])
        wide = both * weight_of(m).astype(f32)
        for tile in range(6):
            ln1_sum = ln1_sum + wide[:, 128 * tile : 128 * tile + 128]
        both = both.astype(bf16)
        c = FF_CHUNKS + 1 + m
        put(c, c % 2, both[:, :384], both[:, 384:])
        if m == 2:
            high, rest = split(ln1_sum)
            ones = jnp.ones((16, 128), bf16)
            ln1_terms = (dot_nt(ones, high) + dot_nt(ones, rest))[0:1] / ln1
            gsend[0] = jnp.concatenate(
                [ln1_terms[:, 128 * i : 128 * i + 128] for i in range(6)]
                + [ln2_terms[:, 128 * i : 128 * i + 128] for i in range(6)]
                + [q_terms, k_terms, jnp.zeros((2, 128), f32)],
                axis=0,
            )
            gain_copy(0).start()
        event(c)

    def unpick(i):
        r = iota((256, 1), 0) + i * 256
        source = jnp.where(
            r < PATCHES * s,
            r,
            jnp.where(r < PATCHES * s + PADDING, r - PATCHES * s + IMAGES * PATCHES, r - PADDING),
        )
        return (iota((256, LENGTH), 1) == source).astype(f32).astype(bf16)

    gsum = outa
    gsum[...] = dot_nt(big[:, 0:768], weight_of(0))
    gsum[...] += dot_nt(big[:, 768:1536], weight_of(1))
    event(10)
    gain_step(0)
    gsum[...] += dot_nt(big[:, 1536:2304], weight_of(2))
    gain_step(1)
    igb = ni
    lob = cp

    def norm1_back(i, _):
        rows = rows_of(i)
        standard, inverse = norm_rows(xp[rows].astype(f32))
        grad = gsum[rows]
        igb[rows] = (gna[rows] + norm_rows_back(grad, standard, inverse, ln1)).astype(bf16)
        lob[rows] = mid[rows].astype(bf16)
        return 0

    lax.fori_loop(0, 4, norm1_back, 0)
    event(11)
    gain_step(2)

    def unpermute(i, _):
        rows = rows_of(i)
        pick = unpick(i)
        tokv[rows] = dot(pick, lob[...]).astype(bf16)
        cotv[rows] = dot(pick, igb[...]).astype(bf16)
        return 0

    lax.fori_loop(0, 2, unpermute, 0)
    event(12)
    gain_step(3)
    lax.fori_loop(2, 4, unpermute, 0)
    outs = [
        pltpu.make_async_copy(tokv, lay_out, osem.at[0]),
        pltpu.make_async_copy(cotv, inp_out, osem.at[1]),
    ]
    for c in outs:
        c.start()
    event(13)
    gain_step(4)
    event(14)
    for c in outs:
        c.wait()


def hand_on(*refs):
    n = 6
    ins, gains = refs[:n], refs[n]
    outs, (ln1, ln2, qg, kg) = refs[n + 1 : 2 * n + 1], refs[2 * n + 1 : 2 * n + 5]
    held, sems = refs[2 * n + 5 : 3 * n + 5], refs[-1]
    copies = []
    for i, (src, dst) in enumerate(zip(ins, outs)):
        parts = 4 if src.shape[0] == LENGTH else 1
        size = src.shape[0] // parts
        for part in range(parts):
            rows = pl.ds(part * size, size)
            sem = sems.at[4 * i + part]
            copies.append(
                (
                    pltpu.make_async_copy(src.at[rows], held[i].at[rows], sem),
                    pltpu.make_async_copy(held[i].at[rows], dst.at[rows], sem),
                )
            )
    for come, _go in copies:
        come.start()
    for i in range(6):
        ln1[pl.ds(128 * i, 128)] = gains[i, :]
        ln2[pl.ds(128 * i, 128)] = gains[6 + i, :]
    qg[...] = gains[12, 0:HD] + gains[12, HD : 2 * HD]
    kg[...] = gains[13, 0:HD] + gains[13, HD : 2 * HD]
    for come, go in copies:
        come.wait()
        go.start()
    for _come, go in copies:
        go.wait()


def local(
    tokens, segment, ln1_gain, w_qkv, q_gain, k_gain, w_out, ln2_gain, w_up, w_down, cotangent
):
    groups = lax.axis_size("dp")
    dp_low = groups // (1 << BITS)
    rows = D >> BITS
    hbm = pl.BlockSpec(memory_space=pl.ANY)
    vmem = pl.BlockSpec(memory_space=pltpu.VMEM)
    shape = jax.ShapeDtypeStruct
    half_ff = w_up.shape[1]
    ff, wide, n_proj = FF_CHUNKS, 2 * FW, CHUNKS - FF_CHUNKS

    def mem(*dims, dtype=bf16):
        return pltpu.VMEM(dims, dtype)

    outs = pl.pallas_call(
        functools.partial(kernel, dp_low),
        out_shape=(
            shape((LENGTH, D), bf16),
            shape((LENGTH, D), bf16),
            shape((rows, half_ff), f32),
            shape((rows, half_ff), f32),
            shape((rows, 384), f32),
            shape((3, rows, 384), f32),
            shape((16, 128), f32),
            shape((D, half_ff), bf16),
            shape((half_ff, D), bf16),
        ),
        in_specs=[hbm] * 11,
        out_specs=(hbm, hbm, vmem, vmem, vmem, vmem, vmem, hbm, hbm),
        scratch_shapes=[
            pltpu.SMEM(segment.shape, jnp.int32),
            mem(D, dtype=f32),
            mem(D, dtype=f32),
            mem(HD, dtype=f32),
            mem(HD, dtype=f32),
            mem(LENGTH, D),
            mem(LENGTH, D),
            mem(LENGTH, D),
            mem(LENGTH, D),
            mem(LENGTH, D),
            mem(PAIRS, PADDED, 128),
            mem(PAIRS, PADDED, 128),
            mem(PAIRS, PADDED, 128),
            mem(PAIRS, LENGTH, 128),
            mem(PAIRS, LENGTH, 128),
            mem(PADDED, 128),
            mem(PADDED, 128),
            mem(LENGTH, D, dtype=f32),
            mem(LENGTH, D, dtype=f32),
            mem(LENGTH, D, dtype=f32),
            mem(LENGTH, 3 * D),
            mem(2, D, wide),
            mem(PADDED, D),
            mem(2, 3, D, 384),
            mem(D, D),
            mem(2, 16, rows, wide),
            mem(2, 16, rows, wide),
            mem(ff, 16, rows, wide),
            mem(ff, 8, rows, wide),
            mem(ff, 4, rows, wide),
            mem(ff, 2, rows, wide),
            mem(ff, 1, rows, wide),
            mem(n_proj, 16, rows, 384),
            mem(n_proj, 8, rows, 384),
            mem(n_proj, 4, rows, 384),
            mem(n_proj, 2, rows, 384),
            mem(n_proj, 1, rows, 384),
            mem(5, 16, 128, dtype=f32),
            mem(5, 16, 128, dtype=f32),
            pltpu.SemaphoreType.DMA((CHUNKS, 5)),
            pltpu.SemaphoreType.DMA((CHUNKS, 5)),
            pltpu.SemaphoreType.DMA((5,)),
            pltpu.SemaphoreType.DMA((5,)),
            pltpu.SemaphoreType.DMA((4,)),
            pltpu.SemaphoreType.DMA((4,)),
            pltpu.SemaphoreType.DMA((9,)),
            pltpu.SemaphoreType.DMA((2, 4)),
            pltpu.SemaphoreType.DMA((2,)),
        ],
        compiler_params=pltpu.CompilerParams(
            collective_id=0, has_side_effects=True, vmem_limit_bytes=63 * 2**20
        ),
        name="layer",
    )(
        segment,
        tokens,
        cotangent,
        ln1_gain,
        ln2_gain,
        q_gain,
        k_gain,
        jnp.transpose(w_qkv, (1, 0, 2)),
        w_out,
        w_up,
        w_down,
    )
    results, gains = list(outs[:6]), outs[6]
    if dp_low > 1:
        peers = [[hi * dp_low + lo for lo in range(dp_low)] for hi in range(1 << BITS)]

        def rest(x, axis):
            return lax.psum_scatter(
                x, "dp", scatter_dimension=axis, axis_index_groups=peers, tiled=True
            )

        results[2:] = [rest(x, x.ndim - 2) for x in results[2:]]
        gains = lax.psum(gains, "dp", axis_index_groups=peers)
    (
        layer_out,
        input_grad,
        up_grad,
        down_grad,
        proj_grad,
        qkv_grad,
        ln1_grad,
        ln2_grad,
        q_grad,
        k_grad,
    ) = pl.pallas_call(
        hand_on,
        out_shape=[shape(x.shape, x.dtype) for x in results]
        + [shape((D,), f32)] * 2
        + [shape((HD,), f32)] * 2,
        in_specs=[pl.BlockSpec(memory_space=pltpu.HBM)] * 6 + [vmem],
        out_specs=[pl.BlockSpec(memory_space=pltpu.HBM)] * 6 + [vmem] * 4,
        scratch_shapes=[pltpu.VMEM(x.shape, x.dtype) for x in results]
        + [pltpu.SemaphoreType.DMA((24,))],
        name="hand_on",
    )(*results, gains)
    return (
        layer_out,
        input_grad,
        ln1_grad,
        jnp.transpose(qkv_grad, (1, 0, 2)),
        q_grad,
        k_grad,
        proj_grad.T,
        ln2_grad,
        up_grad,
        down_grad.T,
    )


def solution(mesh):
    return jax.shard_map(
        local,
        mesh=mesh,
        in_specs=(
            P(("dp", "tensor"), None),
            P("dp"),
            P(),
            P(None, None, "tensor"),
            P(),
            P(),
            P("tensor", None),
            P(),
            P(None, "tensor"),
            P("tensor", None),
            P(("dp", "tensor"), None),
        ),
        out_specs=(
            P(("dp", "tensor"), None),
            P(("dp", "tensor"), None),
            P(),
            P("dp", None, "tensor"),
            P(),
            P(),
            P("tensor", "dp"),
            P(),
            P("dp", "tensor"),
            P("tensor", "dp"),
        ),
        check_vma=False,
    )
```

```python
import functools

import jax
import jax.numpy as jnp
from jax import lax
from jax.experimental import pallas as pl
from jax.experimental.pallas import tpu as pltpu
from jax.sharding import PartitionSpec as P

D = 768
HD = 64
LENGTH = 1024
PATCHES = 196
IMAGES = 5
PADDING = LENGTH - IMAGES * PATCHES
PADDED = 1040
PAIRS = 6
EPS = 1e-06
MESH = pl.DeviceIdType.MESH
f32, bf16 = jnp.float32, jnp.bfloat16

WINDOWS = [
    (PATCHES * i // 16 * 16, 208, PATCHES * i, PATCHES * (i + 1)) for i in range(IMAGES)
] + [(976, 48, 980, 1024)]

FF_CHUNKS = 6
FW = 256
BITS = 4

CHUNKS = 12
START = [0, 1, 2, 3, 4, 5, 6, 8, 10, 12, 12, 12]
FF_LAG = (1, 3, 5, 7, 10)
LAG = [FF_LAG] * FF_CHUNKS + [(1, 3, 5, 6, 9), (1, 3, 5, 6, 8), (1, 3, 4, 5, 7)] + [(1, 2, 3, 4, 5)] * 3

TILES_IN = [
    (0, 256, [(0, 384)]),
    (256, 256, [(256, 384)]),
    (512, 256, [(512, 384)]),
    (768, 128, [(768, 256)]),
    (896, 128, [(0, 1024)]),
]
TILES_OUT = [
    (0, 256, [(0, 256), (896, 128)]),
    (256, 256, [(128, 384), (896, 128)]),
    (512, 256, [(384, 384), (896, 128)]),
    (768, 256, [(640, 384)]),
]


def dot(left, right):
    return jnp.dot(left, right, preferred_element_type=f32)


def dot_nt(left, right):
    return lax.dot_general(left, right, (((1,), (1,)), ((), ())), preferred_element_type=f32)


def dot_tn(left, right):
    return lax.dot_general(left, right, (((0,), (0,)), ((), ())), preferred_element_type=f32)


def gelu_and_slope(h):
    e = jnp.exp(h * h * -0.5)
    t = 1.0 / (1.0 + jnp.abs(h) * (0.3275911 * 0.7071067811865476))
    poly = t * (
        0.5 * 0.254829592
        + t
        * (
            0.5 * -0.284496736
            + t * (0.5 * 1.421413741 + t * (0.5 * -1.453152027 + t * (0.5 * 1.061405429)))
        )
    )
    tail = poly * e
    phi = jnp.where(h >= 0, 1.0 - tail, tail)
    return h * phi, phi + h * e * 0.3989422804014327


def split(x):
    high = x.astype(bf16)
    return high, (x - high.astype(f32)).astype(bf16)


def iota(shape, axis):
    return lax.broadcasted_iota(jnp.int32, shape, axis)


def norm_rows(x):
    centred = x - jnp.mean(x, axis=-1, keepdims=True)
    inverse = lax.rsqrt(jnp.mean(centred * centred, axis=-1, keepdims=True) + EPS)
    return centred * inverse, inverse


def norm_rows_back(grad, standard, inverse, gain):
    c = grad * gain
    return inverse * (
        c
        - jnp.mean(c, axis=-1, keepdims=True)
        - standard * jnp.mean(c * standard, axis=-1, keepdims=True)
    )


def swap(pos):
    return (pos & 4) | (pos & 1) | ((pos & 8) >> 2) | ((pos & 2) << 2)


def kernel(
    dp_low,
    seg_hbm,
    tok,
    cot,
    ln1_hbm,
    ln2_hbm,
    qgain_hbm,
    kgain_hbm,
    wqkv,
    wout,
    wup,
    wdn,
    lay_out,
    inp_out,
    up_out,
    dn_out,
    pr_out,
    qk_out,
    gains_out,
    wup_x,
    wdn_x,
    seg,
    ln1v,
    ln2v,
    qgv,
    kgv,
    tokv,
    cotv,
    xp,
    cp,
    ni,
    q,
    k,
    v,
    invq,
    invk,
    nlg,
    dlt,
    mid,
    outa,
    gna,
    big,
    wus,
    wds,
    wq,
    wo,
    sbuf,
    r0,
    af,
    r1f,
    r2f,
    r3f,
    r4f,
    ap,
    r1p,
    r2p,
    r3p,
    r4p,
    gsend,
    grecv,
    up_sum,
    dn_sum,
    pr_sum,
    qk_sum,
    gains_sum,
    ssem,
    rsem,
    gssem,
    grsem,
    wssem,
    wrsem,
    lsem,
    fsem,
    osem,
):
    att = tokv
    gb = cotv
    lse = mid.at[:, pl.ds(0, 128)]
    do = wds
    g = lax.axis_index("dp")
    t = lax.axis_index("tensor")
    top, low = g // dp_low, g % dp_low
    mine = [(top // (1 << b)) % 2 for b in range(BITS)]

    def peer(b):
        return ((top + (1 - 2 * mine[b]) * (1 << b)) * dp_low + low, t)

    d0, d1 = peer(0)[0], peer(1)[0]
    core = (g, 1 - t)
    first = (jnp.where(t == 0, d0, d1), t)
    third = (jnp.where(t == 0, d1, d0), t)
    partners = (core, first, peer(2), third, peer(3))

    def place(b):
        rel = [mine[i] if (b >> i) & 1 == 0 else 1 - mine[i] for i in range(BITS)]
        one = rel[0] * 8 + rel[1] * 2
        two = rel[1] * 8 + rel[0] * 2
        return one + t * (two - one) + rel[2] * 4 + rel[3]

    places = [place(b) for b in range(16)]

    barrier = pltpu.get_barrier_semaphore()
    for partner in partners:
        pl.semaphore_signal(barrier, inc=1, device_id=partner, device_id_type=MESH)

    loads = [
        pltpu.make_async_copy(tok, tokv, lsem.at[0]),
        pltpu.make_async_copy(cot, cotv, lsem.at[1]),
        pltpu.make_async_copy(wqkv, wq.at[0], lsem.at[2]),
        pltpu.make_async_copy(wout, wo.at[pl.ds(0, 384)], lsem.at[3]),
        pltpu.make_async_copy(seg_hbm, seg, lsem.at[4]),
        pltpu.make_async_copy(ln1_hbm, ln1v, lsem.at[5]),
        pltpu.make_async_copy(ln2_hbm, ln2v, lsem.at[6]),
        pltpu.make_async_copy(qgain_hbm, qgv, lsem.at[7]),
        pltpu.make_async_copy(kgain_hbm, kgv, lsem.at[8]),
    ]
    for c in loads[4:] + loads[:4]:
        c.start()

    def weight_copy(i, src, dst):
        return pltpu.make_async_remote_copy(
            src_ref=src,
            dst_ref=dst,
            send_sem=wssem.at[i],
            recv_sem=wrsem.at[i],
            device_id=core,
            device_id_type=MESH,
        )

    weights = [
        weight_copy(0, wqkv, wq.at[1]),
        weight_copy(1, wout, wo.at[pl.ds(384, 384)]),
        weight_copy(2, wup, wup_x),
        weight_copy(3, wdn, wdn_x),
    ]

    def chunk_refs(c, is_ff):
        if is_ff:
            slot = lax.rem(c, 2)
            return sbuf.at[slot], r0.at[slot], af.at[c], [r.at[c] for r in (r1f, r2f, r3f, r4f)]
        n = min(c, 9) - FF_CHUNKS
        lanes = pl.ds(128 * (c - 9), 128) if c >= 9 else pl.ds(0, 384)
        slot = min(c, 9) % 2
        return (
            sbuf.at[slot, :, :, lanes],
            r0.at[slot, :, :, lanes],
            ap.at[n, :, :, lanes],
            [r.at[n, :, :, lanes] for r in (r1p, r2p, r3p, r4p)],
        )

    def rs_copy(stage, c, is_ff):
        src, dst, a, rs = chunk_refs(c, is_ff)
        if stage > 0:
            half = 16 >> stage
            src, dst = a.at[pl.ds(half, half)], rs[stage - 1]
        return pltpu.make_async_remote_copy(
            src_ref=src,
            dst_ref=dst,
            send_sem=ssem.at[c, stage],
            recv_sem=rsem.at[c, stage],
            device_id=partners[stage],
            device_id_type=MESH,
        )

    def finish(c, is_ff, total):
        if is_ff:
            cols = pl.ds(pl.multiple_of(c * FW, FW), FW)
            up_sum[:, cols] = total[:, :FW]
            dn_sum[:, cols] = total[:, FW:]
        elif c == FF_CHUNKS:
            pr_sum[...] = total
        elif c < 9:
            m = c - FF_CHUNKS - 1
            for part in range(3):
                qk_sum[part, :, 128 * m : 128 * m + 128] = total[:, 128 * part : 128 * part + 128]
        else:
            qk_sum[c - 9, :, 256:384] = total

    def advance(stage, c, is_ff):
        _src, arrived, a, rs = chunk_refs(c, is_ff)
        rs_copy(stage, c, is_ff).wait()
        if stage == 0:
            for pos in range(16):
                a[pos] = a[pos] + arrived[swap(pos)]
        elif stage < 4:
            half = 16 >> stage
            for pos in range(half):
                a[pos] = a[pos] + rs[stage - 1][pos]
        else:
            finish(c, is_ff, a[0].astype(f32) + rs[3][0].astype(f32))
        if stage < 4:
            rs_copy(stage + 1, c, is_ff).start()

    def event(e):
        for stage in range(4, -1, -1):
            for c in range(CHUNKS):
                if START[c] + LAG[c][stage] == e:
                    advance(stage, c, c < FF_CHUNKS)
        for c in range(CHUNKS):
            if START[c] == e:
                rs_copy(0, c, c < FF_CHUNKS).start()

    for c in loads[4:]:
        c.wait()
    s = jnp.int32(0)
    for image in range(IMAGES + 1):
        s = s + jnp.where(seg[t * LENGTH + PATCHES * image] == -1, image, 0)
    ln1 = ln1v[...].reshape(1, D)
    ln2 = ln2v[...].reshape(1, D)
    qg = qgv[...].reshape(1, HD)
    qg = jnp.concatenate([qg, qg], axis=1)
    kg = kgv[...].reshape(1, HD)
    kg = jnp.concatenate([kg, kg], axis=1)
    zero_rows = jnp.zeros((PADDED - LENGTH, 128), bf16)
    for pp in range(PAIRS):
        for ref in (q, k, v):
            ref[pp, LENGTH:, :] = zero_rows
    do[LENGTH:, :] = jnp.zeros((PADDED - LENGTH, D), bf16)
    nlg[LENGTH:, :] = zero_rows
    dlt[LENGTH:, :] = zero_rows

    def rows_of(i):
        return pl.ds(pl.multiple_of(i * 256, 256), 256)

    def pick(first, rows, ranges, source):
        wanted = source(iota((rows, 1), 0) + first)
        parts = [iota((rows, n), 1) + start == wanted for start, n in ranges]
        return jnp.concatenate([p.astype(f32).astype(bf16) for p in parts], axis=1)

    def picked(matrix, ranges, ref):
        return dot(matrix, jnp.concatenate([ref[start : start + n] for start, n in ranges], axis=0))

    def in_order(r):
        image_row = r + jnp.where(r >= PATCHES * s, PADDING, 0)
        return jnp.where(r < IMAGES * PATCHES, image_row, PATCHES * s + r - IMAGES * PATCHES)

    def out_of_order(r):
        behind = jnp.where(
            r < PATCHES * s + PADDING, r - PATCHES * s + IMAGES * PATCHES, r - PADDING
        )
        return jnp.where(r < PATCHES * s, r, behind)

    def permute(first, n, ranges):
        rows = slice(first, first + n)
        matrix = pick(first, n, ranges, in_order)
        x = picked(matrix, ranges, tokv)
        xp[rows] = x.astype(bf16)
        standard, _unused = norm_rows(x)
        ni[rows] = (standard * ln1).astype(bf16)
        cp[rows] = picked(matrix, ranges, cotv).astype(bf16)

    loads[0].wait()
    loads[1].wait()
    for tile in TILES_IN[:2]:
        permute(*tile)
    pl.semaphore_wait(barrier, len(partners))
    for c in weights:
        c.start()
    for tile in TILES_IN[2:]:
        permute(*tile)

    block = (iota((256, 256), 0) // HD == iota((256, 256), 1) // HD).astype(f32) * (1.0 / HD)
    block = block.astype(bf16)

    def head_norm(y, pair_of):
        high, rest = split(y)
        centred = y - (dot(high, block) + dot(rest, block))
        inverse = lax.rsqrt(dot((centred * centred).astype(bf16), block) + EPS)
        standard = centred * inverse
        for half in range(2):
            lanes = slice(128 * half, 128 * half + 128)
            dest, inv_dest, dest_gain, pp = pair_of(half)
            dest[pp, 0:LENGTH, :] = (standard[:, lanes] * dest_gain).astype(bf16)
            inv_dest[pp] = inverse[:, lanes].astype(bf16)

    def project(p):
        for tile in range(3):
            parts = []
            for half in range(2):
                idx = 2 * tile + half
                part, m = idx // 3, idx % 3
                parts.append(wq[p, part, :, 128 * m : 128 * m + 128])
            y = dot(ni[...], jnp.concatenate(parts, axis=1))

            def pair_of(half, tile=tile):
                idx = 2 * tile + half
                pp = p * 3 + idx % 3
                if idx < 3:
                    return q, invq, qg * 0.125, pp
                return k, invk, kg, pp

            head_norm(y, pair_of)
        y = dot(ni[...], wq[p, 2]).astype(bf16)
        for m in range(3):
            v[p * 3 + m, 0:LENGTH, :] = y[:, 128 * m : 128 * m + 128]

    loads[2].wait()
    project(0)
    weights[0].wait()
    project(1)

    def low_lanes(rows):
        return iota((rows, 128), 1) < HD

    def two_heads(x, rows):
        low = low_lanes(rows)
        zero = jnp.zeros_like(x)
        return jnp.concatenate([jnp.where(low, x, zero), jnp.where(low, zero, x)], axis=0)

    def attend(pp, _):
        cols = pl.ds(pl.multiple_of(pp * 128, 128), 128)
        for start, rows, begin, end in WINDOWS:
            window = slice(start, start + rows)
            krows = 256 if rows > 48 else 48
            kwin = slice(start, start + krows)
            scores = dot_nt(two_heads(q[pp, window, :], rows), k[pp, kwin, :])
            weight = jnp.exp(scores).astype(bf16)
            kr = iota((krows, 256), 0) + start
            vone = jnp.concatenate([v[pp, kwin, :], jnp.ones((krows, 128), bf16)], axis=1)
            vone = jnp.where((kr >= begin) & (kr < end), vone, jnp.zeros_like(vone))
            both = dot(weight, vone)
            total = both[:, 128:]
            heads = both[:, :128] / total
            merged = jnp.where(low_lanes(rows), heads[:rows], heads[rows:]).astype(bf16)
            keep = iota((rows, 128), 0) + start < begin
            att[window, cols] = jnp.where(keep, att[window, cols], merged)
            lane = iota((rows, 128), 1) // 2
            sums = lse[window, :]
            sums = jnp.where((lane == 2 * pp) & ~keep, total[:rows], sums)
            sums = jnp.where((lane == 2 * pp + 1) & ~keep, total[rows:], sums)
            lse[window, :] = sums
        return 0

    lse[...] = jnp.ones_like(lse)
    lax.fori_loop(0, PAIRS, attend, 0)
    even = iota((LENGTH, 128), 1) % 2 == 0
    high, rest = split(-jnp.log(lse[...]))
    nlg[0:LENGTH, :] = jnp.where(even, high, rest)

    loads[3].wait()
    weights[1].wait()
    nm = big.at[:, pl.ds(1024, D)]
    act = big.at[:, pl.ds(0, 2 * FW)]
    gh = big.at[:, pl.ds(512, 2 * FW)]

    def middle(i, _):
        rows = rows_of(i)
        m = xp[rows].astype(f32) + dot(att[rows], wo[...])
        mid[rows] = m
        standard, _unused = norm_rows(m)
        nm[rows] = (standard * ln2).astype(bf16)
        return 0

    lax.fori_loop(0, 4, middle, 0)

    def down_rows(i):
        return wds.at[pl.ds(pl.multiple_of(i * FW, FW), FW)]

    def ff_loads(j, slot):
        cols = pl.ds(pl.multiple_of(j * FW, FW), FW)
        return [
            pltpu.make_async_copy(wup.at[:, cols], wus.at[slot, :, pl.ds(0, FW)], fsem.at[slot, 0]),
            pltpu.make_async_copy(
                wup_x.at[:, cols], wus.at[slot, :, pl.ds(FW, FW)], fsem.at[slot, 1]
            ),
            pltpu.make_async_copy(wdn.at[cols], down_rows(2 * slot), fsem.at[slot, 2]),
            pltpu.make_async_copy(wdn_x.at[cols], down_rows(2 * slot + 1), fsem.at[slot, 3]),
        ]

    weights[2].wait()
    weights[3].wait()
    for c in ff_loads(0, 0):
        c.start()
    outa[...] = jnp.zeros_like(outa)
    gna[...] = jnp.zeros_like(gna)

    def feed_event(j):
        for stage in range(4, -1, -1):
            lag = FF_LAG[stage]
            if lag < FF_CHUNKS:

                @pl.when(j >= lag)
                def _(stage=stage, lag=lag):
                    advance(stage, j - lag, True)

    def feed(j, _):
        slot = lax.rem(j, 2)
        for c in ff_loads(j, slot):
            c.wait()

        @pl.when(j < FF_CHUNKS - 1)
        def _():
            for c in ff_loads(j + 1, 1 - slot):
                c.start()

        wu = wus[slot]
        wd = wds[pl.ds(pl.multiple_of(slot * 2 * FW, 2 * FW), 2 * FW), :]
        for r in range(0, LENGTH, 256):
            rows = slice(r, r + 256)
            a, slope = gelu_and_slope(dot(nm[rows], wu))
            act[rows] = a.astype(bf16)
            gh[rows] = (dot_nt(cp[rows], wd) * slope).astype(bf16)
        outa[...] += dot(act[...], wd)
        gna[...] += dot_nt(gh[...], wu)
        up = dot_tn(nm[...], gh[...]).astype(bf16)
        dn = dot_tn(cp[...], act[...]).astype(bf16)
        for b in range(16):
            part = slice(48 * b, 48 * b + 48)
            af[j, places[b], :, 0:FW] = up[part, :FW]
            af[j, places[b], :, FW : 2 * FW] = dn[part, :FW]
            sbuf[slot, places[b], :, 0:FW] = up[part, FW:]
            sbuf[slot, places[b], :, FW : 2 * FW] = dn[part, FW:]
        feed_event(j)
        rs_copy(0, j, True).start()
        return 0

    lax.fori_loop(0, FF_CHUNKS, feed, 0)

    lob = cp

    def norm2_back(i, total):
        rows = rows_of(i)
        m = mid[rows]
        standard, inverse = norm_rows(m)
        grad = gna[rows]
        grad_mid = cp[rows].astype(f32) + norm_rows_back(grad, standard, inverse, ln2)
        gna[rows] = grad_mid
        gb[rows] = grad_mid.astype(bf16)
        lob[rows] = (m + outa[rows]).astype(bf16)
        return total + jnp.sum(grad * standard, axis=0, keepdims=True)

    ln2_terms = lax.fori_loop(0, 4, norm2_back, jnp.zeros((1, D), f32))

    def put(c, slot, own, other):
        for b in range(16):
            part = slice(48 * b, 48 * b + 48)
            ap[c - FF_CHUNKS, places[b]] = own[part]
            sbuf[slot, places[b], :, 0:384] = other[part]

    pg = dot_tn(gb[...], att[...]).astype(bf16)
    put(FF_CHUNKS, 0, pg[:, :384], pg[:, 384:])
    event(6)

    ga = dot_nt(gb[...], wo[...])
    gab = ga.astype(bf16)
    do[0:LENGTH, :] = gab
    high, rest = split(gab.astype(f32) * att[...].astype(f32))
    gather = (iota((D, 128), 0) // HD == iota((D, 128), 1) // 2).astype(f32).astype(bf16)
    delta = dot(high, gather) + dot(rest, gather)
    high, rest = split(delta)
    dlt[0:LENGTH, :] = jnp.where(even, high, rest)

    block2 = (iota((256, 128), 0) % 128 // HD == iota((256, 128), 1) // HD).astype(f32) * (1.0 / HD)
    block2 = block2.astype(bf16)

    def head_mean(x):
        return dot(jnp.concatenate(split(x), axis=1), block2)

    def head_norm_back(grad, standard, inverse, gain):
        c = grad * gain
        return inverse * (c - head_mean(c) - standard * head_mean(c * standard))

    dq, dk, dv = (outa.at[:, pl.ds(128 * i, 128)] for i in range(3))

    def attend_back(pp, col):
        for start, rows, begin, end in WINDOWS:
            window = slice(start, start + rows)
            qrows = 256 if rows > 48 else 48
            qwin = slice(start, start + qrows)
            lane = iota((2 * rows, 128), 1)
            head = 2 * pp + jnp.where(iota((2 * rows, 128), 0) < rows, 0, 1)
            hot = (lane // 2 == head).astype(f32).astype(bf16)
            kb = k[pp, window, :]
            qb = q[pp, qwin, :]
            st = dot_nt(
                jnp.concatenate([two_heads(kb, rows), hot], axis=1),
                jnp.concatenate([qb, nlg[qwin, :]], axis=1),
            )
            pt = jnp.exp(st)
            qr = iota((qrows, 128), 0) + start
            valid = (qr >= begin) & (qr < end)
            dob = do[qwin, pl.ds(pl.multiple_of(pp * 128, 128), 128)]
            zero = jnp.zeros_like(dob)
            dob = jnp.where(valid, dob, zero)
            dpt = dot_nt(
                jnp.concatenate([two_heads(v[pp, window, :], rows), -hot], axis=1),
                jnp.concatenate([dob, jnp.where(valid, dlt[qwin, :], zero)], axis=1),
            )
            dst = (pt * dpt).astype(bf16)
            dv2 = dot(pt.astype(bf16), dob)
            dk2 = dot(dst, qb)
            kr = iota((rows, 128), 0) + start
            kz = jnp.where((kr >= begin) & (kr < end), kb, jnp.zeros_like(kb))
            dq2 = dot_tn(dst, two_heads(kz, rows))[:rows]
            keep = kr < begin
            low = low_lanes(rows)
            dv[window, :] = jnp.where(keep, dv[window, :], jnp.where(low, dv2[:rows], dv2[rows:]))
            dk[window, :] = jnp.where(keep, dk[window, :], jnp.where(low, dk2[:rows], dk2[rows:]))
            dq[window, :] = jnp.where(keep, dq[window, :], dq2)
        standard = q[pp, 0:LENGTH, :].astype(f32) * (8.0 / qg)
        grad = dq[...] * 0.125
        q_terms = jnp.sum(grad * standard, axis=0, keepdims=True)
        big[:, col(0)] = head_norm_back(grad, standard, invq[pp].astype(f32), qg).astype(bf16)
        standard = k[pp, 0:LENGTH, :].astype(f32) * (1.0 / kg)
        grad = dk[...]
        k_terms = jnp.sum(grad * standard, axis=0, keepdims=True)
        big[:, col(1)] = head_norm_back(grad, standard, invk[pp].astype(f32), kg).astype(bf16)
        big[:, col(2)] = dv[...].astype(bf16)
        return q_terms, k_terms

    def weight_of(m):
        return jnp.concatenate(
            [wq[p, part, :, 128 * m : 128 * m + 128] for p in range(2) for part in range(3)], axis=1
        )

    def gain_copy(i):
        return pltpu.make_async_remote_copy(
            src_ref=gsend.at[i],
            dst_ref=grecv.at[i],
            send_sem=gssem.at[i],
            recv_sem=grsem.at[i],
            device_id=partners[i],
            device_id_type=MESH,
        )

    def gain_step(i):
        gain_copy(i).wait()
        total = gsend[i] + grecv[i]
        if i < 4:
            gsend[i + 1] = total
            gain_copy(i + 1).start()
        else:
            gains_sum[...] = total

    ln1_sum = jnp.zeros((D, 128), f32)
    q_terms = jnp.zeros((1, 128), f32)
    k_terms = jnp.zeros((1, 128), f32)
    for m in range(3):

        def pair(i, carry, m=m):
            def col(part):
                return pl.ds(pl.multiple_of(768 * m + 384 * i + 128 * part, 128), 128)

            a, b = attend_back(3 * i + m, col)

            @pl.when(i == 0)
            def _():
                event(7 + 2 * m)

            return carry[0] + a, carry[1] + b

        q_terms, k_terms = lax.fori_loop(0, 2, pair, (q_terms, k_terms))
        both = dot_tn(ni[...], big[:, 768 * m : 768 * m + 768])
        wide = both * weight_of(m).astype(f32)
        for tile in range(6):
            ln1_sum = ln1_sum + wide[:, 128 * tile : 128 * tile + 128]
        both = both.astype(bf16)
        c = FF_CHUNKS + 1 + m
        put(c, c % 2, both[:, :384], both[:, 384:])
        if m == 2:
            high, rest = split(ln1_sum)
            ones = jnp.ones((16, 128), bf16)
            ln1_terms = (dot_nt(ones, high) + dot_nt(ones, rest))[0:1] / ln1
            gsend[0] = jnp.concatenate(
                [ln1_terms[:, 128 * i : 128 * i + 128] for i in range(6)]
                + [ln2_terms[:, 128 * i : 128 * i + 128] for i in range(6)]
                + [q_terms, k_terms, jnp.zeros((2, 128), f32)],
                axis=0,
            )
            gain_copy(0).start()
        event(8 + 2 * m)

    gsum = outa
    gsum[...] = dot_nt(big[:, 0:768], weight_of(0))
    gsum[...] += dot_nt(big[:, 768:1536], weight_of(1))
    gain_step(0)
    event(13)
    gsum[...] += dot_nt(big[:, 1536:2304], weight_of(2))
    igb = ni

    def norm1_back(i, _):
        rows = rows_of(i)
        standard, inverse = norm_rows(xp[rows].astype(f32))
        igb[rows] = (gna[rows] + norm_rows_back(gsum[rows], standard, inverse, ln1)).astype(bf16)
        return 0

    copies = []

    def unpermute(src, dst, out, sem):
        for i, (first, n, ranges) in enumerate(TILES_OUT):
            rows = slice(first, first + n)
            dst[rows] = picked(pick(first, n, ranges, out_of_order), ranges, src).astype(bf16)
            copies.append(
                pltpu.make_async_copy(dst.at[pl.ds(first, n)], out.at[pl.ds(first, n)], sem.at[i])
            )
            copies[-1].start()

    def send_out(i, src, dst):
        copies.append(pltpu.make_async_copy(src, dst, osem.at[2, i]))
        copies[-1].start()

    lax.fori_loop(0, 2, norm1_back, 0)
    unpermute(lob, tokv, lay_out, osem.at[0])
    gain_step(1)
    event(14)
    lax.fori_loop(2, 4, norm1_back, 0)
    unpermute(igb, cotv, inp_out, osem.at[1])
    gain_step(2)
    event(15)
    send_out(0, up_sum, up_out)
    send_out(1, dn_sum, dn_out)
    send_out(2, pr_sum, pr_out)
    gain_step(3)
    event(16)
    gain_step(4)
    send_out(3, gains_sum, gains_out)
    event(17)
    send_out(4, qk_sum, qk_out)
    for c in copies:
        c.wait()


def hand_on(*refs):
    n = 6
    ins, gains_in = refs[:n], refs[n]
    outs, gain_outs = refs[n + 1 : 2 * n + 1], refs[2 * n + 1 : 2 * n + 5]
    held, gains, lines, sems = refs[2 * n + 5 : 3 * n + 5], refs[-6], refs[-5:-1], refs[-1]
    gains_come = pltpu.make_async_copy(gains_in, gains, sems.at[4 * n])
    gains_come.start()
    copies = []
    for i, (src, dst) in enumerate(zip(ins, outs)):
        parts = 4 if src.shape[0] == LENGTH else 1
        size = src.shape[0] // parts
        for part in range(parts):
            rows = pl.ds(part * size, size)
            sem = sems.at[4 * i + part]
            copies.append(
                (
                    pltpu.make_async_copy(src.at[rows], held[i].at[rows], sem),
                    pltpu.make_async_copy(held[i].at[rows], dst.at[rows], sem),
                )
            )
    for come, _go in copies:
        come.start()
    gains_come.wait()
    ln1, ln2, qg, kg = lines
    for i in range(6):
        ln1[pl.ds(128 * i, 128)] = gains[i, :]
        ln2[pl.ds(128 * i, 128)] = gains[6 + i, :]
    qg[...] = gains[12, 0:HD] + gains[12, HD : 2 * HD]
    kg[...] = gains[13, 0:HD] + gains[13, HD : 2 * HD]
    gains_go = [
        pltpu.make_async_copy(src, dst, sems.at[4 * n + 1 + i])
        for i, (src, dst) in enumerate(zip(lines, gain_outs))
    ]
    for go in gains_go:
        go.start()
    for come, go in copies:
        come.wait()
        go.start()
    for go in gains_go:
        go.wait()
    for _come, go in copies:
        go.wait()


def local(
    tokens, segment, ln1_gain, w_qkv, q_gain, k_gain, w_out, ln2_gain, w_up, w_down, cotangent
):
    groups = lax.axis_size("dp")
    dp_low = groups // (1 << BITS)
    rows = D >> BITS
    hbm = pl.BlockSpec(memory_space=pl.ANY)
    shape = jax.ShapeDtypeStruct
    half_ff = w_up.shape[1]
    ff, wide, n_proj = FF_CHUNKS, 2 * FW, CHUNKS - FF_CHUNKS

    def mem(*dims, dtype=bf16):
        return pltpu.VMEM(dims, dtype)

    outs = pl.pallas_call(
        functools.partial(kernel, dp_low),
        out_shape=(
            shape((LENGTH, D), bf16),
            shape((LENGTH, D), bf16),
            shape((rows, half_ff), f32),
            shape((rows, half_ff), f32),
            shape((rows, 384), f32),
            shape((3, rows, 384), f32),
            shape((16, 128), f32),
            shape((D, half_ff), bf16),
            shape((half_ff, D), bf16),
        ),
        in_specs=[hbm] * 11,
        out_specs=(hbm,) * 9,
        scratch_shapes=[
            pltpu.SMEM(segment.shape, jnp.int32),
            mem(D, dtype=f32),
            mem(D, dtype=f32),
            mem(HD, dtype=f32),
            mem(HD, dtype=f32),
            mem(LENGTH, D),
            mem(LENGTH, D),
            mem(LENGTH, D),
            mem(LENGTH, D),
            mem(LENGTH, D),
            mem(PAIRS, PADDED, 128),
            mem(PAIRS, PADDED, 128),
            mem(PAIRS, PADDED, 128),
            mem(PAIRS, LENGTH, 128),
            mem(PAIRS, LENGTH, 128),
            mem(PADDED, 128),
            mem(PADDED, 128),
            mem(LENGTH, D, dtype=f32),
            mem(LENGTH, D, dtype=f32),
            mem(LENGTH, D, dtype=f32),
            mem(LENGTH, 3 * D),
            mem(2, D, wide),
            mem(PADDED, D),
            mem(2, 3, D, 384),
            mem(D, D),
            mem(2, 16, rows, wide),
            mem(2, 16, rows, wide),
            mem(ff, 16, rows, wide),
            mem(ff, 8, rows, wide),
            mem(ff, 4, rows, wide),
            mem(ff, 2, rows, wide),
            mem(ff, 1, rows, wide),
            mem(n_proj, 16, rows, 384),
            mem(n_proj, 8, rows, 384),
            mem(n_proj, 4, rows, 384),
            mem(n_proj, 2, rows, 384),
            mem(n_proj, 1, rows, 384),
            mem(5, 16, 128, dtype=f32),
            mem(5, 16, 128, dtype=f32),
            mem(rows, half_ff, dtype=f32),
            mem(rows, half_ff, dtype=f32),
            mem(rows, 384, dtype=f32),
            mem(3, rows, 384, dtype=f32),
            mem(16, 128, dtype=f32),
            pltpu.SemaphoreType.DMA((CHUNKS, 5)),
            pltpu.SemaphoreType.DMA((CHUNKS, 5)),
            pltpu.SemaphoreType.DMA((5,)),
            pltpu.SemaphoreType.DMA((5,)),
            pltpu.SemaphoreType.DMA((4,)),
            pltpu.SemaphoreType.DMA((4,)),
            pltpu.SemaphoreType.DMA((9,)),
            pltpu.SemaphoreType.DMA((2, 4)),
            pltpu.SemaphoreType.DMA((3, 5)),
        ],
        compiler_params=pltpu.CompilerParams(
            collective_id=0, has_side_effects=True, vmem_limit_bytes=63 * 2**20
        ),
        name="layer",
    )(
        segment,
        tokens,
        cotangent,
        ln1_gain,
        ln2_gain,
        q_gain,
        k_gain,
        jnp.transpose(w_qkv, (1, 0, 2)),
        w_out,
        w_up,
        w_down,
    )
    results, gains = list(outs[:6]), outs[6]
    if dp_low > 1:
        peers = [[hi * dp_low + lo for lo in range(dp_low)] for hi in range(1 << BITS)]

        def rest(x, axis):
            return lax.psum_scatter(
                x, "dp", scatter_dimension=axis, axis_index_groups=peers, tiled=True
            )

        results[2:] = [rest(x, x.ndim - 2) for x in results[2:]]
        gains = lax.psum(gains, "dp", axis_index_groups=peers)
    (
        layer_out,
        input_grad,
        up_grad,
        down_grad,
        proj_grad,
        qkv_grad,
        ln1_grad,
        ln2_grad,
        q_grad,
        k_grad,
    ) = pl.pallas_call(
        hand_on,
        out_shape=[shape(x.shape, x.dtype) for x in results]
        + [shape((D,), f32)] * 2
        + [shape((HD,), f32)] * 2,
        in_specs=[pl.BlockSpec(memory_space=pltpu.HBM)] * 7,
        out_specs=[pl.BlockSpec(memory_space=pltpu.HBM)] * 10,
        scratch_shapes=[pltpu.VMEM(x.shape, x.dtype) for x in results + [gains]]
        + [mem(D, dtype=f32)] * 2
        + [mem(HD, dtype=f32)] * 2
        + [pltpu.SemaphoreType.DMA((29,))],
        name="hand_on",
    )(*results, gains)
    return (
        layer_out,
        input_grad,
        ln1_grad,
        jnp.transpose(qkv_grad, (1, 0, 2)),
        q_grad,
        k_grad,
        proj_grad.T,
        ln2_grad,
        up_grad,
        down_grad.T,
    )


def solution(mesh):
    return jax.shard_map(
        local,
        mesh=mesh,
        in_specs=(
            P(("dp", "tensor"), None),
            P("dp"),
            P(),
            P(None, None, "tensor"),
            P(),
            P(),
            P("tensor", None),
            P(),
            P(None, "tensor"),
            P("tensor", None),
            P(("dp", "tensor"), None),
        ),
        out_specs=(
            P(("dp", "tensor"), None),
            P(("dp", "tensor"), None),
            P(),
            P("dp", None, "tensor"),
            P(),
            P(),
            P("tensor", "dp"),
            P(),
            P("dp", "tensor"),
            P("tensor", "dp"),
        ),
        check_vma=False,
    )
```

```python
import functools

import jax
import jax.numpy as jnp
from jax import lax
from jax.experimental import pallas as pl
from jax.experimental.pallas import tpu as pltpu
from jax.sharding import PartitionSpec as P

D = 768
HD = 64
LENGTH = 1024
PATCHES = 196
IMAGES = 5
PADDING = LENGTH - IMAGES * PATCHES
PADDED = 1040
PAIRS = 6
EPS = 1e-06
MESH = pl.DeviceIdType.MESH
f32, bf16 = jnp.float32, jnp.bfloat16

WINDOWS = [
    (PATCHES * i // 16 * 16, 208, PATCHES * i, PATCHES * (i + 1)) for i in range(IMAGES)
] + [(976, 48, 980, 1024)]

FF_CHUNKS = 6
FW = 256
BITS = 4

CHUNKS = 12
START = [0, 1, 2, 3, 4, 5, 6, 8, 10, 12, 12, 12]
FF_LAG = (1, 3, 6, 8, 11)
LAG = [FF_LAG] * FF_CHUNKS + [(1, 3, 5, 7, 10), (1, 3, 5, 7, 8), (1, 3, 4, 5, 7)] + [(1, 2, 3, 4, 5)] * 3

TILES_IN = [
    (0, 256, [(0, 384)]),
    (256, 256, [(256, 384)]),
    (512, 256, [(512, 384)]),
    (768, 128, [(768, 256)]),
    (896, 128, [(0, 1024)]),
]
TILES_OUT = [
    (0, 256, [(0, 256), (896, 128)]),
    (256, 256, [(128, 384), (896, 128)]),
    (512, 256, [(384, 384), (896, 128)]),
    (768, 256, [(640, 384)]),
]


def dot(left, right):
    return jnp.dot(left, right, preferred_element_type=f32)


def dot_nt(left, right):
    return lax.dot_general(left, right, (((1,), (1,)), ((), ())), preferred_element_type=f32)


def dot_tn(left, right):
    return lax.dot_general(left, right, (((0,), (0,)), ((), ())), preferred_element_type=f32)


def gelu_and_slope(h):
    e = jnp.exp(h * h * -0.5)
    t = 1.0 / (1.0 + jnp.abs(h) * (0.3275911 * 0.7071067811865476))
    poly = t * (
        0.5 * 0.254829592
        + t
        * (
            0.5 * -0.284496736
            + t * (0.5 * 1.421413741 + t * (0.5 * -1.453152027 + t * (0.5 * 1.061405429)))
        )
    )
    tail = poly * e
    phi = jnp.where(h >= 0, 1.0 - tail, tail)
    return h * phi, phi + h * e * 0.3989422804014327


def split(x):
    high = x.astype(bf16)
    return high, (x - high.astype(f32)).astype(bf16)


def iota(shape, axis):
    return lax.broadcasted_iota(jnp.int32, shape, axis)


def norm_rows(x):
    centred = x - jnp.mean(x, axis=-1, keepdims=True)
    inverse = lax.rsqrt(jnp.mean(centred * centred, axis=-1, keepdims=True) + EPS)
    return centred * inverse, inverse


def norm_rows_back(grad, standard, inverse, gain):
    c = grad * gain
    return inverse * (
        c
        - jnp.mean(c, axis=-1, keepdims=True)
        - standard * jnp.mean(c * standard, axis=-1, keepdims=True)
    )


def swap(pos):
    return (pos & 4) | (pos & 1) | ((pos & 8) >> 2) | ((pos & 2) << 2)


def kernel(
    dp_low,
    seg_hbm,
    tok,
    cot,
    ln1_hbm,
    ln2_hbm,
    qgain_hbm,
    kgain_hbm,
    wqkv,
    wout,
    wup,
    wdn,
    lay_out,
    inp_out,
    up_out,
    dn_out,
    pr_out,
    qk_out,
    gains_out,
    wup_x,
    wdn_x,
    seg,
    ln1v,
    ln2v,
    qgv,
    kgv,
    tokv,
    cotv,
    xp,
    cp,
    ni,
    q,
    k,
    v,
    invq,
    invk,
    nlg,
    dlt,
    mid,
    outa,
    gna,
    big,
    wus,
    wds,
    wq,
    wo,
    sbuf,
    r0,
    af,
    r1f,
    r2f,
    r3f,
    r4f,
    ap,
    r1p,
    r2p,
    r3p,
    r4p,
    gsend,
    grecv,
    gains_sum,
    ssem,
    rsem,
    gssem,
    grsem,
    wssem,
    wrsem,
    lsem,
    fsem,
    osem,
):
    att = tokv
    gb = cotv
    lse = mid.at[:, pl.ds(0, 128)]
    do = wds
    g = lax.axis_index("dp")
    t = lax.axis_index("tensor")
    top, low = g // dp_low, g % dp_low
    mine = [(top // (1 << b)) % 2 for b in range(BITS)]

    def peer(b):
        return ((top + (1 - 2 * mine[b]) * (1 << b)) * dp_low + low, t)

    d0, d1 = peer(0)[0], peer(1)[0]
    core = (g, 1 - t)
    first = (jnp.where(t == 0, d0, d1), t)
    third = (jnp.where(t == 0, d1, d0), t)
    partners = (core, first, peer(2), third, peer(3))

    def place(b):
        rel = [mine[i] if (b >> i) & 1 == 0 else 1 - mine[i] for i in range(BITS)]
        one = rel[0] * 8 + rel[1] * 2
        two = rel[1] * 8 + rel[0] * 2
        return one + t * (two - one) + rel[2] * 4 + rel[3]

    places = [place(b) for b in range(16)]

    barrier = pltpu.get_barrier_semaphore()
    for partner in partners:
        pl.semaphore_signal(barrier, inc=1, device_id=partner, device_id_type=MESH)

    loads = [
        pltpu.make_async_copy(tok, tokv, lsem.at[0]),
        pltpu.make_async_copy(cot, cotv, lsem.at[1]),
        pltpu.make_async_copy(wqkv, wq.at[0], lsem.at[2]),
        pltpu.make_async_copy(wout, wo.at[pl.ds(0, 384)], lsem.at[3]),
        pltpu.make_async_copy(seg_hbm, seg, lsem.at[4]),
        pltpu.make_async_copy(ln1_hbm, ln1v, lsem.at[5]),
        pltpu.make_async_copy(ln2_hbm, ln2v, lsem.at[6]),
        pltpu.make_async_copy(qgain_hbm, qgv, lsem.at[7]),
        pltpu.make_async_copy(kgain_hbm, kgv, lsem.at[8]),
    ]
    for c in loads[4:] + loads[:4]:
        c.start()

    def weight_copy(i, src, dst):
        return pltpu.make_async_remote_copy(
            src_ref=src,
            dst_ref=dst,
            send_sem=wssem.at[i],
            recv_sem=wrsem.at[i],
            device_id=core,
            device_id_type=MESH,
        )

    weights = [
        weight_copy(0, wqkv, wq.at[1]),
        weight_copy(1, wout, wo.at[pl.ds(384, 384)]),
        weight_copy(2, wup, wup_x),
        weight_copy(3, wdn, wdn_x),
    ]

    def chunk_refs(c, is_ff):
        if is_ff:
            slot = lax.rem(c, 2)
            return sbuf.at[slot], r0.at[slot], af.at[c], [r.at[c] for r in (r1f, r2f, r3f, r4f)]
        n = min(c, 9) - FF_CHUNKS
        lanes = pl.ds(128 * (c - 9), 128) if c >= 9 else pl.ds(0, 384)
        slot = min(c, 9) % 2
        return (
            sbuf.at[slot, :, :, lanes],
            r0.at[slot, :, :, lanes],
            ap.at[n, :, :, lanes],
            [r.at[n, :, :, lanes] for r in (r1p, r2p, r3p, r4p)],
        )

    def rs_copy(stage, c, is_ff):
        src, dst, a, rs = chunk_refs(c, is_ff)
        if stage > 0:
            half = 16 >> stage
            src, dst = a.at[pl.ds(half, half)], rs[stage - 1]
        return pltpu.make_async_remote_copy(
            src_ref=src,
            dst_ref=dst,
            send_sem=ssem.at[c, stage],
            recv_sem=rsem.at[c, stage],
            device_id=partners[stage],
            device_id_type=MESH,
        )

    copies = []

    def send_out(copy):
        copies.append(copy)
        copy().start()

    def finish(c, total):
        mid[48 * c : 48 * c + 48, 0 : total.shape[1]] = total

        def part(first, width, out, place, i):
            def copy():
                src = mid.at[pl.ds(48 * c, 48), pl.ds(first, width)]
                return pltpu.make_async_copy(src, out.at[place], osem.at[2 + c, i])

            send_out(copy)

        every = slice(None)
        if c < FF_CHUNKS:
            part(0, FW, up_out, (every, pl.ds(c * FW, FW)), 0)
            part(FW, FW, dn_out, (every, pl.ds(c * FW, FW)), 1)
        elif c == FF_CHUNKS:
            part(0, 384, pr_out, (every, every), 0)
        elif c < 9:
            for i in range(3):
                m = c - FF_CHUNKS - 1
                part(128 * i, 128, qk_out, (i, every, pl.ds(128 * m, 128)), i)
        else:
            part(0, 128, qk_out, (c - 9, every, pl.ds(256, 128)), 0)

    def advance(stage, c, is_ff):
        _src, arrived, a, rs = chunk_refs(c, is_ff)
        rs_copy(stage, c, is_ff).wait()
        if stage == 0:
            for pos in range(16):
                a[pos] = a[pos] + arrived[swap(pos)]
        elif stage < 4:
            half = 16 >> stage
            for pos in range(half):
                a[pos] = a[pos] + rs[stage - 1][pos]
        else:
            finish(c, a[0].astype(f32) + rs[3][0].astype(f32))
        if stage < 4:
            rs_copy(stage + 1, c, is_ff).start()

    def event(e):
        for stage in range(4, -1, -1):
            for c in range(CHUNKS):
                if START[c] + LAG[c][stage] == e:
                    advance(stage, c, c < FF_CHUNKS)
        for c in range(CHUNKS):
            if START[c] == e:
                rs_copy(0, c, c < FF_CHUNKS).start()

    for c in loads[4:]:
        c.wait()
    s = jnp.int32(0)
    for image in range(IMAGES + 1):
        s = s + jnp.where(seg[t * LENGTH + PATCHES * image] == -1, image, 0)
    ln1 = ln1v[...].reshape(1, D)
    ln2 = ln2v[...].reshape(1, D)
    qg = qgv[...].reshape(1, HD)
    qg = jnp.concatenate([qg, qg], axis=1)
    kg = kgv[...].reshape(1, HD)
    kg = jnp.concatenate([kg, kg], axis=1)
    zero_rows = jnp.zeros((PADDED - LENGTH, 128), bf16)
    for pp in range(PAIRS):
        for ref in (q, k, v):
            ref[pp, LENGTH:, :] = zero_rows
    do[LENGTH:, :] = jnp.zeros((PADDED - LENGTH, D), bf16)
    nlg[LENGTH:, :] = zero_rows
    dlt[LENGTH:, :] = zero_rows

    def rows_of(i):
        return pl.ds(pl.multiple_of(i * 256, 256), 256)

    def pick(first, rows, ranges, source):
        wanted = source(iota((rows, 1), 0) + first)
        parts = [iota((rows, n), 1) + start == wanted for start, n in ranges]
        return jnp.concatenate([p.astype(f32).astype(bf16) for p in parts], axis=1)

    def picked(matrix, ranges, ref):
        return dot(matrix, jnp.concatenate([ref[start : start + n] for start, n in ranges], axis=0))

    def in_order(r):
        image_row = r + jnp.where(r >= PATCHES * s, PADDING, 0)
        return jnp.where(r < IMAGES * PATCHES, image_row, PATCHES * s + r - IMAGES * PATCHES)

    def out_of_order(r):
        behind = jnp.where(
            r < PATCHES * s + PADDING, r - PATCHES * s + IMAGES * PATCHES, r - PADDING
        )
        return jnp.where(r < PATCHES * s, r, behind)

    def permute(first, n, ranges):
        rows = slice(first, first + n)
        matrix = pick(first, n, ranges, in_order)
        x = picked(matrix, ranges, tokv)
        xp[rows] = x.astype(bf16)
        standard, _unused = norm_rows(x)
        ni[rows] = (standard * ln1).astype(bf16)
        cp[rows] = picked(matrix, ranges, cotv).astype(bf16)

    loads[0].wait()
    loads[1].wait()
    for tile in TILES_IN[:2]:
        permute(*tile)
    pl.semaphore_wait(barrier, len(partners))
    for c in weights:
        c.start()
    for tile in TILES_IN[2:]:
        permute(*tile)

    def lane_means(x):
        out = []
        for first in range(0, x.shape[1], 128):
            part = x[:, first : first + 128]
            low = iota(part.shape, 1) < HD
            low_sum = jnp.sum(jnp.where(low, part, 0.0), axis=1, keepdims=True)
            high_sum = jnp.sum(part, axis=1, keepdims=True) - low_sum
            out.append(jnp.where(low, low_sum, high_sum) * (1.0 / HD))
        return jnp.concatenate(out, axis=1)

    block = (iota((256, 256), 0) // HD == iota((256, 256), 1) // HD).astype(f32) * (1.0 / HD)
    block = block.astype(bf16)

    def head_norm(y, pair_of, by_lanes):
        if by_lanes:
            centred = y - lane_means(y)
            spread = lane_means(centred * centred)
        else:
            high, rest = split(y)
            centred = y - (dot(high, block) + dot(rest, block))
            spread = dot((centred * centred).astype(bf16), block)
        inverse = lax.rsqrt(spread + EPS)
        standard = centred * inverse
        for half in range(2):
            lanes = slice(128 * half, 128 * half + 128)
            dest, inv_dest, dest_gain, pp = pair_of(half)
            dest[pp, 0:LENGTH, :] = (standard[:, lanes] * dest_gain).astype(bf16)
            inv_dest[pp] = inverse[:, lanes].astype(bf16)

    def project(p):
        for tile in range(3):
            parts = []
            for half in range(2):
                idx = 2 * tile + half
                part, m = idx // 3, idx % 3
                parts.append(wq[p, part, :, 128 * m : 128 * m + 128])
            y = dot(ni[...], jnp.concatenate(parts, axis=1))

            def pair_of(half, tile=tile):
                idx = 2 * tile + half
                pp = p * 3 + idx % 3
                if idx < 3:
                    return q, invq, qg * 0.125, pp
                return k, invk, kg, pp

            head_norm(y, pair_of, tile != 1)
        y = dot(ni[...], wq[p, 2]).astype(bf16)
        for m in range(3):
            v[p * 3 + m, 0:LENGTH, :] = y[:, 128 * m : 128 * m + 128]

    loads[2].wait()
    project(0)
    weights[0].wait()
    project(1)

    def low_lanes(rows):
        return iota((rows, 128), 1) < HD

    def two_heads(x, rows):
        low = low_lanes(rows)
        zero = jnp.zeros_like(x)
        return jnp.concatenate([jnp.where(low, x, zero), jnp.where(low, zero, x)], axis=0)

    def place_rows(ref, cols, new, start, begin):
        rows = new.shape[0]
        if begin > start:
            top = slice(start, start + 16)
            keep = iota((16, 128), 0) + start < begin
            ref[top, cols] = jnp.where(keep, ref[top, cols], new[:16])
            ref[start + 16 : start + rows, cols] = new[16:]
        else:
            ref[start : start + rows, cols] = new

    def attend(pp, _):
        cols = pl.ds(pl.multiple_of(pp * 128, 128), 128)
        for start, rows, begin, end in WINDOWS:
            window = slice(start, start + rows)
            krows = 256 if rows > 48 else 48
            kwin = slice(start, start + krows)
            scores = dot_nt(two_heads(q[pp, window, :], rows), k[pp, kwin, :])
            weight = jnp.exp(scores).astype(bf16)
            kr = iota((krows, 256), 0) + start
            vone = jnp.concatenate([v[pp, kwin, :], jnp.ones((krows, 128), bf16)], axis=1)
            vone = jnp.where((kr >= begin) & (kr < end), vone, jnp.zeros_like(vone))
            both = dot(weight, vone)
            total = both[:, 128:]
            heads = both[:, :128] / total
            merged = jnp.where(low_lanes(rows), heads[:rows], heads[rows:]).astype(bf16)
            place_rows(att, cols, merged, start, begin)
            lane = iota((rows, 128), 1) // 2
            sums = lse[window, :]
            sums = jnp.where(lane == 2 * pp, total[:rows], sums)
            sums = jnp.where(lane == 2 * pp + 1, total[rows:], sums)
            place_rows(lse, slice(None), sums, start, begin)
        return 0

    lse[...] = jnp.ones_like(lse)
    lax.fori_loop(0, PAIRS, attend, 0)
    even = iota((LENGTH, 128), 1) % 2 == 0
    high, rest = split(-jnp.log(lse[...]))
    nlg[0:LENGTH, :] = jnp.where(even, high, rest)

    loads[3].wait()
    weights[1].wait()
    nm = big.at[:, pl.ds(1024, D)]
    act = big.at[:, pl.ds(0, 2 * FW)]
    gh = big.at[:, pl.ds(512, 2 * FW)]

    def middle(i, _):
        rows = rows_of(i)
        m = xp[rows].astype(f32) + dot(att[rows], wo[...])
        mid[rows] = m
        standard, _unused = norm_rows(m)
        nm[rows] = (standard * ln2).astype(bf16)
        return 0

    lax.fori_loop(0, 4, middle, 0)

    def down_rows(i):
        return wds.at[pl.ds(pl.multiple_of(i * FW, FW), FW)]

    def ff_loads(j, slot):
        cols = pl.ds(pl.multiple_of(j * FW, FW), FW)
        return [
            pltpu.make_async_copy(wup.at[:, cols], wus.at[slot, :, pl.ds(0, FW)], fsem.at[slot, 0]),
            pltpu.make_async_copy(
                wup_x.at[:, cols], wus.at[slot, :, pl.ds(FW, FW)], fsem.at[slot, 1]
            ),
            pltpu.make_async_copy(wdn.at[cols], down_rows(2 * slot), fsem.at[slot, 2]),
            pltpu.make_async_copy(wdn_x.at[cols], down_rows(2 * slot + 1), fsem.at[slot, 3]),
        ]

    weights[2].wait()
    weights[3].wait()
    for c in ff_loads(0, 0):
        c.start()
    outa[...] = jnp.zeros_like(outa)
    gna[...] = jnp.zeros_like(gna)

    def feed_event(j):
        for stage in range(4, -1, -1):
            lag = FF_LAG[stage]
            if lag < FF_CHUNKS:

                @pl.when(j >= lag)
                def _(stage=stage, lag=lag):
                    advance(stage, j - lag, True)

    def feed(j, _):
        slot = lax.rem(j, 2)
        for c in ff_loads(j, slot):
            c.wait()

        @pl.when(j < FF_CHUNKS - 1)
        def _():
            for c in ff_loads(j + 1, 1 - slot):
                c.start()

        wu = wus[slot]
        wd = wds[pl.ds(pl.multiple_of(slot * 2 * FW, 2 * FW), 2 * FW), :]
        for r in range(0, LENGTH, 256):
            rows = slice(r, r + 256)
            a, slope = gelu_and_slope(dot(nm[rows], wu))
            act[rows] = a.astype(bf16)
            gh[rows] = (dot_nt(cp[rows], wd) * slope).astype(bf16)
        outa[...] += dot(act[...], wd)
        gna[...] += dot_nt(gh[...], wu)
        up = dot_tn(nm[...], gh[...]).astype(bf16)
        dn = dot_tn(cp[...], act[...]).astype(bf16)
        for b in range(16):
            part = slice(48 * b, 48 * b + 48)
            af[j, places[b], :, 0:FW] = up[part, :FW]
            af[j, places[b], :, FW : 2 * FW] = dn[part, :FW]
            sbuf[slot, places[b], :, 0:FW] = up[part, FW:]
            sbuf[slot, places[b], :, FW : 2 * FW] = dn[part, FW:]
        feed_event(j)
        rs_copy(0, j, True).start()
        return 0

    lax.fori_loop(0, FF_CHUNKS, feed, 0)

    lob = cp

    def norm2_back(i, total):
        rows = rows_of(i)
        m = mid[rows]
        standard, inverse = norm_rows(m)
        grad = gna[rows]
        grad_mid = cp[rows].astype(f32) + norm_rows_back(grad, standard, inverse, ln2)
        gna[rows] = grad_mid
        gb[rows] = grad_mid.astype(bf16)
        lob[rows] = (m + outa[rows]).astype(bf16)
        return total + jnp.sum(grad * standard, axis=0, keepdims=True)

    ln2_terms = lax.fori_loop(0, 4, norm2_back, jnp.zeros((1, D), f32))

    def put(c, slot, own, other):
        for b in range(16):
            part = slice(48 * b, 48 * b + 48)
            ap[c - FF_CHUNKS, places[b]] = own[part]
            sbuf[slot, places[b], :, 0:384] = other[part]

    pg = dot_tn(gb[...], att[...]).astype(bf16)
    put(FF_CHUNKS, 0, pg[:, :384], pg[:, 384:])
    event(6)

    ga = dot_nt(gb[...], wo[...])
    gab = ga.astype(bf16)
    do[0:LENGTH, :] = gab
    high, rest = split(gab.astype(f32) * att[...].astype(f32))
    gather = (iota((D, 128), 0) // HD == iota((D, 128), 1) // 2).astype(f32).astype(bf16)
    delta = dot(high, gather) + dot(rest, gather)
    high, rest = split(delta)
    dlt[0:LENGTH, :] = jnp.where(even, high, rest)

    block2 = (iota((256, 128), 0) % 128 // HD == iota((256, 128), 1) // HD).astype(f32) * (1.0 / HD)
    block2 = block2.astype(bf16)

    def head_mean(x):
        return dot(jnp.concatenate(split(x), axis=1), block2)

    def head_norm_back(grad, standard, inverse, gain, means):
        c = grad * gain
        return inverse * (c - means(c) - standard * means(c * standard))

    dq, dk, dv = (outa.at[:, pl.ds(128 * i, 128)] for i in range(3))

    def attend_back(pp, col):
        for start, rows, begin, end in WINDOWS:
            window = slice(start, start + rows)
            qrows = 256 if rows > 48 else 48
            qwin = slice(start, start + qrows)
            lane = iota((2 * rows, 128), 1)
            head = 2 * pp + jnp.where(iota((2 * rows, 128), 0) < rows, 0, 1)
            hot = (lane // 2 == head).astype(f32).astype(bf16)
            kb = k[pp, window, :]
            qb = q[pp, qwin, :]
            st = dot_nt(
                jnp.concatenate([two_heads(kb, rows), hot], axis=1),
                jnp.concatenate([qb, nlg[qwin, :]], axis=1),
            )
            pt = jnp.exp(st)
            qr = iota((qrows, 128), 0) + start
            valid = (qr >= begin) & (qr < end)
            dob = do[qwin, pl.ds(pl.multiple_of(pp * 128, 128), 128)]
            zero = jnp.zeros_like(dob)
            dob = jnp.where(valid, dob, zero)
            dpt = dot_nt(
                jnp.concatenate([two_heads(v[pp, window, :], rows), -hot], axis=1),
                jnp.concatenate([dob, jnp.where(valid, dlt[qwin, :], zero)], axis=1),
            )
            dst = (pt * dpt).astype(bf16)
            dv2 = dot(pt.astype(bf16), dob)
            dk2 = dot(dst, qb)
            kr = iota((rows, 128), 0) + start
            kz = jnp.where((kr >= begin) & (kr < end), kb, jnp.zeros_like(kb))
            dq2 = dot_tn(dst, two_heads(kz, rows))[:rows]
            low = low_lanes(rows)
            every = slice(None)
            place_rows(dv, every, jnp.where(low, dv2[:rows], dv2[rows:]), start, begin)
            place_rows(dk, every, jnp.where(low, dk2[:rows], dk2[rows:]), start, begin)
            place_rows(dq, every, dq2, start, begin)
        standard = q[pp, 0:LENGTH, :].astype(f32) * (8.0 / qg)
        grad = dq[...] * 0.125
        q_terms = jnp.sum(grad * standard, axis=0, keepdims=True)
        big[:, col(0)] = head_norm_back(grad, standard, invq[pp].astype(f32), qg, head_mean).astype(bf16)
        standard = k[pp, 0:LENGTH, :].astype(f32) * (1.0 / kg)
        grad = dk[...]
        k_terms = jnp.sum(grad * standard, axis=0, keepdims=True)
        big[:, col(1)] = head_norm_back(grad, standard, invk[pp].astype(f32), kg, head_mean).astype(bf16)
        big[:, col(2)] = dv[...].astype(bf16)
        return q_terms, k_terms

    def weight_of(m):
        return jnp.concatenate(
            [wq[p, part, :, 128 * m : 128 * m + 128] for p in range(2) for part in range(3)], axis=1
        )

    def gain_copy(i):
        return pltpu.make_async_remote_copy(
            src_ref=gsend.at[i],
            dst_ref=grecv.at[i],
            send_sem=gssem.at[i],
            recv_sem=grsem.at[i],
            device_id=partners[i],
            device_id_type=MESH,
        )

    def gain_step(i):
        gain_copy(i).wait()
        total = gsend[i] + grecv[i]
        if i < 4:
            gsend[i + 1] = total
            gain_copy(i + 1).start()
        else:
            gains_sum[...] = total

    ln1_sum = jnp.zeros((D, 128), f32)
    q_terms = jnp.zeros((1, 128), f32)
    k_terms = jnp.zeros((1, 128), f32)
    for m in range(3):

        def pair(i, carry, m=m):
            def col(part):
                return pl.ds(pl.multiple_of(768 * m + 384 * i + 128 * part, 128), 128)

            a, b = attend_back(3 * i + m, col)

            @pl.when(i == 0)
            def _():
                event(7 + 2 * m)

            return carry[0] + a, carry[1] + b

        q_terms, k_terms = lax.fori_loop(0, 2, pair, (q_terms, k_terms))
        both = dot_tn(ni[...], big[:, 768 * m : 768 * m + 768])
        wide = both * weight_of(m).astype(f32)
        for tile in range(6):
            ln1_sum = ln1_sum + wide[:, 128 * tile : 128 * tile + 128]
        both = both.astype(bf16)
        c = FF_CHUNKS + 1 + m
        put(c, c % 2, both[:, :384], both[:, 384:])
        if m == 2:
            high, rest = split(ln1_sum)
            ones = jnp.ones((16, 128), bf16)
            ln1_terms = (dot_nt(ones, high) + dot_nt(ones, rest))[0:1] / ln1
            gsend[0] = jnp.concatenate(
                [ln1_terms[:, 128 * i : 128 * i + 128] for i in range(6)]
                + [ln2_terms[:, 128 * i : 128 * i + 128] for i in range(6)]
                + [q_terms, k_terms, jnp.zeros((2, 128), f32)],
                axis=0,
            )
            gain_copy(0).start()
        event(8 + 2 * m)

    gsum = outa
    gsum[...] = dot_nt(big[:, 0:768], weight_of(0))
    gsum[...] += dot_nt(big[:, 768:1536], weight_of(1))
    gain_step(0)
    event(13)
    gsum[...] += dot_nt(big[:, 1536:2304], weight_of(2))
    igb = ni

    def norm1_back(i, _):
        rows = rows_of(i)
        standard, inverse = norm_rows(xp[rows].astype(f32))
        igb[rows] = (gna[rows] + norm_rows_back(gsum[rows], standard, inverse, ln1)).astype(bf16)
        return 0

    def unpermute(src, dst, out, sem):
        for i, (first, n, ranges) in enumerate(TILES_OUT):
            rows = slice(first, first + n)
            dst[rows] = picked(pick(first, n, ranges, out_of_order), ranges, src).astype(bf16)
            send_out(
                functools.partial(
                    pltpu.make_async_copy,
                    dst.at[pl.ds(first, n)],
                    out.at[pl.ds(first, n)],
                    sem.at[i],
                )
            )

    lax.fori_loop(0, 2, norm1_back, 0)
    unpermute(lob, tokv, lay_out, osem.at[0])
    gain_step(1)
    event(14)
    lax.fori_loop(2, 4, norm1_back, 0)
    unpermute(igb, cotv, inp_out, osem.at[1])
    gain_step(2)
    event(15)
    gain_step(3)
    event(16)
    gain_step(4)
    send_out(functools.partial(pltpu.make_async_copy, gains_sum, gains_out, osem.at[14, 0]))
    event(17)
    for copy in copies:
        copy().wait()


def hand_on(*refs):
    n = 6
    ins, gains_in = refs[:n], refs[n]
    outs, gain_outs = refs[n + 1 : 2 * n + 1], refs[2 * n + 1 : 2 * n + 5]
    held, gains, lines, sems = refs[2 * n + 5 : 3 * n + 5], refs[-6], refs[-5:-1], refs[-1]
    gains_come = pltpu.make_async_copy(gains_in, gains, sems.at[4 * n])
    gains_come.start()
    copies = []
    for i, (src, dst) in enumerate(zip(ins, outs)):
        parts = 4 if src.shape[0] == LENGTH else 1
        size = src.shape[0] // parts
        for part in range(parts):
            rows = pl.ds(part * size, size)
            sem = sems.at[4 * i + part]
            copies.append(
                (
                    pltpu.make_async_copy(src.at[rows], held[i].at[rows], sem),
                    pltpu.make_async_copy(held[i].at[rows], dst.at[rows], sem),
                )
            )
    for come, _go in copies:
        come.start()
    gains_come.wait()
    ln1, ln2, qg, kg = lines
    for i in range(6):
        ln1[pl.ds(128 * i, 128)] = gains[i, :]
        ln2[pl.ds(128 * i, 128)] = gains[6 + i, :]
    qg[...] = gains[12, 0:HD] + gains[12, HD : 2 * HD]
    kg[...] = gains[13, 0:HD] + gains[13, HD : 2 * HD]
    gains_go = [
        pltpu.make_async_copy(src, dst, sems.at[4 * n + 1 + i])
        for i, (src, dst) in enumerate(zip(lines, gain_outs))
    ]
    for go in gains_go:
        go.start()
    for come, go in copies:
        come.wait()
        go.start()
    for go in gains_go:
        go.wait()
    for _come, go in copies:
        go.wait()


def local(
    tokens, segment, ln1_gain, w_qkv, q_gain, k_gain, w_out, ln2_gain, w_up, w_down, cotangent
):
    groups = lax.axis_size("dp")
    dp_low = groups // (1 << BITS)
    rows = D >> BITS
    hbm = pl.BlockSpec(memory_space=pl.ANY)
    shape = jax.ShapeDtypeStruct
    half_ff = w_up.shape[1]
    ff, wide, n_proj = FF_CHUNKS, 2 * FW, CHUNKS - FF_CHUNKS

    def mem(*dims, dtype=bf16):
        return pltpu.VMEM(dims, dtype)

    outs = pl.pallas_call(
        functools.partial(kernel, dp_low),
        out_shape=(
            shape((LENGTH, D), bf16),
            shape((LENGTH, D), bf16),
            shape((rows, half_ff), f32),
            shape((rows, half_ff), f32),
            shape((rows, 384), f32),
            shape((3, rows, 384), f32),
            shape((16, 128), f32),
            shape((D, half_ff), bf16),
            shape((half_ff, D), bf16),
        ),
        in_specs=[hbm] * 11,
        out_specs=(hbm,) * 9,
        scratch_shapes=[
            pltpu.SMEM(segment.shape, jnp.int32),
            mem(D, dtype=f32),
            mem(D, dtype=f32),
            mem(HD, dtype=f32),
            mem(HD, dtype=f32),
            mem(LENGTH, D),
            mem(LENGTH, D),
            mem(LENGTH, D),
            mem(LENGTH, D),
            mem(LENGTH, D),
            mem(PAIRS, PADDED, 128),
            mem(PAIRS, PADDED, 128),
            mem(PAIRS, PADDED, 128),
            mem(PAIRS, LENGTH, 128),
            mem(PAIRS, LENGTH, 128),
            mem(PADDED, 128),
            mem(PADDED, 128),
            mem(LENGTH, D, dtype=f32),
            mem(LENGTH, D, dtype=f32),
            mem(LENGTH, D, dtype=f32),
            mem(LENGTH, 3 * D),
            mem(2, D, wide),
            mem(PADDED, D),
            mem(2, 3, D, 384),
            mem(D, D),
            mem(2, 16, rows, wide),
            mem(2, 16, rows, wide),
            mem(ff, 16, rows, wide),
            mem(ff, 8, rows, wide),
            mem(ff, 4, rows, wide),
            mem(ff, 2, rows, wide),
            mem(ff, 1, rows, wide),
            mem(n_proj, 16, rows, 384),
            mem(n_proj, 8, rows, 384),
            mem(n_proj, 4, rows, 384),
            mem(n_proj, 2, rows, 384),
            mem(n_proj, 1, rows, 384),
            mem(5, 16, 128, dtype=f32),
            mem(5, 16, 128, dtype=f32),
            mem(16, 128, dtype=f32),
            pltpu.SemaphoreType.DMA((CHUNKS, 5)),
            pltpu.SemaphoreType.DMA((CHUNKS, 5)),
            pltpu.SemaphoreType.DMA((5,)),
            pltpu.SemaphoreType.DMA((5,)),
            pltpu.SemaphoreType.DMA((4,)),
            pltpu.SemaphoreType.DMA((4,)),
            pltpu.SemaphoreType.DMA((9,)),
            pltpu.SemaphoreType.DMA((2, 4)),
            pltpu.SemaphoreType.DMA((15, 4)),
        ],
        compiler_params=pltpu.CompilerParams(
            collective_id=0, has_side_effects=True, vmem_limit_bytes=255 * 2**18
        ),
        name="layer",
    )(
        segment,
        tokens,
        cotangent,
        ln1_gain,
        ln2_gain,
        q_gain,
        k_gain,
        jnp.transpose(w_qkv, (1, 0, 2)),
        w_out,
        w_up,
        w_down,
    )
    results, gains = list(outs[:6]), outs[6]
    if dp_low > 1:
        peers = [[hi * dp_low + lo for lo in range(dp_low)] for hi in range(1 << BITS)]

        def rest(x, axis):
            return lax.psum_scatter(
                x, "dp", scatter_dimension=axis, axis_index_groups=peers, tiled=True
            )

        results[2:] = [rest(x, x.ndim - 2) for x in results[2:]]
        gains = lax.psum(gains, "dp", axis_index_groups=peers)
    (
        layer_out,
        input_grad,
        up_grad,
        down_grad,
        proj_grad,
        qkv_grad,
        ln1_grad,
        ln2_grad,
        q_grad,
        k_grad,
    ) = pl.pallas_call(
        hand_on,
        out_shape=[shape(x.shape, x.dtype) for x in results]
        + [shape((D,), f32)] * 2
        + [shape((HD,), f32)] * 2,
        in_specs=[pl.BlockSpec(memory_space=pltpu.HBM)] * 7,
        out_specs=[pl.BlockSpec(memory_space=pltpu.HBM)] * 10,
        scratch_shapes=[pltpu.VMEM(x.shape, x.dtype) for x in results + [gains]]
        + [mem(D, dtype=f32)] * 2
        + [mem(HD, dtype=f32)] * 2
        + [pltpu.SemaphoreType.DMA((29,))],
        name="hand_on",
    )(*results, gains)
    return (
        layer_out,
        input_grad,
        ln1_grad,
        jnp.transpose(qkv_grad, (1, 0, 2)),
        q_grad,
        k_grad,
        proj_grad.T,
        ln2_grad,
        up_grad,
        down_grad.T,
    )


def solution(mesh):
    return jax.shard_map(
        local,
        mesh=mesh,
        in_specs=(
            P(("dp", "tensor"), None),
            P("dp"),
            P(),
            P(None, None, "tensor"),
            P(),
            P(),
            P("tensor", None),
            P(),
            P(None, "tensor"),
            P("tensor", None),
            P(("dp", "tensor"), None),
        ),
        out_specs=(
            P(("dp", "tensor"), None),
            P(("dp", "tensor"), None),
            P(),
            P("dp", None, "tensor"),
            P(),
            P(),
            P("tensor", "dp"),
            P(),
            P("dp", "tensor"),
            P("tensor", "dp"),
        ),
        check_vma=False,
    )
```

```python
import functools

import jax
import jax.numpy as jnp
from jax import lax
from jax.experimental import pallas as pl
from jax.experimental.pallas import tpu as pltpu
from jax.sharding import PartitionSpec as P

D = 768
HD = 64
LENGTH = 1024
PATCHES = 196
IMAGES = 5
PADDING = LENGTH - IMAGES * PATCHES
PADDED = 1040
PAIRS = 6
EPS = 1e-06
MESH = pl.DeviceIdType.MESH
f32, bf16 = jnp.float32, jnp.bfloat16

WINDOWS = [
    (PATCHES * i // 16 * 16, 208, PATCHES * i, PATCHES * (i + 1)) for i in range(IMAGES)
] + [(976, 48, 980, 1024)]

FF_CHUNKS = 6
FW = 256
BITS = 4

CHUNKS = 12
START = [0, 1, 2, 3, 4, 5, 6, 8, 10, 12, 12, 12]
FF_LAG = (1, 3, 6, 8, 11)
LAG = [FF_LAG] * FF_CHUNKS + [(1, 3, 5, 7, 10), (1, 3, 5, 7, 8), (1, 3, 4, 5, 7)] + [(1, 2, 3, 4, 5)] * 3

LAST_BITS = {}

TILES_IN = [
    (0, 256, [(0, 384)]),
    (256, 256, [(256, 384)]),
    (512, 256, [(512, 384)]),
    (768, 128, [(768, 256)]),
    (896, 128, [(0, 1024)]),
]
TILES_OUT = [
    (0, 256, [(0, 256), (896, 128)]),
    (256, 256, [(128, 384), (896, 128)]),
    (512, 256, [(384, 384), (896, 128)]),
    (768, 256, [(640, 384)]),
]


def dot(left, right):
    return jnp.dot(left, right, preferred_element_type=f32)


def dot_nt(left, right):
    return lax.dot_general(left, right, (((1,), (1,)), ((), ())), preferred_element_type=f32)


def dot_tn(left, right):
    return lax.dot_general(left, right, (((0,), (0,)), ((), ())), preferred_element_type=f32)


def gelu_and_slope(h):
    e = jnp.exp(h * h * -0.5)
    t = 1.0 / (1.0 + jnp.abs(h) * (0.3275911 * 0.7071067811865476))
    poly = t * (
        0.5 * 0.254829592
        + t
        * (
            0.5 * -0.284496736
            + t * (0.5 * 1.421413741 + t * (0.5 * -1.453152027 + t * (0.5 * 1.061405429)))
        )
    )
    tail = poly * e
    phi = jnp.where(h >= 0, 1.0 - tail, tail)
    return h * phi, phi + h * e * 0.3989422804014327


def split(x):
    high = x.astype(bf16)
    return high, (x - high.astype(f32)).astype(bf16)


def iota(shape, axis):
    return lax.broadcasted_iota(jnp.int32, shape, axis)


def norm_rows(x):
    centred = x - jnp.mean(x, axis=-1, keepdims=True)
    inverse = lax.rsqrt(jnp.mean(centred * centred, axis=-1, keepdims=True) + EPS)
    return centred * inverse, inverse


def norm_rows_back(grad, standard, inverse, gain):
    c = grad * gain
    return inverse * (
        c
        - jnp.mean(c, axis=-1, keepdims=True)
        - standard * jnp.mean(c * standard, axis=-1, keepdims=True)
    )


def swap(pos):
    return (pos & 4) | (pos & 1) | ((pos & 8) >> 2) | ((pos & 2) << 2)


def kernel(
    dp_low,
    seg_hbm,
    tok,
    cot,
    ln1_hbm,
    ln2_hbm,
    qgain_hbm,
    kgain_hbm,
    wqkv,
    wout,
    wup,
    wdn,
    lay_out,
    inp_out,
    up_out,
    dn_out,
    pr_out,
    qk_out,
    gains_out,
    wup_x,
    wdn_x,
    seg,
    ln1v,
    ln2v,
    qgv,
    kgv,
    tokv,
    cotv,
    xp,
    cp,
    ni,
    q,
    k,
    v,
    invq,
    invk,
    nlg,
    dlt,
    mid,
    outa,
    gna,
    big,
    wus,
    wds,
    wq,
    wo,
    sbuf,
    r0,
    af,
    r1f,
    r2f,
    r3f,
    r4f,
    ap,
    r1p,
    r2p,
    r3p,
    r4p,
    gsend,
    grecv,
    gains_sum,
    ssem,
    rsem,
    gssem,
    grsem,
    wssem,
    wrsem,
    lsem,
    rsem0,
    fsem,
    osem,
):
    att = tokv
    gb = cotv
    lse = mid.at[:, pl.ds(0, 128)]
    do = wds
    g = lax.axis_index("dp")
    t = lax.axis_index("tensor")
    top, low = g // dp_low, g % dp_low
    mine = [(top // (1 << b)) % 2 for b in range(BITS)]

    def peer(b):
        return ((top + (1 - 2 * mine[b]) * (1 << b)) * dp_low + low, t)

    d0, d1 = peer(0)[0], peer(1)[0]
    core = (g, 1 - t)
    first = (jnp.where(t == 0, d0, d1), t)
    third = (jnp.where(t == 0, d1, d0), t)
    partners = (core, first, peer(2), third, peer(3))

    def place(b):
        rel = [mine[i] if (b >> i) & 1 == 0 else 1 - mine[i] for i in range(BITS)]
        one = rel[0] * 8 + rel[1] * 2
        two = rel[1] * 8 + rel[0] * 2
        return one + t * (two - one) + rel[2] * 4 + rel[3]

    places = [place(b) for b in range(16)]

    def last_place(c, b):
        rel = [mine[i] if (b >> i) & 1 == 0 else 1 - mine[i] for i in LAST_BITS[c]]
        return rel[0] * 8 + rel[1] * 4 + rel[2] * 2 + rel[3]

    def partner_of(stage, c, is_ff):
        if stage > 0 and not is_ff and c in LAST_BITS:
            return peer(LAST_BITS[c][stage - 1])
        return partners[stage]

    barrier = pltpu.get_barrier_semaphore()
    for partner in partners:
        pl.semaphore_signal(barrier, inc=1, device_id=partner, device_id_type=MESH)

    loads = [
        pltpu.make_async_copy(wqkv, wq.at[0], lsem.at[0]),
        pltpu.make_async_copy(wout, wo.at[pl.ds(0, 384)], lsem.at[1]),
        pltpu.make_async_copy(seg_hbm, seg, lsem.at[2]),
        pltpu.make_async_copy(ln1_hbm, ln1v, lsem.at[3]),
        pltpu.make_async_copy(ln2_hbm, ln2v, lsem.at[4]),
        pltpu.make_async_copy(qgain_hbm, qgv, lsem.at[5]),
        pltpu.make_async_copy(kgain_hbm, kgv, lsem.at[6]),
    ]
    row_loads = []
    for i in range(4):
        rows = pl.ds(256 * i, 256)
        row_loads.append(pltpu.make_async_copy(tok.at[rows], tokv.at[rows], rsem0.at[i]))
        row_loads.append(pltpu.make_async_copy(cot.at[rows], cotv.at[rows], rsem0.at[4 + i]))
    for c in loads[2:] + row_loads + loads[:2]:
        c.start()

    def weight_copy(i, src, dst):
        return pltpu.make_async_remote_copy(
            src_ref=src,
            dst_ref=dst,
            send_sem=wssem.at[i],
            recv_sem=wrsem.at[i],
            device_id=core,
            device_id_type=MESH,
        )

    weights = [
        weight_copy(0, wqkv, wq.at[1]),
        weight_copy(1, wout, wo.at[pl.ds(384, 384)]),
        weight_copy(2, wup, wup_x),
        weight_copy(3, wdn, wdn_x),
    ]

    def chunk_refs(c, is_ff):
        if is_ff:
            slot = lax.rem(c, 2)
            return sbuf.at[slot], r0.at[slot], af.at[c], [r.at[c] for r in (r1f, r2f, r3f, r4f)]
        n = min(c, 9) - FF_CHUNKS
        lanes = pl.ds(128 * (c - 9), 128) if c >= 9 else pl.ds(0, 384)
        slot = min(c, 9) % 2
        return (
            sbuf.at[slot, :, :, lanes],
            r0.at[slot, :, :, lanes],
            ap.at[n, :, :, lanes],
            [r.at[n, :, :, lanes] for r in (r1p, r2p, r3p, r4p)],
        )

    def rs_copy(stage, c, is_ff):
        src, dst, a, rs = chunk_refs(c, is_ff)
        if stage > 0:
            half = 16 >> stage
            src, dst = a.at[pl.ds(half, half)], rs[stage - 1]
        return pltpu.make_async_remote_copy(
            src_ref=src,
            dst_ref=dst,
            send_sem=ssem.at[c, stage],
            recv_sem=rsem.at[c, stage],
            device_id=partner_of(stage, c, is_ff),
            device_id_type=MESH,
        )

    copies = []

    def send_out(copy):
        copies.append(copy)
        copy().start()

    def finish(c, total):
        mid[48 * c : 48 * c + 48, 0 : total.shape[1]] = total

        def part(first, width, out, place, i):
            def copy():
                src = mid.at[pl.ds(48 * c, 48), pl.ds(first, width)]
                return pltpu.make_async_copy(src, out.at[place], osem.at[2 + c, i])

            send_out(copy)

        every = slice(None)
        if c < FF_CHUNKS:
            part(0, FW, up_out, (every, pl.ds(c * FW, FW)), 0)
            part(FW, FW, dn_out, (every, pl.ds(c * FW, FW)), 1)
        elif c == FF_CHUNKS:
            part(0, 384, pr_out, (every, every), 0)
        elif c < 9:
            for i in range(3):
                m = c - FF_CHUNKS - 1
                part(128 * i, 128, qk_out, (i, every, pl.ds(128 * m, 128)), i)
        else:
            part(0, 128, qk_out, (c - 9, every, pl.ds(256, 128)), 0)

    def advance(stage, c, is_ff):
        _src, arrived, a, rs = chunk_refs(c, is_ff)
        rs_copy(stage, c, is_ff).wait()
        if stage == 0:
            for pos in range(16):
                same_way = not is_ff and c in LAST_BITS
                a[pos] = a[pos] + arrived[pos if same_way else swap(pos)]
        elif stage < 4:
            half = 16 >> stage
            for pos in range(half):
                a[pos] = a[pos] + rs[stage - 1][pos]
        else:
            finish(c, a[0].astype(f32) + rs[3][0].astype(f32))
        if stage < 4:
            rs_copy(stage + 1, c, is_ff).start()

    def event(e):
        for stage in range(4, -1, -1):
            for c in range(CHUNKS):
                if START[c] + LAG[c][stage] == e:
                    advance(stage, c, c < FF_CHUNKS)
        for c in range(CHUNKS):
            if START[c] == e:
                rs_copy(0, c, c < FF_CHUNKS).start()

    for c in loads[2:]:
        c.wait()
    s = jnp.int32(0)
    for image in range(IMAGES + 1):
        s = s + jnp.where(seg[t * LENGTH + PATCHES * image] == -1, image, 0)
    ln1 = ln1v[...].reshape(1, D)
    ln2 = ln2v[...].reshape(1, D)
    qg = qgv[...].reshape(1, HD)
    qg = jnp.concatenate([qg, qg], axis=1)
    kg = kgv[...].reshape(1, HD)
    kg = jnp.concatenate([kg, kg], axis=1)
    zero_rows = jnp.zeros((PADDED - LENGTH, 128), bf16)
    for pp in range(PAIRS):
        for ref in (q, k, v):
            ref[pp, LENGTH:, :] = zero_rows
    do[LENGTH:, :] = jnp.zeros((PADDED - LENGTH, D), bf16)
    nlg[LENGTH:, :] = zero_rows
    dlt[LENGTH:, :] = zero_rows

    def rows_of(i):
        return pl.ds(pl.multiple_of(i * 256, 256), 256)

    def pick(first, rows, ranges, source):
        wanted = source(iota((rows, 1), 0) + first)
        parts = [iota((rows, n), 1) + start == wanted for start, n in ranges]
        return jnp.concatenate([p.astype(f32).astype(bf16) for p in parts], axis=1)

    def picked(matrix, ranges, ref):
        return dot(matrix, jnp.concatenate([ref[start : start + n] for start, n in ranges], axis=0))

    def in_order(r):
        image_row = r + jnp.where(r >= PATCHES * s, PADDING, 0)
        return jnp.where(r < IMAGES * PATCHES, image_row, PATCHES * s + r - IMAGES * PATCHES)

    def out_of_order(r):
        behind = jnp.where(
            r < PATCHES * s + PADDING, r - PATCHES * s + IMAGES * PATCHES, r - PADDING
        )
        return jnp.where(r < PATCHES * s, r, behind)

    def permute(first, n, ranges):
        rows = slice(first, first + n)
        matrix = pick(first, n, ranges, in_order)
        x = picked(matrix, ranges, tokv)
        xp[rows] = x.astype(bf16)
        standard, _unused = norm_rows(x)
        ni[rows] = (standard * ln1).astype(bf16)
        cp[rows] = picked(matrix, ranges, cotv).astype(bf16)

    for c in row_loads[:4]:
        c.wait()
    permute(*TILES_IN[0])
    for c in row_loads[4:6]:
        c.wait()
    permute(*TILES_IN[1])
    pl.semaphore_wait(barrier, len(partners))
    for c in weights:
        c.start()
    for c in row_loads[6:]:
        c.wait()
    for tile in TILES_IN[2:]:
        permute(*tile)

    def lane_means(x):
        out = []
        for first in range(0, x.shape[1], 128):
            part = x[:, first : first + 128]
            low = iota(part.shape, 1) < HD
            low_sum = jnp.sum(jnp.where(low, part, 0.0), axis=1, keepdims=True)
            high_sum = jnp.sum(part, axis=1, keepdims=True) - low_sum
            out.append(jnp.where(low, low_sum, high_sum) * (1.0 / HD))
        return jnp.concatenate(out, axis=1)

    block = (iota((256, 256), 0) // HD == iota((256, 256), 1) // HD).astype(f32) * (1.0 / HD)
    block = block.astype(bf16)

    def head_norm(y, pair_of, by_lanes):
        if by_lanes:
            centred = y - lane_means(y)
            spread = lane_means(centred * centred)
        else:
            high, rest = split(y)
            centred = y - (dot(high, block) + dot(rest, block))
            spread = dot((centred * centred).astype(bf16), block)
        inverse = lax.rsqrt(spread + EPS)
        standard = centred * inverse
        for half in range(2):
            lanes = slice(128 * half, 128 * half + 128)
            dest, inv_dest, dest_gain, pp = pair_of(half)
            dest[pp, 0:LENGTH, :] = (standard[:, lanes] * dest_gain).astype(bf16)
            inv_dest[pp] = inverse[:, lanes].astype(bf16)

    def project(p):
        for tile in range(3):
            parts = []
            for half in range(2):
                idx = 2 * tile + half
                part, m = idx // 3, idx % 3
                parts.append(wq[p, part, :, 128 * m : 128 * m + 128])
            y = dot(ni[...], jnp.concatenate(parts, axis=1))

            def pair_of(half, tile=tile):
                idx = 2 * tile + half
                pp = p * 3 + idx % 3
                if idx < 3:
                    return q, invq, qg * 0.125, pp
                return k, invk, kg, pp

            head_norm(y, pair_of, tile != 1)
        y = dot(ni[...], wq[p, 2]).astype(bf16)
        for m in range(3):
            v[p * 3 + m, 0:LENGTH, :] = y[:, 128 * m : 128 * m + 128]

    loads[0].wait()
    project(0)
    weights[0].wait()
    project(1)

    def low_lanes(rows):
        return iota((rows, 128), 1) < HD

    def two_heads(x, rows):
        low = low_lanes(rows)
        zero = jnp.zeros_like(x)
        return jnp.concatenate([jnp.where(low, x, zero), jnp.where(low, zero, x)], axis=0)

    def place_rows(ref, cols, new, start, begin):
        rows = new.shape[0]
        if begin > start:
            top = slice(start, start + 16)
            keep = iota((16, 128), 0) + start < begin
            ref[top, cols] = jnp.where(keep, ref[top, cols], new[:16])
            ref[start + 16 : start + rows, cols] = new[16:]
        else:
            ref[start : start + rows, cols] = new

    def attend(pp, _):
        cols = pl.ds(pl.multiple_of(pp * 128, 128), 128)
        for start, rows, begin, end in WINDOWS:
            window = slice(start, start + rows)
            krows = 256 if rows > 48 else 48
            kwin = slice(start, start + krows)
            scores = dot_nt(two_heads(q[pp, window, :], rows), k[pp, kwin, :])
            weight = jnp.exp(scores).astype(bf16)
            kr = iota((krows, 256), 0) + start
            vone = jnp.concatenate([v[pp, kwin, :], jnp.ones((krows, 128), bf16)], axis=1)
            vone = jnp.where((kr >= begin) & (kr < end), vone, jnp.zeros_like(vone))
            both = dot(weight, vone)
            total = both[:, 128:]
            heads = both[:, :128] / total
            merged = jnp.where(low_lanes(rows), heads[:rows], heads[rows:]).astype(bf16)
            place_rows(att, cols, merged, start, begin)
            lane = iota((rows, 128), 1) // 2
            sums = lse[window, :]
            sums = jnp.where(lane == 2 * pp, total[:rows], sums)
            sums = jnp.where(lane == 2 * pp + 1, total[rows:], sums)
            place_rows(lse, slice(None), sums, start, begin)
        return 0

    lse[...] = jnp.ones_like(lse)
    lax.fori_loop(0, PAIRS, attend, 0)
    even = iota((LENGTH, 128), 1) % 2 == 0
    high, rest = split(-jnp.log(lse[...]))
    nlg[0:LENGTH, :] = jnp.where(even, high, rest)

    loads[1].wait()
    weights[1].wait()
    nm = big.at[:, pl.ds(1024, D)]
    act = big.at[:, pl.ds(0, 2 * FW)]
    gh = big.at[:, pl.ds(512, 2 * FW)]

    def middle(i, _):
        rows = rows_of(i)
        m = xp[rows].astype(f32) + dot(att[rows], wo[...])
        mid[rows] = m
        standard, _unused = norm_rows(m)
        nm[rows] = (standard * ln2).astype(bf16)
        return 0

    lax.fori_loop(0, 4, middle, 0)

    def down_rows(i):
        return wds.at[pl.ds(pl.multiple_of(i * FW, FW), FW)]

    def ff_loads(j, slot):
        cols = pl.ds(pl.multiple_of(j * FW, FW), FW)
        return [
            pltpu.make_async_copy(wup.at[:, cols], wus.at[slot, :, pl.ds(0, FW)], fsem.at[slot, 0]),
            pltpu.make_async_copy(
                wup_x.at[:, cols], wus.at[slot, :, pl.ds(FW, FW)], fsem.at[slot, 1]
            ),
            pltpu.make_async_copy(wdn.at[cols], down_rows(2 * slot), fsem.at[slot, 2]),
            pltpu.make_async_copy(wdn_x.at[cols], down_rows(2 * slot + 1), fsem.at[slot, 3]),
        ]

    weights[2].wait()
    weights[3].wait()
    for c in ff_loads(0, 0):
        c.start()
    outa[...] = jnp.zeros_like(outa)
    gna[...] = jnp.zeros_like(gna)

    def feed_event(j):
        for stage in range(5):
            lag = FF_LAG[stage]
            if lag < FF_CHUNKS:

                @pl.when(j >= lag)
                def _(stage=stage, lag=lag):
                    advance(stage, j - lag, True)
            if stage == 0:
                rs_copy(0, j, True).start()

    def feed(j, _):
        slot = lax.rem(j, 2)
        for c in ff_loads(j, slot):
            c.wait()

        @pl.when(j < FF_CHUNKS - 1)
        def _():
            for c in ff_loads(j + 1, 1 - slot):
                c.start()

        wu = wus[slot]
        wd = wds[pl.ds(pl.multiple_of(slot * 2 * FW, 2 * FW), 2 * FW), :]
        for r in range(0, LENGTH, 256):
            rows = slice(r, r + 256)
            a, slope = gelu_and_slope(dot(nm[rows], wu))
            act[rows] = a.astype(bf16)
            gh[rows] = (dot_nt(cp[rows], wd) * slope).astype(bf16)
        outa[...] += dot(act[...], wd)
        gna[...] += dot_nt(gh[...], wu)
        up = dot_tn(nm[...], gh[...]).astype(bf16)
        dn = dot_tn(cp[...], act[...]).astype(bf16)
        for b in range(16):
            part = slice(48 * b, 48 * b + 48)
            af[j, places[b], :, 0:FW] = up[part, :FW]
            af[j, places[b], :, FW : 2 * FW] = dn[part, :FW]
            sbuf[slot, places[b], :, 0:FW] = up[part, FW:]
            sbuf[slot, places[b], :, FW : 2 * FW] = dn[part, FW:]
        feed_event(j)
        return 0

    lax.fori_loop(0, FF_CHUNKS, feed, 0)

    lob = cp

    def norm2_back(i, total):
        rows = rows_of(i)
        m = mid[rows]
        standard, inverse = norm_rows(m)
        grad = gna[rows]
        grad_mid = cp[rows].astype(f32) + norm_rows_back(grad, standard, inverse, ln2)
        gna[rows] = grad_mid
        gb[rows] = grad_mid.astype(bf16)
        lob[rows] = (m + outa[rows]).astype(bf16)
        return total + jnp.sum(grad * standard, axis=0, keepdims=True)

    ln2_terms = lax.fori_loop(0, 4, norm2_back, jnp.zeros((1, D), f32))

    def put(c, slot, own, other):
        for b in range(16):
            part = slice(48 * b, 48 * b + 48)
            ap[c - FF_CHUNKS, places[b]] = own[part]
            sbuf[slot, places[b], :, 0:384] = other[part]

    pg = dot_tn(gb[...], att[...]).astype(bf16)
    put(FF_CHUNKS, 0, pg[:, :384], pg[:, 384:])
    event(6)

    ga = dot_nt(gb[...], wo[...])
    gab = ga.astype(bf16)
    do[0:LENGTH, :] = gab
    high, rest = split(gab.astype(f32) * att[...].astype(f32))
    gather = (iota((D, 128), 0) // HD == iota((D, 128), 1) // 2).astype(f32).astype(bf16)
    delta = dot(high, gather) + dot(rest, gather)
    high, rest = split(delta)
    dlt[0:LENGTH, :] = jnp.where(even, high, rest)

    block2 = (iota((256, 128), 0) % 128 // HD == iota((256, 128), 1) // HD).astype(f32) * (1.0 / HD)
    block2 = block2.astype(bf16)

    def head_mean(x):
        return dot(jnp.concatenate(split(x), axis=1), block2)

    def head_norm_back(grad, standard, inverse, gain, means):
        c = grad * gain
        return inverse * (c - means(c) - standard * means(c * standard))

    dq, dk, dv = (outa.at[:, pl.ds(128 * i, 128)] for i in range(3))

    def attend_back(pp, col):
        for start, rows, begin, end in WINDOWS:
            window = slice(start, start + rows)
            qrows = 256 if rows > 48 else 48
            qwin = slice(start, start + qrows)
            lane = iota((2 * rows, 128), 1)
            head = 2 * pp + jnp.where(iota((2 * rows, 128), 0) < rows, 0, 1)
            hot = (lane // 2 == head).astype(f32).astype(bf16)
            kb = k[pp, window, :]
            qb = q[pp, qwin, :]
            st = dot_nt(
                jnp.concatenate([two_heads(kb, rows), hot], axis=1),
                jnp.concatenate([qb, nlg[qwin, :]], axis=1),
            )
            pt = jnp.exp(st)
            qr = iota((qrows, 128), 0) + start
            valid = (qr >= begin) & (qr < end)
            dob = do[qwin, pl.ds(pl.multiple_of(pp * 128, 128), 128)]
            zero = jnp.zeros_like(dob)
            dob = jnp.where(valid, dob, zero)
            dpt = dot_nt(
                jnp.concatenate([two_heads(v[pp, window, :], rows), -hot], axis=1),
                jnp.concatenate([dob, jnp.where(valid, dlt[qwin, :], zero)], axis=1),
            )
            dst = (pt * dpt).astype(bf16)
            dv2 = dot(pt.astype(bf16), dob)
            dk2 = dot(dst, qb)
            kr = iota((rows, 128), 0) + start
            kz = jnp.where((kr >= begin) & (kr < end), kb, jnp.zeros_like(kb))
            dq2 = dot_tn(dst, two_heads(kz, rows))[:rows]
            low = low_lanes(rows)
            every = slice(None)
            place_rows(dv, every, jnp.where(low, dv2[:rows], dv2[rows:]), start, begin)
            place_rows(dk, every, jnp.where(low, dk2[:rows], dk2[rows:]), start, begin)
            place_rows(dq, every, dq2, start, begin)
        standard = q[pp, 0:LENGTH, :].astype(f32) * (8.0 / qg)
        grad = dq[...] * 0.125
        q_terms = jnp.sum(grad * standard, axis=0, keepdims=True)
        big[:, col(0)] = head_norm_back(grad, standard, invq[pp].astype(f32), qg, head_mean).astype(bf16)
        standard = k[pp, 0:LENGTH, :].astype(f32) * (1.0 / kg)
        grad = dk[...]
        k_terms = jnp.sum(grad * standard, axis=0, keepdims=True)
        big[:, col(1)] = head_norm_back(grad, standard, invk[pp].astype(f32), kg, head_mean).astype(bf16)
        big[:, col(2)] = dv[...].astype(bf16)
        return q_terms, k_terms

    def weight_of(m):
        return jnp.concatenate(
            [wq[p, part, :, 128 * m : 128 * m + 128] for p in range(2) for part in range(3)], axis=1
        )

    def gain_copy(i):
        return pltpu.make_async_remote_copy(
            src_ref=gsend.at[i],
            dst_ref=grecv.at[i],
            send_sem=gssem.at[i],
            recv_sem=grsem.at[i],
            device_id=partners[i],
            device_id_type=MESH,
        )

    def gain_step(i):
        gain_copy(i).wait()
        total = gsend[i] + grecv[i]
        if i < 4:
            gsend[i + 1] = total
            gain_copy(i + 1).start()
        else:
            gains_sum[...] = total

    ln1_sum = jnp.zeros((D, 128), f32)
    q_terms = jnp.zeros((1, 128), f32)
    k_terms = jnp.zeros((1, 128), f32)
    for m in range(3):

        def pair(i, carry, m=m):
            def col(part):
                return pl.ds(pl.multiple_of(768 * m + 384 * i + 128 * part, 128), 128)

            a, b = attend_back(3 * i + m, col)

            @pl.when(i == 0)
            def _():
                event(7 + 2 * m)

            return carry[0] + a, carry[1] + b

        q_terms, k_terms = lax.fori_loop(0, 2, pair, (q_terms, k_terms))
        both = dot_tn(ni[...], big[:, 768 * m : 768 * m + 768])
        wide = both * weight_of(m).astype(f32)
        for tile in range(6):
            ln1_sum = ln1_sum + wide[:, 128 * tile : 128 * tile + 128]
        both = both.astype(bf16)
        c = FF_CHUNKS + 1 + m
        put(c, c % 2, both[:, :384], both[:, 384:])
        if m == 2:
            high, rest = split(ln1_sum)
            ones = jnp.ones((16, 128), bf16)
            ln1_terms = (dot_nt(ones, high) + dot_nt(ones, rest))[0:1] / ln1
            gsend[0] = jnp.concatenate(
                [ln1_terms[:, 128 * i : 128 * i + 128] for i in range(6)]
                + [ln2_terms[:, 128 * i : 128 * i + 128] for i in range(6)]
                + [q_terms, k_terms, jnp.zeros((2, 128), f32)],
                axis=0,
            )
            gain_copy(0).start()
        event(8 + 2 * m)

    gsum = outa
    gsum[...] = dot_nt(big[:, 0:768], weight_of(0))
    gsum[...] += dot_nt(big[:, 768:1536], weight_of(1))
    gain_step(0)
    event(13)
    gsum[...] += dot_nt(big[:, 1536:2304], weight_of(2))
    igb = ni

    def norm1_back(i, _):
        rows = rows_of(i)
        standard, inverse = norm_rows(xp[rows].astype(f32))
        igb[rows] = (gna[rows] + norm_rows_back(gsum[rows], standard, inverse, ln1)).astype(bf16)
        return 0

    def unpermute(src, dst, out, sem):
        for i, (first, n, ranges) in enumerate(TILES_OUT):
            rows = slice(first, first + n)
            dst[rows] = picked(pick(first, n, ranges, out_of_order), ranges, src).astype(bf16)
            send_out(
                functools.partial(
                    pltpu.make_async_copy,
                    dst.at[pl.ds(first, n)],
                    out.at[pl.ds(first, n)],
                    sem.at[i],
                )
            )

    lax.fori_loop(0, 2, norm1_back, 0)
    gain_step(1)
    event(14)
    lax.fori_loop(2, 4, norm1_back, 0)
    unpermute(igb, cotv, inp_out, osem.at[1])
    gain_step(2)
    event(15)
    unpermute(lob, tokv, lay_out, osem.at[0])
    gain_step(3)
    event(16)
    gain_step(4)
    send_out(functools.partial(pltpu.make_async_copy, gains_sum, gains_out, osem.at[14, 0]))
    event(17)
    for copy in copies:
        copy().wait()


def hand_on(*refs):
    n = 6
    ins, gains_in = refs[:n], refs[n]
    outs, gain_outs = refs[n + 1 : 2 * n + 1], refs[2 * n + 1 : 2 * n + 5]
    held, gains, lines, sems = refs[2 * n + 5 : 3 * n + 5], refs[-6], refs[-5:-1], refs[-1]
    gains_come = pltpu.make_async_copy(gains_in, gains, sems.at[4 * n])
    gains_come.start()
    copies = []
    for i, (src, dst) in enumerate(zip(ins, outs)):
        parts = 4 if src.shape[0] == LENGTH else 1
        size = src.shape[0] // parts
        for part in range(parts):
            rows = pl.ds(part * size, size)
            sem = sems.at[4 * i + part]
            copies.append(
                (
                    pltpu.make_async_copy(src.at[rows], held[i].at[rows], sem),
                    pltpu.make_async_copy(held[i].at[rows], dst.at[rows], sem),
                )
            )
    for come, _go in copies:
        come.start()
    gains_come.wait()
    ln1, ln2, qg, kg = lines
    for i in range(6):
        ln1[pl.ds(128 * i, 128)] = gains[i, :]
        ln2[pl.ds(128 * i, 128)] = gains[6 + i, :]
    qg[...] = gains[12, 0:HD] + gains[12, HD : 2 * HD]
    kg[...] = gains[13, 0:HD] + gains[13, HD : 2 * HD]
    gains_go = [
        pltpu.make_async_copy(src, dst, sems.at[4 * n + 1 + i])
        for i, (src, dst) in enumerate(zip(lines, gain_outs))
    ]
    for go in gains_go:
        go.start()
    for come, go in copies:
        come.wait()
        go.start()
    for go in gains_go:
        go.wait()
    for _come, go in copies:
        go.wait()


def local(
    tokens, segment, ln1_gain, w_qkv, q_gain, k_gain, w_out, ln2_gain, w_up, w_down, cotangent
):
    groups = lax.axis_size("dp")
    dp_low = groups // (1 << BITS)
    rows = D >> BITS
    hbm = pl.BlockSpec(memory_space=pl.ANY)
    shape = jax.ShapeDtypeStruct
    half_ff = w_up.shape[1]
    ff, wide, n_proj = FF_CHUNKS, 2 * FW, CHUNKS - FF_CHUNKS

    def mem(*dims, dtype=bf16):
        return pltpu.VMEM(dims, dtype)

    outs = pl.pallas_call(
        functools.partial(kernel, dp_low),
        out_shape=(
            shape((LENGTH, D), bf16),
            shape((LENGTH, D), bf16),
            shape((rows, half_ff), f32),
            shape((rows, half_ff), f32),
            shape((rows, 384), f32),
            shape((3, rows, 384), f32),
            shape((16, 128), f32),
            shape((D, half_ff), bf16),
            shape((half_ff, D), bf16),
        ),
        in_specs=[hbm] * 11,
        out_specs=(hbm,) * 9,
        scratch_shapes=[
            pltpu.SMEM(segment.shape, jnp.int32),
            mem(D, dtype=f32),
            mem(D, dtype=f32),
            mem(HD, dtype=f32),
            mem(HD, dtype=f32),
            mem(LENGTH, D),
            mem(LENGTH, D),
            mem(LENGTH, D),
            mem(LENGTH, D),
            mem(LENGTH, D),
            mem(PAIRS, PADDED, 128),
            mem(PAIRS, PADDED, 128),
            mem(PAIRS, PADDED, 128),
            mem(PAIRS, LENGTH, 128),
            mem(PAIRS, LENGTH, 128),
            mem(PADDED, 128),
            mem(PADDED, 128),
            mem(LENGTH, D, dtype=f32),
            mem(LENGTH, D, dtype=f32),
            mem(LENGTH, D, dtype=f32),
            mem(LENGTH, 3 * D),
            mem(2, D, wide),
            mem(PADDED, D),
            mem(2, 3, D, 384),
            mem(D, D),
            mem(2, 16, rows, wide),
            mem(2, 16, rows, wide),
            mem(ff, 16, rows, wide),
            mem(ff, 8, rows, wide),
            mem(ff, 4, rows, wide),
            mem(ff, 2, rows, wide),
            mem(ff, 1, rows, wide),
            mem(n_proj, 16, rows, 384),
            mem(n_proj, 8, rows, 384),
            mem(n_proj, 4, rows, 384),
            mem(n_proj, 2, rows, 384),
            mem(n_proj, 1, rows, 384),
            mem(5, 16, 128, dtype=f32),
            mem(5, 16, 128, dtype=f32),
            mem(16, 128, dtype=f32),
            pltpu.SemaphoreType.DMA((CHUNKS, 5)),
            pltpu.SemaphoreType.DMA((CHUNKS, 5)),
            pltpu.SemaphoreType.DMA((5,)),
            pltpu.SemaphoreType.DMA((5,)),
            pltpu.SemaphoreType.DMA((4,)),
            pltpu.SemaphoreType.DMA((4,)),
            pltpu.SemaphoreType.DMA((7,)),
            pltpu.SemaphoreType.DMA((8,)),
            pltpu.SemaphoreType.DMA((2, 4)),
            pltpu.SemaphoreType.DMA((15, 4)),
        ],
        compiler_params=pltpu.CompilerParams(
            collective_id=0, has_side_effects=True, vmem_limit_bytes=255 * 2**18
        ),
        name="layer",
    )(
        segment,
        tokens,
        cotangent,
        ln1_gain,
        ln2_gain,
        q_gain,
        k_gain,
        jnp.transpose(w_qkv, (1, 0, 2)),
        w_out,
        w_up,
        w_down,
    )
    results, gains = list(outs[:6]), outs[6]
    if dp_low > 1:
        peers = [[hi * dp_low + lo for lo in range(dp_low)] for hi in range(1 << BITS)]

        def rest(x, axis):
            return lax.psum_scatter(
                x, "dp", scatter_dimension=axis, axis_index_groups=peers, tiled=True
            )

        results[2:] = [rest(x, x.ndim - 2) for x in results[2:]]
        gains = lax.psum(gains, "dp", axis_index_groups=peers)
    (
        layer_out,
        input_grad,
        up_grad,
        down_grad,
        proj_grad,
        qkv_grad,
        ln1_grad,
        ln2_grad,
        q_grad,
        k_grad,
    ) = pl.pallas_call(
        hand_on,
        out_shape=[shape(x.shape, x.dtype) for x in results]
        + [shape((D,), f32)] * 2
        + [shape((HD,), f32)] * 2,
        in_specs=[pl.BlockSpec(memory_space=pltpu.HBM)] * 7,
        out_specs=[pl.BlockSpec(memory_space=pltpu.HBM)] * 10,
        scratch_shapes=[pltpu.VMEM(x.shape, x.dtype) for x in results + [gains]]
        + [mem(D, dtype=f32)] * 2
        + [mem(HD, dtype=f32)] * 2
        + [pltpu.SemaphoreType.DMA((29,))],
        name="hand_on",
    )(*results, gains)
    return (
        layer_out,
        input_grad,
        ln1_grad,
        jnp.transpose(qkv_grad, (1, 0, 2)),
        q_grad,
        k_grad,
        proj_grad.T,
        ln2_grad,
        up_grad,
        down_grad.T,
    )


def solution(mesh):
    return jax.shard_map(
        local,
        mesh=mesh,
        in_specs=(
            P(("dp", "tensor"), None),
            P("dp"),
            P(),
            P(None, None, "tensor"),
            P(),
            P(),
            P("tensor", None),
            P(),
            P(None, "tensor"),
            P("tensor", None),
            P(("dp", "tensor"), None),
        ),
        out_specs=(
            P(("dp", "tensor"), None),
            P(("dp", "tensor"), None),
            P(),
            P("dp", None, "tensor"),
            P(),
            P(),
            P("tensor", "dp"),
            P(),
            P("dp", "tensor"),
            P("tensor", "dp"),
        ),
        check_vma=False,
    )
```

```python
import functools

import jax
import jax.numpy as jnp
from jax import lax
from jax.experimental import pallas as pl
from jax.experimental.pallas import tpu as pltpu
from jax.sharding import PartitionSpec as P

D = 768
HD = 64
LENGTH = 1024
PATCHES = 196
IMAGES = 5
PADDING = LENGTH - IMAGES * PATCHES
PADDED = 1040
PAIRS = 6
EPS = 1e-06
MESH = pl.DeviceIdType.MESH
f32, bf16 = jnp.float32, jnp.bfloat16

WINDOWS = [
    (PATCHES * i // 16 * 16, 208, PATCHES * i, PATCHES * (i + 1)) for i in range(IMAGES)
] + [(976, 48, 980, 1024)]

FF_CHUNKS = 6
FW = 256
BITS = 4

CHUNKS = 12
START = [0, 1, 2, 3, 4, 5, 6, 8, 10, 12, 12, 12]
FF_LAG = (1, 3, 6, 8, 11)
LAG = [FF_LAG] * FF_CHUNKS + [(1, 3, 5, 7, 10), (1, 3, 5, 7, 8), (1, 3, 4, 5, 7)] + [(1, 2, 3, 4, 5)] * 3

LAST_BITS = {}

TILES_IN = [
    (0, 256, [(0, 384)]),
    (256, 256, [(256, 384)]),
    (512, 256, [(512, 384)]),
    (768, 128, [(768, 256)]),
    (896, 128, [(0, 1024)]),
]
TILES_OUT = [
    (0, 256, [(0, 256), (896, 128)]),
    (256, 256, [(128, 384), (896, 128)]),
    (512, 256, [(384, 384), (896, 128)]),
    (768, 256, [(640, 384)]),
]


def dot(left, right):
    return jnp.dot(left, right, preferred_element_type=f32)


def dot_nt(left, right):
    return lax.dot_general(left, right, (((1,), (1,)), ((), ())), preferred_element_type=f32)


def dot_tn(left, right):
    return lax.dot_general(left, right, (((0,), (0,)), ((), ())), preferred_element_type=f32)


def gelu_and_slope(h):
    e = jnp.exp(h * h * -0.5)
    t = 1.0 / (1.0 + jnp.abs(h) * (0.3275911 * 0.7071067811865476))
    poly = t * (
        0.5 * 0.254829592
        + t
        * (
            0.5 * -0.284496736
            + t * (0.5 * 1.421413741 + t * (0.5 * -1.453152027 + t * (0.5 * 1.061405429)))
        )
    )
    tail = poly * e
    phi = jnp.where(h >= 0, 1.0 - tail, tail)
    return h * phi, phi + h * e * 0.3989422804014327


def split(x):
    high = x.astype(bf16)
    return high, (x - high.astype(f32)).astype(bf16)


def iota(shape, axis):
    return lax.broadcasted_iota(jnp.int32, shape, axis)


def norm_rows(x):
    centred = x - jnp.mean(x, axis=-1, keepdims=True)
    inverse = lax.rsqrt(jnp.mean(centred * centred, axis=-1, keepdims=True) + EPS)
    return centred * inverse, inverse


def norm_rows_back(grad, standard, inverse, gain):
    c = grad * gain
    return inverse * (
        c
        - jnp.mean(c, axis=-1, keepdims=True)
        - standard * jnp.mean(c * standard, axis=-1, keepdims=True)
    )


def swap(pos):
    return (pos & 4) | (pos & 1) | ((pos & 8) >> 2) | ((pos & 2) << 2)


def kernel(
    dp_low,
    seg_hbm,
    tok,
    cot,
    ln1_hbm,
    ln2_hbm,
    qgain_hbm,
    kgain_hbm,
    wqkv,
    wout,
    wup,
    wdn,
    lay_out,
    inp_out,
    up_out,
    dn_out,
    pr_out,
    qk_out,
    gains_out,
    wup_x,
    wdn_x,
    seg,
    ln1v,
    ln2v,
    qgv,
    kgv,
    tokv,
    cotv,
    xp,
    cp,
    ni,
    q,
    k,
    v,
    invq,
    invk,
    nlg,
    dlt,
    mid,
    outa,
    gna,
    big,
    wus,
    wds,
    wq,
    wo,
    sbuf,
    r0,
    af,
    r1f,
    r2f,
    r3f,
    r4f,
    ap,
    r1p,
    r2p,
    r3p,
    r4p,
    gsend,
    grecv,
    gains_sum,
    ssem,
    rsem,
    gssem,
    grsem,
    wssem,
    wrsem,
    lsem,
    rsem0,
    fsem,
    osem,
):
    att = tokv
    gb = cotv
    lse = mid.at[:, pl.ds(0, 128)]
    do = wds
    g = lax.axis_index("dp")
    t = lax.axis_index("tensor")
    top, low = g // dp_low, g % dp_low
    mine = [(top // (1 << b)) % 2 for b in range(BITS)]

    def peer(b):
        return ((top + (1 - 2 * mine[b]) * (1 << b)) * dp_low + low, t)

    d0, d1 = peer(0)[0], peer(1)[0]
    core = (g, 1 - t)
    first = (jnp.where(t == 0, d0, d1), t)
    third = (jnp.where(t == 0, d1, d0), t)
    partners = (core, first, peer(2), third, peer(3))

    def place(b):
        rel = [mine[i] if (b >> i) & 1 == 0 else 1 - mine[i] for i in range(BITS)]
        one = rel[0] * 8 + rel[1] * 2
        two = rel[1] * 8 + rel[0] * 2
        return one + t * (two - one) + rel[2] * 4 + rel[3]

    places = [place(b) for b in range(16)]

    def last_place(c, b):
        rel = [mine[i] if (b >> i) & 1 == 0 else 1 - mine[i] for i in LAST_BITS[c]]
        return rel[0] * 8 + rel[1] * 4 + rel[2] * 2 + rel[3]

    def partner_of(stage, c, is_ff):
        if stage > 0 and not is_ff and c in LAST_BITS:
            return peer(LAST_BITS[c][stage - 1])
        return partners[stage]

    barrier = pltpu.get_barrier_semaphore()
    for partner in partners:
        pl.semaphore_signal(barrier, inc=1, device_id=partner, device_id_type=MESH)

    loads = [
        pltpu.make_async_copy(wqkv, wq.at[0], lsem.at[0]),
        pltpu.make_async_copy(wout, wo.at[pl.ds(0, 384)], lsem.at[1]),
        pltpu.make_async_copy(seg_hbm, seg, lsem.at[2]),
        pltpu.make_async_copy(ln1_hbm, ln1v, lsem.at[3]),
        pltpu.make_async_copy(ln2_hbm, ln2v, lsem.at[4]),
        pltpu.make_async_copy(qgain_hbm, qgv, lsem.at[5]),
        pltpu.make_async_copy(kgain_hbm, kgv, lsem.at[6]),
    ]
    row_loads = []
    for i in range(4):
        rows = pl.ds(256 * i, 256)
        row_loads.append(pltpu.make_async_copy(tok.at[rows], tokv.at[rows], rsem0.at[i]))
        row_loads.append(pltpu.make_async_copy(cot.at[rows], cotv.at[rows], rsem0.at[4 + i]))
    for c in loads[2:] + row_loads + loads[:2]:
        c.start()

    def weight_copy(i, src, dst):
        return pltpu.make_async_remote_copy(
            src_ref=src,
            dst_ref=dst,
            send_sem=wssem.at[i],
            recv_sem=wrsem.at[i],
            device_id=core,
            device_id_type=MESH,
        )

    weights = [
        weight_copy(0, wqkv, wq.at[1]),
        weight_copy(1, wout, wo.at[pl.ds(384, 384)]),
        weight_copy(2, wup, wup_x),
        weight_copy(3, wdn, wdn_x),
    ]

    def chunk_refs(c, is_ff):
        if is_ff:
            slot = lax.rem(c, 2)
            return sbuf.at[slot], r0.at[slot], af.at[c], [r.at[c] for r in (r1f, r2f, r3f, r4f)]
        n = min(c, 9) - FF_CHUNKS
        lanes = pl.ds(128 * (c - 9), 128) if c >= 9 else pl.ds(0, 384)
        slot = min(c, 9) % 2
        return (
            sbuf.at[slot, :, :, lanes],
            r0.at[slot, :, :, lanes],
            ap.at[n, :, :, lanes],
            [r.at[n, :, :, lanes] for r in (r1p, r2p, r3p, r4p)],
        )

    def rs_copy(stage, c, is_ff):
        src, dst, a, rs = chunk_refs(c, is_ff)
        if stage > 0:
            half = 16 >> stage
            src, dst = a.at[pl.ds(half, half)], rs[stage - 1]
        return pltpu.make_async_remote_copy(
            src_ref=src,
            dst_ref=dst,
            send_sem=ssem.at[c, stage],
            recv_sem=rsem.at[c, stage],
            device_id=partner_of(stage, c, is_ff),
            device_id_type=MESH,
        )

    copies = []

    def send_out(copy):
        copies.append(copy)
        copy().start()

    def finish(c, total):
        mid[48 * c : 48 * c + 48, 0 : total.shape[1]] = total

        def part(first, width, out, place, i):
            def copy():
                src = mid.at[pl.ds(48 * c, 48), pl.ds(first, width)]
                return pltpu.make_async_copy(src, out.at[place], osem.at[2 + c, i])

            send_out(copy)

        every = slice(None)
        if c < FF_CHUNKS:
            part(0, FW, up_out, (every, pl.ds(c * FW, FW)), 0)
            part(FW, FW, dn_out, (every, pl.ds(c * FW, FW)), 1)
        elif c == FF_CHUNKS:
            part(0, 384, pr_out, (every, every), 0)
        elif c < 9:
            for i in range(3):
                m = c - FF_CHUNKS - 1
                part(128 * i, 128, qk_out, (i, every, pl.ds(128 * m, 128)), i)
        else:
            part(0, 128, qk_out, (c - 9, every, pl.ds(256, 128)), 0)

    def advance(stage, c, is_ff):
        _src, arrived, a, rs = chunk_refs(c, is_ff)
        rs_copy(stage, c, is_ff).wait()
        if stage == 0:
            for pos in range(16):
                same_way = not is_ff and c in LAST_BITS
                a[pos] = a[pos] + arrived[pos if same_way else swap(pos)]
        elif stage < 4:
            half = 16 >> stage
            for pos in range(half):
                a[pos] = a[pos] + rs[stage - 1][pos]
        else:
            finish(c, a[0].astype(f32) + rs[3][0].astype(f32))
        if stage < 4:
            rs_copy(stage + 1, c, is_ff).start()

    def event(e):
        for stage in range(4, -1, -1):
            for c in range(CHUNKS):
                if START[c] + LAG[c][stage] == e:
                    advance(stage, c, c < FF_CHUNKS)
        for c in range(CHUNKS):
            if START[c] == e:
                rs_copy(0, c, c < FF_CHUNKS).start()

    for c in loads[2:]:
        c.wait()
    s = jnp.int32(0)
    for image in range(IMAGES + 1):
        s = s + jnp.where(seg[t * LENGTH + PATCHES * image] == -1, image, 0)
    ln1 = ln1v[...].reshape(1, D)
    ln2 = ln2v[...].reshape(1, D)
    qg = qgv[...].reshape(1, HD)
    qg = jnp.concatenate([qg, qg], axis=1)
    kg = kgv[...].reshape(1, HD)
    kg = jnp.concatenate([kg, kg], axis=1)
    zero_rows = jnp.zeros((PADDED - LENGTH, 128), bf16)
    for pp in range(PAIRS):
        for ref in (q, k, v):
            ref[pp, LENGTH:, :] = zero_rows
    do[LENGTH:, :] = jnp.zeros((PADDED - LENGTH, D), bf16)
    nlg[LENGTH:, :] = zero_rows
    dlt[LENGTH:, :] = zero_rows

    def rows_of(i):
        return pl.ds(pl.multiple_of(i * 256, 256), 256)

    def pick(first, rows, ranges, source):
        wanted = source(iota((rows, 1), 0) + first)
        parts = [iota((rows, n), 1) + start == wanted for start, n in ranges]
        return jnp.concatenate([p.astype(f32).astype(bf16) for p in parts], axis=1)

    def picked(matrix, ranges, ref):
        return dot(matrix, jnp.concatenate([ref[start : start + n] for start, n in ranges], axis=0))

    def in_order(r):
        image_row = r + jnp.where(r >= PATCHES * s, PADDING, 0)
        return jnp.where(r < IMAGES * PATCHES, image_row, PATCHES * s + r - IMAGES * PATCHES)

    def out_of_order(r):
        behind = jnp.where(
            r < PATCHES * s + PADDING, r - PATCHES * s + IMAGES * PATCHES, r - PADDING
        )
        return jnp.where(r < PATCHES * s, r, behind)

    def permute(first, n, ranges):
        rows = slice(first, first + n)
        matrix = pick(first, n, ranges, in_order)
        x = picked(matrix, ranges, tokv)
        xp[rows] = x.astype(bf16)
        standard, _unused = norm_rows(x)
        ni[rows] = (standard * ln1).astype(bf16)
        cp[rows] = picked(matrix, ranges, cotv).astype(bf16)

    for c in row_loads[:4]:
        c.wait()
    permute(*TILES_IN[0])
    for c in row_loads[4:6]:
        c.wait()
    permute(*TILES_IN[1])
    pl.semaphore_wait(barrier, len(partners))
    for c in weights:
        c.start()
    for c in row_loads[6:]:
        c.wait()
    for tile in TILES_IN[2:]:
        permute(*tile)

    def lane_means(x):
        out = []
        for first in range(0, x.shape[1], 128):
            part = x[:, first : first + 128]
            low = iota(part.shape, 1) < HD
            low_sum = jnp.sum(jnp.where(low, part, 0.0), axis=1, keepdims=True)
            high_sum = jnp.sum(part, axis=1, keepdims=True) - low_sum
            out.append(jnp.where(low, low_sum, high_sum) * (1.0 / HD))
        return jnp.concatenate(out, axis=1)

    block = (iota((256, 256), 0) // HD == iota((256, 256), 1) // HD).astype(f32) * (1.0 / HD)
    block = block.astype(bf16)

    def head_norm(y, pair_of, by_lanes):
        if by_lanes:
            centred = y - lane_means(y)
            spread = lane_means(centred * centred)
        else:
            high, rest = split(y)
            centred = y - (dot(high, block) + dot(rest, block))
            spread = dot((centred * centred).astype(bf16), block)
        inverse = lax.rsqrt(spread + EPS)
        standard = centred * inverse
        for half in range(2):
            lanes = slice(128 * half, 128 * half + 128)
            dest, inv_dest, dest_gain, pp = pair_of(half)
            dest[pp, 0:LENGTH, :] = (standard[:, lanes] * dest_gain).astype(bf16)
            inv_dest[pp] = inverse[:, lanes].astype(bf16)

    def project(p):
        for tile in range(3):
            parts = []
            for half in range(2):
                idx = 2 * tile + half
                part, m = idx // 3, idx % 3
                parts.append(wq[p, part, :, 128 * m : 128 * m + 128])
            y = dot(ni[...], jnp.concatenate(parts, axis=1))

            def pair_of(half, tile=tile):
                idx = 2 * tile + half
                pp = p * 3 + idx % 3
                if idx < 3:
                    return q, invq, qg * 0.125, pp
                return k, invk, kg, pp

            head_norm(y, pair_of, tile != 1)
        y = dot(ni[...], wq[p, 2]).astype(bf16)
        for m in range(3):
            v[p * 3 + m, 0:LENGTH, :] = y[:, 128 * m : 128 * m + 128]

    loads[0].wait()
    project(0)
    weights[0].wait()
    project(1)

    def low_lanes(rows):
        return iota((rows, 128), 1) < HD

    def two_heads(x, rows):
        low = low_lanes(rows)
        zero = jnp.zeros_like(x)
        return jnp.concatenate([jnp.where(low, x, zero), jnp.where(low, zero, x)], axis=0)

    def place_rows(ref, cols, new, start, begin):
        rows = new.shape[0]
        if begin > start:
            top = slice(start, start + 16)
            keep = iota((16, 128), 0) + start < begin
            ref[top, cols] = jnp.where(keep, ref[top, cols], new[:16])
            ref[start + 16 : start + rows, cols] = new[16:]
        else:
            ref[start : start + rows, cols] = new

    def attend(pp, _):
        cols = pl.ds(pl.multiple_of(pp * 128, 128), 128)
        for start, rows, begin, end in WINDOWS:
            window = slice(start, start + rows)
            krows = 256 if rows > 48 else 48
            kwin = slice(start, start + krows)
            scores = dot_nt(two_heads(q[pp, window, :], rows), k[pp, kwin, :])
            weight = jnp.exp(scores).astype(bf16)
            kr = iota((krows, 256), 0) + start
            vone = jnp.concatenate([v[pp, kwin, :], jnp.ones((krows, 128), bf16)], axis=1)
            vone = jnp.where((kr >= begin) & (kr < end), vone, jnp.zeros_like(vone))
            both = dot(weight, vone)
            total = both[:, 128:]
            heads = both[:, :128] / total
            merged = jnp.where(low_lanes(rows), heads[:rows], heads[rows:]).astype(bf16)
            place_rows(att, cols, merged, start, begin)
            lane = iota((rows, 128), 1) // 2
            sums = lse[window, :]
            sums = jnp.where(lane == 2 * pp, total[:rows], sums)
            sums = jnp.where(lane == 2 * pp + 1, total[rows:], sums)
            place_rows(lse, slice(None), sums, start, begin)
        return 0

    lse[...] = jnp.ones_like(lse)
    lax.fori_loop(0, PAIRS, attend, 0)
    even = iota((LENGTH, 128), 1) % 2 == 0
    high, rest = split(-jnp.log(lse[...]))
    nlg[0:LENGTH, :] = jnp.where(even, high, rest)

    loads[1].wait()
    weights[1].wait()
    nm = big.at[:, pl.ds(1024, D)]
    act = big.at[:, pl.ds(0, 2 * FW)]
    gh = big.at[:, pl.ds(512, 2 * FW)]

    def middle(i, _):
        rows = rows_of(i)
        m = xp[rows].astype(f32) + dot(att[rows], wo[...])
        mid[rows] = m
        outa[rows] = m
        standard, _unused = norm_rows(m)
        nm[rows] = (standard * ln2).astype(bf16)
        return 0

    lax.fori_loop(0, 4, middle, 0)

    def down_rows(i):
        return wds.at[pl.ds(pl.multiple_of(i * FW, FW), FW)]

    def ff_loads(j, slot):
        cols = pl.ds(pl.multiple_of(j * FW, FW), FW)
        return [
            pltpu.make_async_copy(wup.at[:, cols], wus.at[slot, :, pl.ds(0, FW)], fsem.at[slot, 0]),
            pltpu.make_async_copy(
                wup_x.at[:, cols], wus.at[slot, :, pl.ds(FW, FW)], fsem.at[slot, 1]
            ),
            pltpu.make_async_copy(wdn.at[cols], down_rows(2 * slot), fsem.at[slot, 2]),
            pltpu.make_async_copy(wdn_x.at[cols], down_rows(2 * slot + 1), fsem.at[slot, 3]),
        ]

    weights[2].wait()
    weights[3].wait()
    for c in ff_loads(0, 0):
        c.start()
    gna[...] = jnp.zeros_like(gna)

    def feed_event(j):
        for stage in range(5):
            lag = FF_LAG[stage]
            if lag < FF_CHUNKS:

                @pl.when(j >= lag)
                def _(stage=stage, lag=lag):
                    advance(stage, j - lag, True)
            if stage == 0:
                rs_copy(0, j, True).start()

    def feed(j, _):
        slot = lax.rem(j, 2)
        for c in ff_loads(j, slot):
            c.wait()

        @pl.when(j < FF_CHUNKS - 1)
        def _():
            for c in ff_loads(j + 1, 1 - slot):
                c.start()

        wu = wus[slot]
        wd = wds[pl.ds(pl.multiple_of(slot * 2 * FW, 2 * FW), 2 * FW), :]
        for r in range(0, LENGTH, 256):
            rows = slice(r, r + 256)
            a, slope = gelu_and_slope(dot(nm[rows], wu))
            act[rows] = a.astype(bf16)
            gh[rows] = (dot_nt(cp[rows], wd) * slope).astype(bf16)
        outa[...] += dot(act[...], wd)
        gna[...] += dot_nt(gh[...], wu)
        up = dot_tn(nm[...], gh[...]).astype(bf16)
        dn = dot_tn(cp[...], act[...]).astype(bf16)
        for b in range(16):
            part = slice(48 * b, 48 * b + 48)
            af[j, places[b], :, 0:FW] = up[part, :FW]
            af[j, places[b], :, FW : 2 * FW] = dn[part, :FW]
            sbuf[slot, places[b], :, 0:FW] = up[part, FW:]
            sbuf[slot, places[b], :, FW : 2 * FW] = dn[part, FW:]
        feed_event(j)
        return 0

    lax.fori_loop(0, FF_CHUNKS, feed, 0)

    lob = cp

    def norm2_back(i, total):
        rows = rows_of(i)
        m = mid[rows]
        standard, inverse = norm_rows(m)
        grad = gna[rows]
        grad_mid = cp[rows].astype(f32) + norm_rows_back(grad, standard, inverse, ln2)
        gna[rows] = grad_mid
        gb[rows] = grad_mid.astype(bf16)
        lob[rows] = outa[rows].astype(bf16)
        return total + jnp.sum(grad * standard, axis=0, keepdims=True)

    ln2_terms = lax.fori_loop(0, 4, norm2_back, jnp.zeros((1, D), f32))

    def put(c, slot, own, other):
        for b in range(16):
            part = slice(48 * b, 48 * b + 48)
            ap[c - FF_CHUNKS, places[b]] = own[part]
            sbuf[slot, places[b], :, 0:384] = other[part]

    pg = dot_tn(gb[...], att[...]).astype(bf16)
    put(FF_CHUNKS, 0, pg[:, :384], pg[:, 384:])
    event(6)

    ga = dot_nt(gb[...], wo[...])
    gab = ga.astype(bf16)
    do[0:LENGTH, :] = gab
    high, rest = split(gab.astype(f32) * att[...].astype(f32))
    gather = (iota((D, 128), 0) // HD == iota((D, 128), 1) // 2).astype(f32).astype(bf16)
    delta = dot(high, gather) + dot(rest, gather)
    high, rest = split(delta)
    dlt[0:LENGTH, :] = jnp.where(even, high, rest)

    block2 = (iota((256, 128), 0) % 128 // HD == iota((256, 128), 1) // HD).astype(f32) * (1.0 / HD)
    block2 = block2.astype(bf16)

    def head_mean(x):
        return dot(jnp.concatenate(split(x), axis=1), block2)

    def head_norm_back(grad, standard, inverse, gain, means):
        c = grad * gain
        return inverse * (c - means(c) - standard * means(c * standard))

    dq, dk, dv = (outa.at[:, pl.ds(128 * i, 128)] for i in range(3))

    def attend_back(pp, col):
        for start, rows, begin, end in WINDOWS:
            window = slice(start, start + rows)
            qrows = 256 if rows > 48 else 48
            qwin = slice(start, start + qrows)
            lane = iota((2 * rows, 128), 1)
            head = 2 * pp + jnp.where(iota((2 * rows, 128), 0) < rows, 0, 1)
            hot = (lane // 2 == head).astype(f32).astype(bf16)
            kb = k[pp, window, :]
            qb = q[pp, qwin, :]
            st = dot_nt(
                jnp.concatenate([two_heads(kb, rows), hot], axis=1),
                jnp.concatenate([qb, nlg[qwin, :]], axis=1),
            )
            pt = jnp.exp(st)
            qr = iota((qrows, 128), 0) + start
            valid = (qr >= begin) & (qr < end)
            dob = do[qwin, pl.ds(pl.multiple_of(pp * 128, 128), 128)]
            zero = jnp.zeros_like(dob)
            dob = jnp.where(valid, dob, zero)
            dpt = dot_nt(
                jnp.concatenate([two_heads(v[pp, window, :], rows), -hot], axis=1),
                jnp.concatenate([dob, jnp.where(valid, dlt[qwin, :], zero)], axis=1),
            )
            dst = (pt * dpt).astype(bf16)
            dv2 = dot(pt.astype(bf16), dob)
            dk2 = dot(dst, qb)
            kr = iota((rows, 128), 0) + start
            kz = jnp.where((kr >= begin) & (kr < end), kb, jnp.zeros_like(kb))
            dq2 = dot_tn(dst, two_heads(kz, rows))[:rows]
            low = low_lanes(rows)
            every = slice(None)
            place_rows(dv, every, jnp.where(low, dv2[:rows], dv2[rows:]), start, begin)
            place_rows(dk, every, jnp.where(low, dk2[:rows], dk2[rows:]), start, begin)
            place_rows(dq, every, dq2, start, begin)
        standard = q[pp, 0:LENGTH, :].astype(f32) * (8.0 / qg)
        grad = dq[...] * 0.125
        q_terms = jnp.sum(grad * standard, axis=0, keepdims=True)
        big[:, col(0)] = head_norm_back(grad, standard, invq[pp].astype(f32), qg, head_mean).astype(bf16)
        standard = k[pp, 0:LENGTH, :].astype(f32) * (1.0 / kg)
        grad = dk[...]
        k_terms = jnp.sum(grad * standard, axis=0, keepdims=True)
        big[:, col(1)] = head_norm_back(grad, standard, invk[pp].astype(f32), kg, head_mean).astype(bf16)
        big[:, col(2)] = dv[...].astype(bf16)
        return q_terms, k_terms

    def weight_of(m):
        return jnp.concatenate(
            [wq[p, part, :, 128 * m : 128 * m + 128] for p in range(2) for part in range(3)], axis=1
        )

    def gain_copy(i):
        return pltpu.make_async_remote_copy(
            src_ref=gsend.at[i],
            dst_ref=grecv.at[i],
            send_sem=gssem.at[i],
            recv_sem=grsem.at[i],
            device_id=partners[i],
            device_id_type=MESH,
        )

    def gain_step(i):
        gain_copy(i).wait()
        total = gsend[i] + grecv[i]
        if i < 4:
            gsend[i + 1] = total
            gain_copy(i + 1).start()
        else:
            gains_sum[...] = total

    ln1_sum = jnp.zeros((D, 128), f32)
    q_terms = jnp.zeros((1, 128), f32)
    k_terms = jnp.zeros((1, 128), f32)
    for m in range(3):

        def pair(i, carry, m=m):
            def col(part):
                return pl.ds(pl.multiple_of(768 * m + 384 * i + 128 * part, 128), 128)

            a, b = attend_back(3 * i + m, col)

            @pl.when(i == 0)
            def _():
                event(7 + 2 * m)

            return carry[0] + a, carry[1] + b

        q_terms, k_terms = lax.fori_loop(0, 2, pair, (q_terms, k_terms))
        both = dot_tn(ni[...], big[:, 768 * m : 768 * m + 768])
        wide = both * weight_of(m).astype(f32)
        for tile in range(6):
            ln1_sum = ln1_sum + wide[:, 128 * tile : 128 * tile + 128]
        both = both.astype(bf16)
        c = FF_CHUNKS + 1 + m
        put(c, c % 2, both[:, :384], both[:, 384:])
        if m == 2:
            high, rest = split(ln1_sum)
            ones = jnp.ones((16, 128), bf16)
            ln1_terms = (dot_nt(ones, high) + dot_nt(ones, rest))[0:1] / ln1
            gsend[0] = jnp.concatenate(
                [ln1_terms[:, 128 * i : 128 * i + 128] for i in range(6)]
                + [ln2_terms[:, 128 * i : 128 * i + 128] for i in range(6)]
                + [q_terms, k_terms, jnp.zeros((2, 128), f32)],
                axis=0,
            )
            gain_copy(0).start()
        event(8 + 2 * m)

    gsum = outa
    gsum[...] = dot_nt(big[:, 0:768], weight_of(0))
    gsum[...] += dot_nt(big[:, 768:1536], weight_of(1))
    gain_step(0)
    event(13)
    gsum[...] += dot_nt(big[:, 1536:2304], weight_of(2))
    igb = ni

    def norm1_back(i, _):
        rows = rows_of(i)
        standard, inverse = norm_rows(xp[rows].astype(f32))
        igb[rows] = (gna[rows] + norm_rows_back(gsum[rows], standard, inverse, ln1)).astype(bf16)
        return 0

    def unpermute(src, dst, out, sem):
        for i, (first, n, ranges) in enumerate(TILES_OUT):
            rows = slice(first, first + n)
            dst[rows] = picked(pick(first, n, ranges, out_of_order), ranges, src).astype(bf16)
            send_out(
                functools.partial(
                    pltpu.make_async_copy,
                    dst.at[pl.ds(first, n)],
                    out.at[pl.ds(first, n)],
                    sem.at[i],
                )
            )

    lax.fori_loop(0, 2, norm1_back, 0)
    gain_step(1)
    event(14)
    lax.fori_loop(2, 4, norm1_back, 0)
    unpermute(igb, cotv, inp_out, osem.at[1])
    gain_step(2)
    event(15)
    unpermute(lob, tokv, lay_out, osem.at[0])
    gain_step(3)
    event(16)
    gain_step(4)
    send_out(functools.partial(pltpu.make_async_copy, gains_sum, gains_out, osem.at[14, 0]))
    event(17)
    for copy in copies:
        copy().wait()


def hand_on(*refs):
    n = 6
    ins, gains_in = refs[:n], refs[n]
    outs, gain_outs = refs[n + 1 : 2 * n + 1], refs[2 * n + 1 : 2 * n + 5]
    held, gains, lines, sems = refs[2 * n + 5 : 3 * n + 5], refs[-6], refs[-5:-1], refs[-1]
    gains_come = pltpu.make_async_copy(gains_in, gains, sems.at[8 * n])
    gains_come.start()
    copies = []
    for i, (src, dst) in enumerate(zip(ins, outs)):
        parts = 8 if src.shape[0] == LENGTH else 1
        size = src.shape[0] // parts
        for part in range(parts):
            rows = pl.ds(part * size, size)
            sem = sems.at[8 * i + part]
            copies.append(
                (
                    pltpu.make_async_copy(src.at[rows], held[i].at[rows], sem),
                    pltpu.make_async_copy(held[i].at[rows], dst.at[rows], sem),
                )
            )
    for come, _go in copies:
        come.start()
    gains_come.wait()
    ln1, ln2, qg, kg = lines
    for i in range(6):
        ln1[pl.ds(128 * i, 128)] = gains[i, :]
        ln2[pl.ds(128 * i, 128)] = gains[6 + i, :]
    qg[...] = gains[12, 0:HD] + gains[12, HD : 2 * HD]
    kg[...] = gains[13, 0:HD] + gains[13, HD : 2 * HD]
    gains_go = [
        pltpu.make_async_copy(src, dst, sems.at[8 * n + 1 + i])
        for i, (src, dst) in enumerate(zip(lines, gain_outs))
    ]
    for go in gains_go:
        go.start()
    for come, go in copies:
        come.wait()
        go.start()
    for go in gains_go:
        go.wait()
    for _come, go in copies:
        go.wait()


def local(
    tokens, segment, ln1_gain, w_qkv, q_gain, k_gain, w_out, ln2_gain, w_up, w_down, cotangent
):
    groups = lax.axis_size("dp")
    dp_low = groups // (1 << BITS)
    rows = D >> BITS
    hbm = pl.BlockSpec(memory_space=pl.ANY)
    shape = jax.ShapeDtypeStruct
    half_ff = w_up.shape[1]
    ff, wide, n_proj = FF_CHUNKS, 2 * FW, CHUNKS - FF_CHUNKS

    def mem(*dims, dtype=bf16):
        return pltpu.VMEM(dims, dtype)

    outs = pl.pallas_call(
        functools.partial(kernel, dp_low),
        out_shape=(
            shape((LENGTH, D), bf16),
            shape((LENGTH, D), bf16),
            shape((rows, half_ff), f32),
            shape((rows, half_ff), f32),
            shape((rows, 384), f32),
            shape((3, rows, 384), f32),
            shape((16, 128), f32),
            shape((D, half_ff), bf16),
            shape((half_ff, D), bf16),
        ),
        in_specs=[hbm] * 11,
        out_specs=(hbm,) * 9,
        scratch_shapes=[
            pltpu.SMEM(segment.shape, jnp.int32),
            mem(D, dtype=f32),
            mem(D, dtype=f32),
            mem(HD, dtype=f32),
            mem(HD, dtype=f32),
            mem(LENGTH, D),
            mem(LENGTH, D),
            mem(LENGTH, D),
            mem(LENGTH, D),
            mem(LENGTH, D),
            mem(PAIRS, PADDED, 128),
            mem(PAIRS, PADDED, 128),
            mem(PAIRS, PADDED, 128),
            mem(PAIRS, LENGTH, 128),
            mem(PAIRS, LENGTH, 128),
            mem(PADDED, 128),
            mem(PADDED, 128),
            mem(LENGTH, D, dtype=f32),
            mem(LENGTH, D, dtype=f32),
            mem(LENGTH, D, dtype=f32),
            mem(LENGTH, 3 * D),
            mem(2, D, wide),
            mem(PADDED, D),
            mem(2, 3, D, 384),
            mem(D, D),
            mem(2, 16, rows, wide),
            mem(2, 16, rows, wide),
            mem(ff, 16, rows, wide),
            mem(ff, 8, rows, wide),
            mem(ff, 4, rows, wide),
            mem(ff, 2, rows, wide),
            mem(ff, 1, rows, wide),
            mem(n_proj, 16, rows, 384),
            mem(n_proj, 8, rows, 384),
            mem(n_proj, 4, rows, 384),
            mem(n_proj, 2, rows, 384),
            mem(n_proj, 1, rows, 384),
            mem(5, 16, 128, dtype=f32),
            mem(5, 16, 128, dtype=f32),
            mem(16, 128, dtype=f32),
            pltpu.SemaphoreType.DMA((CHUNKS, 5)),
            pltpu.SemaphoreType.DMA((CHUNKS, 5)),
            pltpu.SemaphoreType.DMA((5,)),
            pltpu.SemaphoreType.DMA((5,)),
            pltpu.SemaphoreType.DMA((4,)),
            pltpu.SemaphoreType.DMA((4,)),
            pltpu.SemaphoreType.DMA((7,)),
            pltpu.SemaphoreType.DMA((8,)),
            pltpu.SemaphoreType.DMA((2, 4)),
            pltpu.SemaphoreType.DMA((15, 4)),
        ],
        compiler_params=pltpu.CompilerParams(
            collective_id=0, has_side_effects=True, vmem_limit_bytes=255 * 2**18
        ),
        name="layer",
    )(
        segment,
        tokens,
        cotangent,
        ln1_gain,
        ln2_gain,
        q_gain,
        k_gain,
        jnp.transpose(w_qkv, (1, 0, 2)),
        w_out,
        w_up,
        w_down,
    )
    results, gains = list(outs[:6]), outs[6]
    if dp_low > 1:
        peers = [[hi * dp_low + lo for lo in range(dp_low)] for hi in range(1 << BITS)]

        def rest(x, axis):
            return lax.psum_scatter(
                x, "dp", scatter_dimension=axis, axis_index_groups=peers, tiled=True
            )

        results[2:] = [rest(x, x.ndim - 2) for x in results[2:]]
        gains = lax.psum(gains, "dp", axis_index_groups=peers)
    (
        layer_out,
        input_grad,
        up_grad,
        down_grad,
        proj_grad,
        qkv_grad,
        ln1_grad,
        ln2_grad,
        q_grad,
        k_grad,
    ) = pl.pallas_call(
        hand_on,
        out_shape=[shape(x.shape, x.dtype) for x in results]
        + [shape((D,), f32)] * 2
        + [shape((HD,), f32)] * 2,
        in_specs=[pl.BlockSpec(memory_space=pltpu.HBM)] * 7,
        out_specs=[pl.BlockSpec(memory_space=pltpu.HBM)] * 10,
        scratch_shapes=[pltpu.VMEM(x.shape, x.dtype) for x in results + [gains]]
        + [mem(D, dtype=f32)] * 2
        + [mem(HD, dtype=f32)] * 2
        + [pltpu.SemaphoreType.DMA((53,))],
        name="hand_on",
    )(*results, gains)
    return (
        layer_out,
        input_grad,
        ln1_grad,
        jnp.transpose(qkv_grad, (1, 0, 2)),
        q_grad,
        k_grad,
        proj_grad.T,
        ln2_grad,
        up_grad,
        down_grad.T,
    )


def solution(mesh):
    return jax.shard_map(
        local,
        mesh=mesh,
        in_specs=(
            P(("dp", "tensor"), None),
            P("dp"),
            P(),
            P(None, None, "tensor"),
            P(),
            P(),
            P("tensor", None),
            P(),
            P(None, "tensor"),
            P("tensor", None),
            P(("dp", "tensor"), None),
        ),
        out_specs=(
            P(("dp", "tensor"), None),
            P(("dp", "tensor"), None),
            P(),
            P("dp", None, "tensor"),
            P(),
            P(),
            P("tensor", "dp"),
            P(),
            P("dp", "tensor"),
            P("tensor", "dp"),
        ),
        check_vma=False,
    )
```
